32 devices in a mesh: dp: 8 (over z, x), seq: 4 (over y, core).
Axes of the slice: x: 2, y: 2, z: 4, core: 2. Of those that a mesh axis runs over, the one named last changes fastest.
Arguments:
- text_embed: bfloat16 [24, 512, 768], P('dp', 'seq'), may hold values from -6 to 6
- region_feature: bfloat16 [24, 512, 768], P('dp', 'seq')
- token_mask: int32 [24, 512], P('dp', 'seq'), may hold values from 0 to 1, as said below
- segment_mask: int32 [24, 512], P('dp', 'seq'), may hold values from 0 to 1, as said below
- mask_vector: float32 [768], replicated, may hold values from -6 to 6
- batch_gain: float32 [768], replicated, may hold values from 0.5 to 1.5
- batch_shift: float32 [768], replicated, may hold values from -3 to 3
- query_weight: bfloat16 [768, 768], P('seq'), may hold values from -0.21875 to 0.21875
- query_bias: float32 [768], replicated, may hold values from -3 to 3
- key_weight: bfloat16 [768, 768], P('seq'), may hold values from -0.21875 to 0.21875
- value_weight: bfloat16 [768, 768], P('seq'), may hold values from -0.21875 to 0.21875
- value_bias: float32 [768], replicated, may hold values from -3 to 3
- output_weight: bfloat16 [768, 768], P('seq'), may hold values from -0.875 to 0.875
- output_bias: float32 [768], replicated, may hold values from -3 to 3
- first_gain: float32 [768], replicated, may hold values from 0.5 to 1.5
- first_shift: float32 [768], replicated, may hold values from -3 to 3
- up_weight: bfloat16 [768, 3072], P('seq'), may hold values from -0.21875 to 0.21875
- up_bias: float32 [3072], replicated, may hold values from -3 to 3
- down_weight: bfloat16 [3072, 768], P('seq'), may hold values from -0.109375 to 0.109375
- down_bias: float32 [768], replicated, may hold values from -3 to 3
- second_gain: float32 [768], replicated, may hold values from 0.5 to 1.5
- second_shift: float32 [768], replicated, may hold values from -3 to 3
- cotangent: bfloat16 [24, 512, 768], P('dp', 'seq'), may hold values from -6 to 6
Outputs:
- layer_output: bfloat16 [24, 512, 768], P('dp', 'seq')
- text_gradient: bfloat16 [24, 512, 768], P('dp', 'seq')
- region_gradient: bfloat16 [24, 512, 768], P('dp', 'seq')
- mask_vector_gradient: float32 [768], replicated
- batch_gain_gradient: float32 [768], replicated
- batch_shift_gradient: float32 [768], replicated
- query_weight_gradient: float32 [768, 768], P('seq')
- query_bias_gradient: float32 [768], replicated
- key_weight_gradient: float32 [768, 768], P('seq')
- value_weight_gradient: float32 [768, 768], P('seq')
- value_bias_gradient: float32 [768], replicated
- output_weight_gradient: float32 [768, 768], P('seq')
- output_bias_gradient: float32 [768], replicated
- first_gain_gradient: float32 [768], replicated
- first_shift_gradient: float32 [768], replicated
- up_weight_gradient: float32 [768, 3072], P('seq')
- up_bias_gradient: float32 [3072], replicated
- down_weight_gradient: float32 [3072, 768], P('seq')
- down_bias_gradient: float32 [768], replicated
- second_gain_gradient: float32 [768], replicated
- second_shift_gradient: float32 [768], replicated
The draws below stay inside these ranges and needn't reach their ends.
Inputs may be any that keep to these rules, and one draw needn't show every extreme that they name: `token_mask`: 1 marks a masked token position; the share differs from document to document. `segment_mask`: 1 marks a position whose segment box is replaced; the share differs from document to document.
All inputs are finite; a program needn't handle non-finite values.
Results may differ from the reference program's by a relative error of at most 0.024.
The reference program's roundings to bfloat16 on the way count: a program that leaves them out, or rounds other values in their place, can miss the bound.
Values may be sent and summed in bfloat16 or wider, within the bound.
No kernel may reach another device: no remote copies, remote signals or barrier semaphores. Data moves between devices by JAX's collectives and lax.ppermute only.
A program may use at most 192 MiB of HBM per device.

```python
import math
import jax
import jax.numpy as jnp
from jax import lax

D = 768
HEADS = 12
HEAD_DIM = 64
FF = 3072
LEN = 512
DOCS_ALL = 24


def draw_region_feature(key, part):
    key = jax.random.fold_in(key, 11)
    noise_key, row_key, column_key, offset_key = jax.random.split(key, 4)
    doc_place = jnp.arange(DOCS_ALL, dtype=jnp.float32) / max(DOCS_ALL - 1, 1)
    token_place = jnp.arange(LEN, dtype=jnp.float32) / max(LEN - 1, 1)
    rising = jnp.exp(math.log(3.0) * doc_place[:, None] + math.log(1.5) * token_place[None, :])
    noise = jax.random.normal(noise_key, (DOCS_ALL, LEN, D), jnp.float32)
    row_scale = rising * jnp.exp(jax.random.uniform(row_key, (DOCS_ALL, LEN), jnp.float32, 0.0, math.log(2.0)))
    column_scale = jnp.exp(jax.random.uniform(column_key, (D,), jnp.float32, 0.0, math.log(10.0)))
    offsets = jax.random.normal(offset_key, (D,), jnp.float32) * 2.0
    values = (noise * row_scale[:, :, None] + offsets) * column_scale
    return values.astype(jnp.bfloat16)


def mask_from(key, lowest, highest):
    share_key, roll_key = jax.random.split(key)
    shares = jax.random.randint(share_key, (DOCS_ALL, 1), lowest, highest)
    rolling = jax.random.randint(roll_key, (DOCS_ALL, LEN), 0, 100)
    return (rolling < shares).astype(jnp.int32)


def draw_token_mask(key, part):
    key = jax.random.fold_in(key, 21)
    return mask_from(key, 8, 23)


def draw_segment_mask(key, part):
    key = jax.random.fold_in(key, 31)
    return mask_from(key, 8, 23)


def steps_of(stream_key, extent, cuts, smallest, high):
    level = 1.0
    for dim, parts in cuts:
        steps = jax.random.uniform(jax.random.fold_in(jax.random.fold_in(stream_key, 6), dim), (parts,), jnp.float32, smallest / len(cuts), high / len(cuts))
        level = level * jnp.repeat(jnp.exp(steps), extent[dim] // parts).reshape((-1,) + (1,) * (len(extent) - 1 - dim))
    return level


def scatter_about(own_key, dims, deviation, reach, cuts=(), kind=jnp.bfloat16):
    values = deviation * jax.random.normal(own_key, dims, jnp.float32)
    if cuts:
        values = values * steps_of(own_key, dims, cuts, -0.22, 0.18)
    return jnp.clip(values, -reach, reach).astype(kind)


def setup_inputs(seed: int = 0) -> dict:
    key_of = jax.random.split(jax.random.key(seed), 24)
    text_embed = scatter_about(key_of[0], (DOCS_ALL, LEN, D), 1.0, 6.0, ((0, 8), (1, 4)))
    region_feature = draw_region_feature(jax.random.fold_in(key_of[23], 71), 0)
    token_mask = draw_token_mask(jax.random.fold_in(key_of[23], 71), 0)
    segment_mask = draw_segment_mask(jax.random.fold_in(key_of[23], 71), 0)
    mask_vector = scatter_about(key_of[4], (D,), 1.0, 6.0, (), jnp.float32)
    batch_gain = jnp.clip(1.0 + 0.1 * jax.random.normal(key_of[5], (D,), jnp.float32), 0.5, 1.5)
    batch_shift = scatter_about(key_of[6], (D,), 0.5, 3.0, (), jnp.float32)
    query_weight = scatter_about(key_of[7], (D, D), D ** -0.5, 0.21875, ((0, 4),))
    query_bias = scatter_about(key_of[8], (D,), 0.5, 3.0, (), jnp.float32)
    key_weight = scatter_about(key_of[9], (D, D), D ** -0.5, 0.21875, ((0, 4),))
    value_weight = scatter_about(key_of[10], (D, D), D ** -0.5, 0.21875, ((0, 4),))
    value_bias = scatter_about(key_of[11], (D,), 0.5, 3.0, (), jnp.float32)
    output_weight = scatter_about(key_of[12], (D, D), (D // 16) ** -0.5, 0.875, ((0, 4),))
    output_bias = scatter_about(key_of[13], (D,), 0.5, 3.0, (), jnp.float32)
    first_gain = jnp.clip(1.0 + 0.1 * jax.random.normal(key_of[14], (D,), jnp.float32), 0.5, 1.5)
    first_shift = scatter_about(key_of[15], (D,), 0.5, 3.0, (), jnp.float32)
    up_weight = scatter_about(key_of[16], (D, FF), D ** -0.5, 0.21875, ((0, 4),))
    up_bias = scatter_about(key_of[17], (FF,), 0.5, 3.0, (), jnp.float32)
    down_weight = scatter_about(key_of[18], (FF, D), FF ** -0.5, 0.109375, ((0, 4),))
    down_bias = scatter_about(key_of[19], (D,), 0.5, 3.0, (), jnp.float32)
    second_gain = jnp.clip(1.0 + 0.1 * jax.random.normal(key_of[20], (D,), jnp.float32), 0.5, 1.5)
    second_shift = scatter_about(key_of[21], (D,), 0.5, 3.0, (), jnp.float32)
    cotangent = scatter_about(key_of[22], (DOCS_ALL, LEN, D), 1.0, 6.0, ((0, 8), (1, 4)))
    return dict(text_embed=text_embed, region_feature=region_feature, token_mask=token_mask, segment_mask=segment_mask, mask_vector=mask_vector, batch_gain=batch_gain, batch_shift=batch_shift, query_weight=query_weight, query_bias=query_bias, key_weight=key_weight, value_weight=value_weight, value_bias=value_bias, output_weight=output_weight, output_bias=output_bias, first_gain=first_gain, first_shift=first_shift, up_weight=up_weight, up_bias=up_bias, down_weight=down_weight, down_bias=down_bias, second_gain=second_gain, second_shift=second_shift, cotangent=cotangent)


@jax.custom_vjp
def low(v):
    return lax.optimization_barrier(v.astype(jnp.bfloat16)).astype(jnp.float32)

@jax.custom_vjp
def low_back(v):
    return v

def low_keep(v):
    return (low(v), None)

def low_pass(kept, grad):
    return (grad,)

def back_keep(v):
    return (v, None)

def back_low(kept, grad):
    return (low(grad),)
low.defvjp(low_keep, low_pass)
low_back.defvjp(back_keep, back_low)
EPS_NORM = 1e-12
EPS_BATCH = 1e-05
HIGHEST = lax.Precision.HIGHEST

def matmul(matrix, other):
    return jnp.dot(matrix, other, precision=HIGHEST, preferred_element_type=jnp.float32)

def layer_norm(values, scaling, offset):
    average = lax.optimization_barrier(jnp.mean(values, axis=-1, keepdims=True))
    centred = values - average
    variance = lax.optimization_barrier(jnp.mean(centred * centred, axis=-1, keepdims=True))
    return centred * lax.rsqrt(variance + EPS_NORM) * scaling + offset

def heads_view(values):
    return values.reshape(values.shape[0], values.shape[1], HEADS, HEAD_DIM)

def encoder_block(inputs, params):
    query_weight, query_bias, key_weight, value_weight, value_bias, output_weight, output_bias, first_gain, first_shift, up_weight, up_bias, down_weight, down_bias, second_gain, second_shift = params
    documents = inputs.shape[0]
    flat_rows = inputs.reshape(documents * LEN, D)
    low_in = low(flat_rows)
    queries = low_back(low(matmul(low_in, query_weight) + query_bias)).reshape(documents, LEN, D)
    key_rows = low_back(low(matmul(low_in, key_weight))).reshape(documents, LEN, D)
    values = low_back(low(matmul(low_in, value_weight) + value_bias)).reshape(documents, LEN, D)
    scores = jnp.einsum('gqhe,gkhe->ghqk', heads_view(queries), heads_view(key_rows), precision=HIGHEST)
    scores = low_back(scores * (1.0 / math.sqrt(HEAD_DIM)))
    maxima = lax.optimization_barrier(jnp.max(scores, axis=-1, keepdims=True))
    raised = jnp.exp(scores - maxima)
    probabilities = raised / lax.optimization_barrier(jnp.sum(raised, axis=-1, keepdims=True))
    attention = jnp.einsum('ghqk,gkhe->gqhe', low(probabilities), heads_view(values), precision=HIGHEST)
    attn_low = low_back(low(attention.reshape(documents * LEN, D)))
    out_pre = low_back(matmul(attn_low, output_weight) + output_bias)
    first_out = layer_norm(flat_rows + out_pre, first_gain, first_shift)
    up_pre = low_back(matmul(low(first_out), up_weight) + up_bias)
    act_low = low_back(low(jax.nn.gelu(up_pre, approximate=True)))
    down_pre = low_back(matmul(act_low, down_weight) + down_bias)
    return layer_norm(first_out + down_pre, second_gain, second_shift).reshape(documents, LEN, D)

def reference(text_embed, region_feature, token_mask, segment_mask, mask_vector, batch_gain, batch_shift, query_weight, query_bias, key_weight, value_weight, value_bias, output_weight, output_bias, first_gain, first_shift, up_weight, up_bias, down_weight, down_bias, second_gain, second_shift, cotangent):
    token_hit = token_mask.astype(jnp.float32)[..., None]
    segment_keep = 1.0 - segment_mask.astype(jnp.float32)[..., None]
    group_size = math.gcd(DOCS_ALL, 8)

    def forward(text, region, mask_vec, gain_batch, shift_batch, *params):
        average = lax.optimization_barrier(jnp.mean(region, axis=(0, 1)))
        second = lax.optimization_barrier(jnp.mean(region * region, axis=(0, 1)))
        standard = (region - average) * lax.rsqrt(second - average * average + EPS_BATCH)
        normed = standard * gain_batch + shift_batch
        embedded = text * (1.0 - token_hit) + token_hit * mask_vec + segment_keep * normed
        blocks = embedded.reshape(DOCS_ALL // group_size, group_size, LEN, D)
        checked = jax.checkpoint(encoder_block)

        def scan_step(carry, block):
            return (carry, checked(block, params))
        unused, outputs = lax.scan(scan_step, None, blocks)
        return outputs.reshape(DOCS_ALL, LEN, D)
    floats = (text_embed.astype(jnp.float32), region_feature.astype(jnp.float32), mask_vector.astype(jnp.float32), batch_gain.astype(jnp.float32), batch_shift.astype(jnp.float32), query_weight.astype(jnp.float32), query_bias.astype(jnp.float32), key_weight.astype(jnp.float32), value_weight.astype(jnp.float32), value_bias.astype(jnp.float32), output_weight.astype(jnp.float32), output_bias.astype(jnp.float32), first_gain.astype(jnp.float32), first_shift.astype(jnp.float32), up_weight.astype(jnp.float32), up_bias.astype(jnp.float32), down_weight.astype(jnp.float32), down_bias.astype(jnp.float32), second_gain.astype(jnp.float32), second_shift.astype(jnp.float32))
    result, backward = jax.vjp(forward, *floats)
    grad_text, grad_region, grad_mask, grad_batch_gain, grad_batch_shift, grad_query_weight, grad_query_bias, grad_key_weight, grad_value_weight, grad_value_bias, grad_output_weight, grad_output_bias, grad_first_gain, grad_first_shift, grad_up_weight, grad_up_bias, grad_down_weight, grad_down_bias, grad_second_gain, grad_second_shift = backward(cotangent.astype(jnp.float32))
    return (result.astype(jnp.bfloat16), grad_text.astype(jnp.bfloat16), grad_region.astype(jnp.bfloat16), grad_mask, grad_batch_gain, grad_batch_shift, grad_query_weight, grad_query_bias, grad_key_weight, grad_value_weight, grad_value_bias, grad_output_weight, grad_output_bias, grad_first_gain, grad_first_shift, grad_up_weight, grad_up_bias, grad_down_weight, grad_down_bias, grad_second_gain, grad_second_shift)
```

```python
import math

import jax
import jax.numpy as jnp
from jax import lax
from jax.sharding import PartitionSpec as P

HEAD_DIM = 64
EPS_NORM = 1e-12
EPS_BATCH = 1e-05
F32 = jnp.float32
BF16 = jnp.bfloat16
GELU_IN = math.sqrt(2.0 / math.pi)
GELU_CUBE = 0.044715


def swap(x, axis, by):
    return lax.ppermute(x, axis, [(i, i ^ by) for i in range(lax.axis_size(axis))])


def bits(axis):
    found, by = [], 1
    while by < lax.axis_size(axis):
        found.append(by)
        by *= 2
    return found


def sum_all(x):
    for axis in ("seq", "dp"):
        for by in bits(axis):
            x = x + swap(x, axis, by)
    return x


def nn(a, b):
    return jnp.dot(a, b, preferred_element_type=F32)


def tn(a, b):
    return lax.dot_general(a, b, (((0,), (0,)), ((), ())), preferred_element_type=F32)


def nt(a, b):
    return lax.dot_general(a, b, (((1,), (1,)), ((), ())), preferred_element_type=F32)


def norm_parts(x):
    centred = x - jnp.mean(x, axis=-1, keepdims=True)
    scale = lax.rsqrt(jnp.mean(centred * centred, axis=-1, keepdims=True) + EPS_NORM)
    return centred * scale, scale


def norm_back(grad, unit, scale, gain):
    g = grad * gain
    return scale * (
        g
        - jnp.mean(g, axis=-1, keepdims=True)
        - unit * jnp.mean(g * unit, axis=-1, keepdims=True)
    )


def gather_rows(x):
    two = swap(x, "seq", 2)
    one, three = swap(x, "seq", 1), swap(two, "seq", 1)
    return [x, one, two, three]


def gather_weight(w, dp):
    half = w.shape[0] // 2
    bit = dp % 2
    near = swap(lax.dynamic_slice_in_dim(w, bit * half, half, 0), "seq", 2)
    far = swap(near, "dp", 1)
    two = jnp.where(bit == 0, jnp.concatenate([near, far]), jnp.concatenate([far, near]))
    one, three = swap(w, "seq", 1), swap(two, "seq", 1)
    return [w, one, two, three]


def scatter_rows(blocks):
    keep = blocks[0].astype(F32) + swap(blocks[1], "seq", 1).astype(F32)
    pass_on = blocks[2].astype(F32) + swap(blocks[3], "seq", 1).astype(F32)
    return keep + swap(pass_on.astype(BF16), "seq", 2).astype(F32)


def exchange_blocks(blocks):
    return [blocks[0]] + [swap(blocks[r], "seq", r) for r in (1, 2, 3)]


def halve(x, by, dp, dim):
    half = x.shape[dim] // 2
    bit = (dp // by) % 2
    keep = lax.dynamic_slice_in_dim(x, bit * half, half, dim)
    give = lax.dynamic_slice_in_dim(x, (1 - bit) * half, half, dim)
    return keep.astype(F32) + swap(give.astype(BF16), "dp", by).astype(F32)


def double(x, by, dp, dim):
    other = swap(x, "dp", by)
    bit = (dp // by) % 2
    return jnp.where(
        bit == 0,
        jnp.concatenate([x, other], axis=dim),
        jnp.concatenate([other, x], axis=dim),
    )


def order_of(turn):
    found = bits("dp")
    if turn % 2 and len(found) > 1:
        found = [found[1], found[0]] + found[2:]
    return found


def sum_dp(x, dp, dim, turn, between=None):
    halved = []
    for by in order_of(turn):
        if x.shape[dim] % 2 == 0 and x.shape[dim] >= 16:
            x = halve(x, by, dp, dim)
            halved.append(by)
        else:
            x = x.astype(F32) + swap(x.astype(BF16), "dp", by).astype(F32)
    x = x.astype(BF16)
    if between is not None:
        x = between(x)
    for by in reversed(halved):
        x = double(x, by, dp, dim)
    return x


def sum_gradient(blocks, dp, turn):
    return sum_dp(scatter_rows(blocks), dp, 0, turn)


def in_place(blocks, seq):
    stacked = jnp.stack(blocks)
    return [lax.dynamic_index_in_dim(stacked, seq ^ j, 0, keepdims=False) for j in range(4)]


def body(
    text_embed,
    region_feature,
    token_mask,
    segment_mask,
    mask_vector,
    batch_gain,
    batch_shift,
    query_weight,
    query_bias,
    key_weight,
    value_weight,
    value_bias,
    output_weight,
    output_bias,
    first_gain,
    first_shift,
    up_weight,
    up_bias,
    down_weight,
    down_bias,
    second_gain,
    second_shift,
    cotangent,
):
    documents, span, features = text_embed.shape
    rows = documents * span
    seq, dp = lax.axis_index("seq"), lax.axis_index("dp")
    group = lax.axis_size("seq")
    population = rows * lax.axis_size("dp") * group
    score_scale = 1.0 / math.sqrt(HEAD_DIM)
    part = features // group
    heads = part // HEAD_DIM

    region = region_feature.astype(F32).reshape(rows, features)
    sums = sum_all(jnp.stack([jnp.sum(region, axis=0), jnp.sum(region * region, axis=0)]))
    average = sums[0] / population
    inverse = lax.rsqrt(sums[1] / population - average * average + EPS_BATCH)

    cut = (
        jnp.stack([query_weight, key_weight, value_weight], axis=1)
        .reshape(part, 3, group, part)
        .transpose(2, 0, 1, 3)
        .reshape(group, part, 3 * part)
    )
    mine = exchange_blocks(
        [lax.dynamic_index_in_dim(cut, seq ^ r, 0, keepdims=False) for r in range(group)]
    )
    head_weight = jnp.concatenate(in_place(mine, seq))
    bias3 = jnp.stack([query_bias, jnp.zeros_like(query_bias), value_bias]).reshape(3, group, part)
    head_bias = lax.dynamic_index_in_dim(bias3, seq, 1, keepdims=False).reshape(3 * part)

    out_blocks = gather_weight(output_weight, dp)
    up_blocks = gather_weight(up_weight, dp)
    down_blocks = gather_weight(down_weight, dp)

    standard = (region - average) * inverse
    token_hit = token_mask.astype(F32).reshape(rows, 1)
    segment_keep = 1.0 - segment_mask.astype(F32).reshape(rows, 1)
    embedded = (
        text_embed.astype(F32).reshape(rows, features) * (1.0 - token_hit)
        + token_hit * mask_vector
        + segment_keep * (standard * batch_gain + batch_shift)
    )
    low_in = embedded.astype(BF16).reshape(documents, span, features)

    saved, given = [], []
    for d in range(documents):
        whole = jnp.concatenate(gather_rows(low_in[d]))
        projected = (nn(whole, head_weight) + head_bias).astype(BF16)
        q, k, v = (projected[:, i * part : (i + 1) * part].reshape(-1, heads, HEAD_DIM) for i in range(3))
        scores = jnp.einsum("qhe,khe->hqk", q, k, preferred_element_type=F32) * score_scale
        top = jnp.max(scores, axis=-1, keepdims=True)
        raised = jnp.exp(scores - top)
        total = jnp.sum(raised, axis=-1, keepdims=True)
        attended = jnp.einsum(
            "hqk,khe->hqe", raised.astype(BF16), v, preferred_element_type=F32
        ) / total
        attended = attended.transpose(1, 0, 2).reshape(group * span, part)
        saved.append((whole, q, k, v, top + jnp.log(total), attended))
        given.append(exchange_blocks(list(attended.astype(BF16).reshape(group, span, part))))
    attn_blocks = [jnp.concatenate([g[r] for g in given]) for r in range(group)]
    attn_low = jnp.concatenate(attn_blocks, axis=1)

    out_weight = jnp.concatenate(out_blocks)
    residual = embedded + nn(attn_low, out_weight) + output_bias
    first_unit, first_scale = norm_parts(residual)
    first_out = first_unit * first_gain + first_shift
    first_low = first_out.astype(BF16)
    full_up = jnp.concatenate(in_place(up_blocks, seq))
    full_down = jnp.concatenate(in_place(down_blocks, seq))
    up_pre = nn(first_low, full_up) + up_bias
    square = up_pre * up_pre
    bend = jnp.tanh(GELU_IN * up_pre * (1.0 + GELU_CUBE * square))
    act_low = (0.5 * up_pre * (1.0 + bend)).astype(BF16)
    second_in = first_out + nn(act_low, full_down) + down_bias
    second_unit, second_scale = norm_parts(second_in)
    layer_output = (second_unit * second_gain + second_shift).astype(BF16)

    incoming = cotangent.astype(F32).reshape(rows, features)
    grad_second = norm_back(incoming, second_unit, second_scale, second_gain)
    grad_down = grad_second.astype(BF16)
    term_down = tn(act_low, grad_down).astype(BF16)
    grad_act = nt(grad_down, full_down).astype(BF16).astype(F32)
    slope = 0.5 * (1.0 + bend) + 0.5 * up_pre * (1.0 - bend * bend) * GELU_IN * (
        1.0 + 3.0 * GELU_CUBE * square
    )
    grad_up = (grad_act * slope).astype(BF16)
    term_up = tn(first_low, grad_up).astype(BF16)
    grad_first = grad_second + nt(grad_up, full_up)
    grad_residual = norm_back(grad_first, first_unit, first_scale, first_gain)
    grad_out = grad_residual.astype(BF16)
    term_out = tn(attn_low, grad_out).astype(BF16)
    grad_attn = nt(grad_out, out_weight).astype(BF16).reshape(documents, span, group, part)

    middle_sums = [
        jnp.sum(incoming * second_unit, axis=0),
        jnp.sum(incoming, axis=0),
        jnp.sum(grad_down.astype(F32), axis=0),
        jnp.sum(grad_up.astype(F32), axis=0),
        jnp.sum(grad_first * first_unit, axis=0),
        jnp.sum(grad_first, axis=0),
        jnp.sum(grad_out.astype(F32), axis=0),
    ]

    def by_device(term, turn, pieces):
        blocks = term.reshape(group, -1, term.shape[-1])
        blocks = [lax.dynamic_index_in_dim(blocks, seq ^ r, 0, keepdims=False) for r in range(group)]
        wide = blocks[0].shape[1] > blocks[0].shape[0]
        cuts = [jnp.split(b, pieces, axis=1 if wide else 0) for b in blocks]
        return jnp.concatenate(
            [sum_gradient([c[i] for c in cuts], dp, turn + i) for i in range(pieces)],
            axis=1 if wide else 0,
        ).astype(F32)

    total_down = by_device(term_down, 0, 2)
    total_up = by_device(term_up, 0, 2)
    total_out = sum_gradient(list(term_out.reshape(group, part, features)), dp, 1).astype(F32)

    inner, turned, query_sums, value_sums = [], [], 0.0, 0.0
    for d in range(documents):
        whole, q, k, v, log_total, attended = saved[d]
        got = exchange_blocks([grad_attn[d, :, r] for r in range(group)])
        g = jnp.concatenate(got)
        correction = jnp.sum((g.astype(F32) * attended).reshape(-1, heads, HEAD_DIM), axis=-1)
        g = g.reshape(-1, heads, HEAD_DIM)
        scores = jnp.einsum("qhe,khe->hqk", q, k, preferred_element_type=F32) * score_scale
        probabilities = jnp.exp(scores - log_total)
        grad_v = jnp.einsum("hqk,qhe->khe", probabilities.astype(BF16), g, preferred_element_type=F32)
        grad_probs = jnp.einsum("qhe,khe->hqk", g, v, preferred_element_type=F32)
        grad_scores = (probabilities * (grad_probs - correction.T[..., None])).astype(BF16)
        grad_q = jnp.einsum("hqk,khe->qhe", grad_scores, k, preferred_element_type=F32) * score_scale
        grad_k = jnp.einsum("hqk,qhe->khe", grad_scores, q, preferred_element_type=F32) * score_scale
        grads = jnp.concatenate(
            [x.reshape(-1, part).astype(BF16) for x in (grad_q, grad_k, grad_v)], axis=1
        )
        query_sums = query_sums + jnp.sum(grads[:, :part].astype(F32), axis=0)
        value_sums = value_sums + jnp.sum(grads[:, 2 * part :].astype(F32), axis=0)
        turned.append(grads)
        inner.append(
            scatter_rows(list(nt(grads, head_weight).astype(BF16).reshape(group, span, features)))
        )
    term_heads = tn(
        jnp.concatenate([s[0] for s in saved]), jnp.concatenate(turned)
    ).reshape(group, part, 3 * part)

    def to_rows(x):
        got = exchange_blocks(
            [lax.dynamic_index_in_dim(x, seq ^ r, 0, keepdims=False) for r in range(group)]
        )
        return jnp.stack(in_place(got, seq))

    total_heads = sum_dp(term_heads, dp, 1, 0, to_rows).astype(F32)
    total_heads = total_heads.reshape(group, part, 3, part).transpose(2, 1, 0, 3)
    total_query, total_key, total_value = total_heads.reshape(3, part, features)

    grad_embedded = grad_residual + jnp.concatenate(inner)
    text_gradient = (grad_embedded * (1.0 - token_hit)).astype(BF16)
    grad_normed = grad_embedded * segment_keep

    def widen(x):
        return lax.dynamic_update_slice_in_dim(jnp.zeros((features,), F32), x, seq * part, 0)

    last = [
        jnp.sum(grad_normed * standard, axis=0),
        jnp.sum(grad_normed, axis=0),
        jnp.sum(grad_embedded * token_hit, axis=0),
        widen(query_sums),
        widen(value_sums),
    ]
    sum_gain, sum_shift, sum_mask, sum_query_bias, sum_value_bias = sum_all(jnp.stack(last))
    lengths = [x.shape[0] for x in middle_sums]
    middle = sum_all(jnp.concatenate(middle_sums))
    pieces, at = [], 0
    for length in lengths:
        pieces.append(middle[at : at + length])
        at += length
    (
        sum_second_gain,
        sum_second_shift,
        sum_down_bias,
        sum_up_bias,
        sum_first_gain,
        sum_first_shift,
        sum_output_bias,
    ) = pieces

    region_gradient = (
        batch_gain
        * inverse
        * (grad_normed - sum_shift / population - standard * (sum_gain / population))
    ).astype(BF16)
    shape = (documents, span, features)
    return (
        layer_output.reshape(shape),
        text_gradient.reshape(shape),
        region_gradient.reshape(shape),
        sum_mask,
        sum_gain,
        sum_shift,
        total_query,
        sum_query_bias,
        total_key,
        total_value,
        sum_value_bias,
        total_out,
        sum_output_bias,
        sum_first_gain,
        sum_first_shift,
        total_up,
        sum_up_bias,
        total_down,
        sum_down_bias,
        sum_second_gain,
        sum_second_shift,
    )


def solution(mesh):
    rows, weight, copied = P("dp", "seq", None), P("seq", None), P()
    mask = P("dp", "seq")
    in_specs = (
        (rows, rows, mask, mask, copied, copied, copied)
        + (weight, copied, weight, weight, copied, weight, copied, copied, copied)
        + (weight, copied, weight, copied, copied, copied, rows)
    )
    out_specs = (
        (rows, rows, rows, copied, copied, copied)
        + (weight, copied, weight, weight, copied, weight, copied, copied, copied)
        + (weight, copied, weight, copied, copied, copied)
    )
    return jax.shard_map(body, mesh=mesh, in_specs=in_specs, out_specs=out_specs, check_vma=False)
```

```python
import functools
import math

import jax
import jax.numpy as jnp
from jax import lax
from jax.experimental import pallas as pl
from jax.experimental.pallas import tpu as pltpu
from jax.sharding import PartitionSpec as P

HEAD_DIM = 64
EPS_NORM = 1e-12
EPS_BATCH = 1e-05
F32 = jnp.float32
BF16 = jnp.bfloat16
GELU_IN = math.sqrt(2.0 / math.pi)
GELU_CUBE = 0.044715
PIECES = 8
DOWN_ORDER = (1, 2, 4)
UP_ORDER = (2, 1, 4)
HEAD_ORDER = (1, 2, 4)


def swap(x, axis, by):
    return lax.ppermute(x, axis, [(i, i ^ by) for i in range(lax.axis_size(axis))])


def bits(axis):
    found, by = [], 1
    while by < lax.axis_size(axis):
        found.append(by)
        by *= 2
    return found


def sum_all(x):
    for axis in ("seq", "dp"):
        for by in bits(axis):
            x = x + swap(x, axis, by)
    return x


def nn(a, b):
    return jnp.dot(a, b, preferred_element_type=F32)


def tn(a, b):
    return lax.dot_general(a, b, (((0,), (0,)), ((), ())), preferred_element_type=F32)


def nt(a, b):
    return lax.dot_general(a, b, (((1,), (1,)), ((), ())), preferred_element_type=F32)


def norm_parts(x):
    centred = x - jnp.mean(x, axis=-1, keepdims=True)
    scale = lax.rsqrt(jnp.mean(centred * centred, axis=-1, keepdims=True) + EPS_NORM)
    return centred * scale, scale


def norm_back(grad, unit, scale, gain):
    g = grad * gain
    return scale * (
        g
        - jnp.mean(g, axis=-1, keepdims=True)
        - unit * jnp.mean(g * unit, axis=-1, keepdims=True)
    )


def gather_rows(x):
    two = swap(x, "seq", 2)
    one, three = swap(x, "seq", 1), swap(two, "seq", 1)
    return [x, one, two, three]


def gather_weight(halves, dp):
    near = swap(lax.dynamic_index_in_dim(halves, dp % 2, 0, keepdims=False), "seq", 2)
    far = swap(near, "dp", 1)
    return [halves, near, far, swap(halves, "seq", 1), swap(near, "seq", 1), swap(far, "seq", 1)]


def scatter_pairs(keep, give):
    got = swap(give, "seq", 1)
    pass_on = (keep[1].astype(F32) + got[1].astype(F32)).astype(BF16)
    own = keep[0].astype(F32) + got[0].astype(F32)
    return own + swap(pass_on, "seq", 2).astype(F32)


def exchange_blocks(blocks):
    return [blocks[0]] + [swap(blocks[r], "seq", r) for r in (1, 2, 3)]


VMEM_BYTES = 56 * 1024 * 1024


def params(*semantics):
    return pltpu.CompilerParams(vmem_limit_bytes=VMEM_BYTES)


def whole_spec():
    return pl.BlockSpec(memory_space=pltpu.VMEM)


def attend_kernel(seq_ref, *refs):
    x_refs, w_refs, bias_ref = refs[:4], refs[4:8], refs[8]
    q_ref, k_ref, v_ref, wc_ref, out_refs = refs[9], refs[10], refs[11], refs[12], refs[13:17]
    part = w_refs[0].shape[1]
    span = x_refs[0].shape[1]

    @pl.when(pl.program_id(0) == 0)
    def _():
        for r in range(4):
            at = pl.multiple_of((seq_ref[0] ^ r) * part, part)
            wc_ref[:, pl.ds(at, part), :] = w_refs[r][...]

    x = jnp.concatenate([ref[0] for ref in x_refs], axis=0)
    for i, ref in enumerate((q_ref, k_ref, v_ref)):
        ref[0] = (nn(x, wc_ref[i]) + bias_ref[i]).astype(BF16)
    q, k, v = q_ref[0], k_ref[0], v_ref[0]
    lane = lax.broadcasted_iota(jnp.int32, (1, part), 1) // HEAD_DIM
    for h in range(part // HEAD_DIM):
        pick = jnp.where(lane == h, 1.0 / math.sqrt(HEAD_DIM), 0.0).astype(BF16)
        scores = nt(k, q * pick)
        raised = jnp.exp(scores - jnp.max(scores, axis=0, keepdims=True))
        chances = (raised * (1.0 / jnp.sum(raised, axis=0, keepdims=True))).astype(BF16)
        attended = tn(v, chances)[h * HEAD_DIM : (h + 1) * HEAD_DIM].astype(BF16)
        for r in range(4):
            out_refs[r][h * HEAD_DIM : (h + 1) * HEAD_DIM, :] = attended[:, r * span : (r + 1) * span]


def attend(seq, x_blocks, w_blocks, bias):
    documents, span, features = x_blocks[0].shape
    part = w_blocks[0].shape[1]
    length = 4 * span
    flops = documents * (2 * length * features * 3 * part + 4 * length * length * part)
    per_doc = pl.BlockSpec((1, length, part), lambda d: (d, 0, 0))
    return pl.pallas_call(
        attend_kernel,
        grid=(documents,),
        in_specs=[pl.BlockSpec(memory_space=pltpu.SMEM)]
        + [pl.BlockSpec((1, span, features), lambda d: (d, 0, 0))] * 4
        + [pl.BlockSpec((3, part, part), lambda d: (0, 0, 0))] * 4
        + [pl.BlockSpec((3, 1, part), lambda d: (0, 0, 0))],
        out_specs=[per_doc] * 3
        + [pl.BlockSpec((3, features, part), lambda d: (0, 0, 0))]
        + [pl.BlockSpec((part, span), lambda d: (0, d))] * 4,
        out_shape=[jax.ShapeDtypeStruct((documents, length, part), BF16)] * 3
        + [jax.ShapeDtypeStruct((3, features, part), BF16)]
        + [jax.ShapeDtypeStruct((part, documents * span), BF16)] * 4,
        compiler_params=params(),
        cost_estimate=pl.CostEstimate(
            flops=flops, bytes_accessed=8 * 1024 * 1024, transcendentals=documents * length * length * 3
        ),
        name="attend",
    )(seq, *x_blocks, *w_blocks, bias)


def attend_back_kernel(place_ref, *refs):
    g_refs, x_refs = refs[:4], refs[4:8]
    q_ref, k_ref, v_ref, wc_ref = refs[8:12]
    keep_ref, give_ref, dw_ref, sums_ref, acc_ref = refs[12:]
    part = q_ref.shape[2]
    span = x_refs[0].shape[1]
    first = pl.program_id(0) == 0
    q, k, v = q_ref[0], k_ref[0], v_ref[0]
    g = jnp.concatenate([ref[...] for ref in g_refs], axis=1)
    lane = lax.broadcasted_iota(jnp.int32, (1, part), 1) // HEAD_DIM
    scale = 1.0 / math.sqrt(HEAD_DIM)
    dq = dk = dv = None
    for h in range(part // HEAD_DIM):
        on = lane == h
        pick = jnp.where(on, scale, 0.0).astype(BF16)
        mask = jnp.where(on, 1.0, 0.0)
        scores = nt(k, q * pick)
        raised = jnp.exp(scores - jnp.max(scores, axis=0, keepdims=True))
        chances = raised * (1.0 / jnp.sum(raised, axis=0, keepdims=True))
        grad = nn(v * mask.astype(BF16), g)
        both = chances * grad
        grad = (both - chances * jnp.sum(both, axis=0, keepdims=True)).astype(BF16)
        part_v = nt(chances.astype(BF16), g) * mask
        part_k = nn(grad, q) * (mask * scale)
        part_q = tn(grad, k) * (mask * scale)
        dq = part_q if dq is None else dq + part_q
        dk = part_k if dk is None else dk + part_k
        dv = part_v if dv is None else dv + part_v
    low = [t.astype(BF16) for t in (dq, dk, dv)]
    sums = jnp.concatenate(
        [jnp.sum(low[i].astype(F32), axis=0, keepdims=True) for i in (0, 2)], axis=0
    )
    x = jnp.concatenate([ref[0] for ref in x_refs], axis=0)
    x_t = x.T
    inner = nt(low[0], wc_ref[0]) + nt(low[1], wc_ref[1]) + nt(low[2], wc_ref[2])
    inner = inner.astype(BF16)
    for r in range(4):
        (give_ref if r % 2 else keep_ref)[r // 2, 0] = inner[r * span : (r + 1) * span]

    @pl.when(first)
    def _():
        sums_ref[...] = sums
        for i in range(3):
            acc_ref[i] = nn(x_t, low[i])

    @pl.when(jnp.logical_not(first))
    def _():
        sums_ref[...] += sums
        for i in range(3):
            acc_ref[i] += nn(x_t, low[i])

    @pl.when(pl.program_id(0) == pl.num_programs(0) - 1)
    def _():
        tall = part // PIECES
        for p in range(PIECES):
            spot = place(p ^ (place_ref[1] % PIECES), HEAD_ORDER)
            for block in range(4):
                at = block * part + p * tall
                for i in range(3):
                    dw_ref[spot, place_ref[0] ^ block, :, i * part : (i + 1) * part] = acc_ref[
                        i, at : at + tall, :
                    ].astype(BF16)


def attend_back(place_word, g_blocks, x_blocks, q, k, v, wc):
    documents, span, features = x_blocks[0].shape
    part = q.shape[2]
    length = 4 * span
    flops = documents * (4 * length * features * 3 * part + 10 * length * length * part)
    per_doc = pl.BlockSpec((1, length, part), lambda d: (d, 0, 0))
    pair = pl.BlockSpec((2, 1, span, features), lambda d: (0, d, 0, 0))
    return pl.pallas_call(
        attend_back_kernel,
        grid=(documents,),
        in_specs=[pl.BlockSpec(memory_space=pltpu.SMEM)]
        + [pl.BlockSpec((part, span), lambda d: (0, d))] * 4
        + [pl.BlockSpec((1, span, features), lambda d: (d, 0, 0))] * 4
        + [per_doc] * 3
        + [pl.BlockSpec((3, features, part), lambda d: (0, 0, 0))],
        out_specs=[
            pair,
            pair,
            pl.BlockSpec((PIECES, 4, part // PIECES, 3 * part), lambda d: (0, 0, 0, 0)),
            pl.BlockSpec((2, part), lambda d: (0, 0)),
        ],
        out_shape=[jax.ShapeDtypeStruct((2, documents, span, features), BF16)] * 2
        + [
            jax.ShapeDtypeStruct((PIECES, 4, part // PIECES, 3 * part), BF16),
            jax.ShapeDtypeStruct((2, part), F32),
        ],
        scratch_shapes=[pltpu.VMEM((3, features, part), F32)],
        compiler_params=params(),
        cost_estimate=pl.CostEstimate(
            flops=flops, bytes_accessed=12 * 1024 * 1024, transcendentals=documents * length * length * 3
        ),
        name="attend_back",
    )(place_word, *g_blocks, *x_blocks, q, k, v, wc)


def place(index, order):
    at = 0
    for by in order:
        at = 2 * at + (index // by) % 2
    return at


def gelu_parts(x):
    bend = jnp.tanh(GELU_IN * x * (1.0 + GELU_CUBE * x * x))
    return 0.5 * (1.0 + bend), bend


def middle_kernel(place_ref, *refs):
    (a_refs, in_ref, cot_ref, vec_ref, upb_ref), refs = (refs[:4], *refs[4:8]), refs[8:]
    pieces, refs = refs[:12], refs[12:]
    out_ref, res_ref, g_refs, sums_ref, upsum_ref = refs[0], refs[1], refs[2:6], refs[6], refs[7]
    down_out, up_out = refs[8:11], refs[11:14]
    wo, up, down, low, low_t, act, pre, acc, tmp, sems = refs[14:]
    seq, dp = place_ref[0], place_ref[1]
    bit = dp % 2
    part, features = wo.shape[1], wo.shape[2]
    half = part // 2
    count = PIECES

    copies = []

    def bring(source, target):
        copies.append(pltpu.make_async_copy(source, target, sems.at[len(copies)]))

    for group, first in ((0, True), (6, False)):
        own, near, far, one, near_one, far_one = pieces[group : group + 6]
        parts = [(own.at[h], 0, h) for h in range(2)] + [(one.at[h], 1, h) for h in range(2)]
        parts += [(near, 2, bit), (far, 2, 1 - bit), (near_one, 3, bit), (far_one, 3, 1 - bit)]
        for source, r, h in parts:
            if first:
                bring(source.at[pl.ds(0, half)], wo.at[r, pl.ds(pl.multiple_of(h * half, half), half)])
                at = pl.multiple_of((seq ^ r) * part + h * half, half)
                for j in range(4):
                    bring(source.at[pl.ds(half * (j + 1), half)], up.at[j, pl.ds(at, half)])
            else:
                size = 2 * part
                bring(source, down.at[seq ^ r, pl.ds(pl.multiple_of(h * size, size), size)])
    for copy in copies:
        copy.start()
    out_bias, gain1, shift1, down_bias, gain2, shift2 = (vec_ref[i : i + 1, :] for i in range(6))
    for copy in copies[:-8]:
        copy.wait()

    residual = in_ref[...] + out_bias
    for r in range(4):
        residual += tn(a_refs[r][...], wo[r])
    unit1, scale1 = norm_parts(residual)
    first_out = unit1 * gain1 + shift1
    low[...] = first_out.astype(BF16)
    low_t[...] = first_out.T.astype(BF16)
    acc[...] = first_out + down_bias
    for copy in copies[-8:]:
        copy.wait()

    def forward(j, carry):
        x = nn(low[...], up[j]) + upb_ref[pl.ds(j, 1), :]
        pre[j] = x
        gate, _ = gelu_parts(x)
        a = (x * gate).astype(BF16)
        act[j] = a
        acc[...] += nn(a, down[j])
        return carry

    lax.fori_loop(0, 4, forward, 0)
    unit2, scale2 = norm_parts(acc[...])
    out_ref[...] = (unit2 * gain2 + shift2).astype(BF16)
    incoming = cot_ref[...].astype(F32)
    grad_second = norm_back(incoming, unit2, scale2, gain2)
    grad_down = grad_second.astype(BF16)
    sums_ref[0:1, :] = jnp.sum(incoming * unit2, axis=0, keepdims=True)
    sums_ref[1:2, :] = jnp.sum(incoming, axis=0, keepdims=True)
    sums_ref[2:3, :] = jnp.sum(grad_down.astype(F32), axis=0, keepdims=True)
    acc[...] = grad_second

    def give(outs, r, store):
        for i in range(4):

            @pl.when(r == i)
            def _(i=i):
                store(outs[2], (i // 2,)) if i % 2 else store(outs[i // 2], ())

    size = features // count

    def backward(j, carry):
        a = act[j]
        tmp[...] = tn(a, grad_down).astype(BF16)

        def store_down(ref, lead):
            for p in range(count):
                ref[(*lead, place(p ^ (dp % count), DOWN_ORDER))] = tmp[p * size : (p + 1) * size, :]

        give(down_out, seq ^ j, store_down)
        x = pre[j]
        gate, bend = gelu_parts(x)
        slope = gate + 0.5 * x * (1.0 - bend * bend) * (GELU_IN * (1.0 + 3.0 * GELU_CUBE * x * x))
        grad_act = nt(grad_down, down[j]).astype(BF16).astype(F32)
        grad_up = (grad_act * slope).astype(BF16)
        upsum_ref[pl.ds(j, 1), :] = jnp.sum(grad_up.astype(F32), axis=0, keepdims=True)
        acc[...] += nt(grad_up, up[j])
        tmp[...] = nn(low_t[...], grad_up).astype(BF16)
        for r in range(4):
            for h in range(2):
                at = pl.multiple_of((seq ^ r) * part + h * half, half)
                ref, lead = (up_out[2], (r // 2,)) if r % 2 else (up_out[r // 2], ())
                spot = place((2 * j + h) ^ (dp % count), UP_ORDER)
                ref[(*lead, spot, pl.ds(0, half))] = tmp[pl.ds(at, half), :]
        return carry

    lax.fori_loop(0, 4, backward, 0)
    grad_first = acc[...]
    grad_residual = norm_back(grad_first, unit1, scale1, gain1)
    res_ref[...] = grad_residual
    grad_out = grad_residual.astype(BF16)
    sums_ref[3:4, :] = jnp.sum(grad_first * unit1, axis=0, keepdims=True)
    sums_ref[4:5, :] = jnp.sum(grad_first, axis=0, keepdims=True)
    sums_ref[5:6, :] = jnp.sum(grad_out.astype(F32), axis=0, keepdims=True)
    for r in range(4):
        g_refs[r][...] = nt(wo[r], grad_out).astype(BF16)
        tall = part // count
        value = nn(a_refs[r][...], grad_out)
        ref, lead = (up_out[2], (r // 2,)) if r % 2 else (up_out[r // 2], ())
        for p in range(count):
            spot = place(p ^ (dp % count), UP_ORDER)
            ref[(*lead, spot, pl.ds(half, tall))] = value[p * tall : (p + 1) * tall].astype(BF16)


def middle(place_word, attended, embedded, cotangent, vectors, up_bias, pieces):
    rows, features = embedded.shape
    part = attended[0].shape[0]
    size = features // PIECES
    tall = size + part // PIECES
    kept = jax.ShapeDtypeStruct((PIECES, size, features), BF16)
    given = jax.ShapeDtypeStruct((2, PIECES, size, features), BF16)
    kept_up = jax.ShapeDtypeStruct((PIECES, tall, features), BF16)
    given_up = jax.ShapeDtypeStruct((2, PIECES, tall, features), BF16)
    hidden = 4 * features
    return pl.pallas_call(
        middle_kernel,
        in_specs=[pl.BlockSpec(memory_space=pltpu.SMEM)]
        + [whole_spec()] * 8
        + [pl.BlockSpec(memory_space=pl.ANY)] * 12,
        out_specs=[whole_spec()] * 14,
        out_shape=[
            jax.ShapeDtypeStruct((rows, features), BF16),
            jax.ShapeDtypeStruct((rows, features), F32),
        ]
        + [jax.ShapeDtypeStruct((part, rows), BF16)] * 4
        + [jax.ShapeDtypeStruct((6, features), F32), jax.ShapeDtypeStruct((4, features), F32)]
        + [kept, kept, given, kept_up, kept_up, given_up],
        scratch_shapes=[
            pltpu.VMEM((4, part, features), BF16),
            pltpu.VMEM((4, features, features), BF16),
            pltpu.VMEM((4, features, features), BF16),
            pltpu.VMEM((rows, features), BF16),
            pltpu.VMEM((features, rows), BF16),
            pltpu.VMEM((4, rows, features), BF16),
            pltpu.VMEM((4, rows, features), F32),
            pltpu.VMEM((rows, features), F32),
            pltpu.VMEM((features, features), BF16),
            pltpu.SemaphoreType.DMA((48,)),
        ],
        compiler_params=params(),
        cost_estimate=pl.CostEstimate(
            flops=12 * rows * features * hidden,
            bytes_accessed=30 * 1024 * 1024,
            transcendentals=2 * rows * hidden,
        ),
        name="middle",
    )(place_word, *attended, embedded, cotangent, vectors, up_bias, *pieces)


def settle_kernel(place_ref, *refs, order, store):
    held, outs = refs[:2], refs[2:]
    seq, dp = place_ref[0], place_ref[1] % PIECES
    half = PIECES // 2
    for index in range(PIECES):
        spot = place(index, order)
        store(outs, held[spot // half].at[spot % half], index ^ dp, seq)


def store_down(outs, piece, p, seq):
    size = piece.shape[0]
    outs[0][pl.ds(pl.multiple_of(p * size, size), size), :] = piece[...].astype(F32)


def store_up(outs, piece, p, seq):
    size = outs[0].shape[0] // 2
    wide = piece.shape[1]
    tall = piece.shape[0] - size
    row, column = pl.multiple_of((p % 2) * size, size), pl.multiple_of((p // 2) * wide, wide)
    outs[0][pl.ds(row, size), pl.ds(column, wide)] = piece[:size].astype(F32)
    outs[1][pl.ds(pl.multiple_of(p * tall, 8), tall), :] = piece[size:].astype(F32)


def store_heads(outs, piece, p, seq):
    tall, part = piece.shape[1], piece.shape[2] // 3
    for c in range(4):
        block = piece[seq ^ c].astype(F32)
        for i in range(3):
            outs[i][pl.ds(pl.multiple_of(p * tall, 8), tall), c * part : (c + 1) * part] = block[
                :, i * part : (i + 1) * part
            ]


def settle(place_word, held, order, store, shapes):
    return pl.pallas_call(
        functools.partial(settle_kernel, order=order, store=store),
        in_specs=[pl.BlockSpec(memory_space=pltpu.SMEM)] + [whole_spec()] * 2,
        out_specs=[whole_spec()] * len(shapes),
        out_shape=[jax.ShapeDtypeStruct(shape, F32) for shape in shapes],
        compiler_params=params(),
        cost_estimate=pl.CostEstimate(flops=0, bytes_accessed=4 * 1024 * 1024, transcendentals=0),
        name="settle",
    )(place_word, *held)


def reduce_dp(x, orders):
    for by in orders:
        half = x.shape[0] // 2
        x = x[:half].astype(F32) + swap(x[half:].astype(BF16), "dp", by).astype(F32)
    return x


def reduce_rest(x):
    for by in bits("dp")[3:]:
        x = x.astype(F32) + swap(x.astype(BF16), "dp", by).astype(F32)
    return x.astype(BF16)


def spread_dp(x, order):
    for by in reversed(order[1:]):
        x = jnp.concatenate([x, swap(x, "dp", by)])
    return x, swap(x, "dp", order[0])


def body(
    text_embed,
    region_feature,
    token_mask,
    segment_mask,
    mask_vector,
    batch_gain,
    batch_shift,
    query_weight,
    query_bias,
    key_weight,
    value_weight,
    value_bias,
    output_weight,
    output_bias,
    first_gain,
    first_shift,
    up_weight,
    up_bias,
    down_weight,
    down_bias,
    second_gain,
    second_shift,
    cotangent,
):
    documents, span, features = text_embed.shape
    rows = documents * span
    seq, dp = lax.axis_index("seq"), lax.axis_index("dp")
    group = lax.axis_size("seq")
    population = rows * lax.axis_size("dp") * group
    score_scale = 1.0 / math.sqrt(HEAD_DIM)
    part = features // group
    heads = part // HEAD_DIM

    region = region_feature.astype(F32).reshape(rows, features)
    sums = sum_all(jnp.stack([jnp.sum(region, axis=0), jnp.sum(region * region, axis=0)]))
    average = sums[0] / population
    inverse = lax.rsqrt(sums[1] / population - average * average + EPS_BATCH)

    cut = (
        jnp.stack([query_weight, key_weight, value_weight])
        .reshape(3, part, group, part)
        .transpose(2, 0, 1, 3)
    )
    head_blocks = exchange_blocks(
        [lax.dynamic_index_in_dim(cut, seq ^ r, 0, keepdims=False) for r in range(group)]
    )
    bias3 = jnp.stack([query_bias, jnp.zeros_like(query_bias), value_bias]).reshape(3, group, part)
    head_bias = lax.dynamic_slice_in_dim(bias3, seq, 1, 1)

    half = part // 2
    early = jnp.concatenate(
        [
            output_weight.reshape(2, half, features),
            up_weight.reshape(2, half, group, features).transpose(0, 2, 1, 3).reshape(2, group * half, features),
        ],
        axis=1,
    )
    pieces = gather_weight(early, dp) + gather_weight(down_weight.reshape(2, -1, features), dp)

    standard = (region - average) * inverse
    token_hit = token_mask.astype(F32).reshape(rows, 1)
    segment_keep = 1.0 - segment_mask.astype(F32).reshape(rows, 1)
    embedded = (
        text_embed.astype(F32).reshape(rows, features) * (1.0 - token_hit)
        + token_hit * mask_vector
        + segment_keep * (standard * batch_gain + batch_shift)
    )
    low_in = embedded.astype(BF16).reshape(documents, span, features)

    place_word = jnp.stack([seq, dp]).astype(jnp.int32)
    x_blocks = gather_rows(low_in)
    q, k, v, head_weight, *attended = attend(place_word, x_blocks, head_blocks, head_bias)
    attn_blocks = exchange_blocks(attended)

    vectors = jnp.stack([output_bias, first_gain, first_shift, down_bias, second_gain, second_shift])
    layer_output, grad_residual, *rest = middle(
        place_word,
        attn_blocks,
        embedded,
        cotangent.reshape(rows, features),
        vectors,
        up_bias.reshape(group, features),
        pieces,
    )
    grad_attn, (middle_sums, up_sums) = rest[:4], rest[4:6]
    down_keep, down_far, down_give, up_keep, up_far, up_give = rest[6:]

    got = swap(down_give, "seq", 1)
    pass_on = (down_far.astype(F32) + got[1].astype(F32)).astype(BF16)
    own = down_keep.astype(F32) + got[0].astype(F32) + swap(pass_on, "seq", 2).astype(F32)
    own = reduce_rest(reduce_dp(own, DOWN_ORDER))
    (total_down,) = settle(
        place_word, spread_dp(own, DOWN_ORDER), DOWN_ORDER, store_down, [down_weight.shape]
    )

    got = swap(up_give, "seq", 1)
    both = jnp.stack(
        [up_keep.astype(F32) + got[0].astype(F32), up_far.astype(F32) + got[1].astype(F32)], axis=1
    )
    both = reduce_dp(both, UP_ORDER[:1])
    own = both[:, 0] + swap(both[:, 1].astype(BF16), "seq", 2).astype(F32)
    own = reduce_rest(reduce_dp(own, UP_ORDER[1:]))
    total_up, total_out = settle(
        place_word, spread_dp(own, UP_ORDER), UP_ORDER, store_up, [up_weight.shape, output_weight.shape]
    )

    g_blocks = exchange_blocks(grad_attn)
    keep, give, term_heads, head_sums = attend_back(place_word, g_blocks, x_blocks, q, k, v, head_weight)
    query_sums, value_sums = head_sums[0], head_sums[1]
    inner = scatter_pairs(keep, give).reshape(rows, features)
    own = reduce_rest(reduce_dp(term_heads, HEAD_ORDER))
    own = jnp.stack(exchange_blocks([own[:, r] for r in range(group)]), axis=1)
    total_query, total_key, total_value = settle(
        place_word, spread_dp(own, HEAD_ORDER), HEAD_ORDER, store_heads, [query_weight.shape] * 3
    )

    grad_embedded = grad_residual + inner
    text_gradient = (grad_embedded * (1.0 - token_hit)).astype(BF16)
    grad_normed = grad_embedded * segment_keep

    def widen(x):
        return lax.dynamic_update_slice_in_dim(jnp.zeros((features,), F32), x, seq * part, 0)

    sums = sum_all(
        jnp.concatenate(
            [
                jnp.stack(
                    [
                        jnp.sum(grad_normed * standard, axis=0),
                        jnp.sum(grad_normed, axis=0),
                        jnp.sum(grad_embedded * token_hit, axis=0),
                        widen(query_sums),
                        widen(value_sums),
                    ]
                ),
                middle_sums,
                up_sums,
            ]
        )
    )
    (
        sum_gain,
        sum_shift,
        sum_mask,
        sum_query_bias,
        sum_value_bias,
        sum_second_gain,
        sum_second_shift,
        sum_down_bias,
        sum_first_gain,
        sum_first_shift,
        sum_output_bias,
    ) = sums[:11]
    sum_up_bias = sums[11:].reshape(-1)

    region_gradient = (
        batch_gain
        * inverse
        * (grad_normed - sum_shift / population - standard * (sum_gain / population))
    ).astype(BF16)
    shape = (documents, span, features)
    return (
        layer_output.reshape(shape),
        text_gradient.reshape(shape),
        region_gradient.reshape(shape),
        sum_mask,
        sum_gain,
        sum_shift,
        total_query,
        sum_query_bias,
        total_key,
        total_value,
        sum_value_bias,
        total_out,
        sum_output_bias,
        sum_first_gain,
        sum_first_shift,
        total_up,
        sum_up_bias,
        total_down,
        sum_down_bias,
        sum_second_gain,
        sum_second_shift,
    )


def solution(mesh):
    rows, weight, copied = P("dp", "seq", None), P("seq", None), P()
    mask = P("dp", "seq")
    in_specs = (
        (rows, rows, mask, mask, copied, copied, copied)
        + (weight, copied, weight, weight, copied, weight, copied, copied, copied)
        + (weight, copied, weight, copied, copied, copied, rows)
    )
    out_specs = (
        (rows, rows, rows, copied, copied, copied)
        + (weight, copied, weight, weight, copied, weight, copied, copied, copied)
        + (weight, copied, weight, copied, copied, copied)
    )
    return jax.shard_map(body, mesh=mesh, in_specs=in_specs, out_specs=out_specs, check_vma=False)
```

```python
import functools
import math

import jax
import jax.numpy as jnp
from jax import lax
from jax.experimental import pallas as pl
from jax.experimental.pallas import tpu as pltpu
from jax.sharding import PartitionSpec as P

HEAD_DIM = 64
EPS_NORM = 1e-12
EPS_BATCH = 1e-05
F32 = jnp.float32
BF16 = jnp.bfloat16
GELU_IN = math.sqrt(2.0 / math.pi)
GELU_CUBE = 0.044715
PIECES = 8
NEAR = 4
DOWN_ORDER = (2, 1, 4)
UP_ORDER = (1, 2, 4)
HEAD_ORDER = (1, 2, 4)


def swap(x, axis, by):
    return lax.ppermute(x, axis, [(i, i ^ by) for i in range(lax.axis_size(axis))])


def bits(axis):
    found, by = [], 1
    while by < lax.axis_size(axis):
        found.append(by)
        by *= 2
    return found


def sum_all(x):
    for axis in ("seq", "dp"):
        for by in bits(axis):
            x = x + swap(x, axis, by)
    return x


def nn(a, b):
    return jnp.dot(a, b, preferred_element_type=F32)


def tn(a, b):
    return lax.dot_general(a, b, (((0,), (0,)), ((), ())), preferred_element_type=F32)


def nt(a, b):
    return lax.dot_general(a, b, (((1,), (1,)), ((), ())), preferred_element_type=F32)


def norm_parts(x):
    centred = x - jnp.mean(x, axis=-1, keepdims=True)
    scale = lax.rsqrt(jnp.mean(centred * centred, axis=-1, keepdims=True) + EPS_NORM)
    return centred * scale, scale


def norm_back(grad, unit, scale, gain):
    g = grad * gain
    return scale * (
        g
        - jnp.mean(g, axis=-1, keepdims=True)
        - unit * jnp.mean(g * unit, axis=-1, keepdims=True)
    )


def gather_rows(x):
    two = swap(x, "seq", 2)
    one, three = swap(x, "seq", 1), swap(two, "seq", 1)
    return [x, one, two, three]


def gather_weight(halves, mine, by):
    near = swap(mine, "seq", 2)
    far = swap(near, "dp", by)
    return [halves, near, far, swap(halves, "seq", 1), swap(near, "seq", 1), swap(far, "seq", 1)]


def scatter_pairs(keep, give):
    got = swap(give, "seq", 1)
    pass_on = (keep[1].astype(F32) + got[1].astype(F32)).astype(BF16)
    own = keep[0].astype(F32) + got[0].astype(F32)
    return own + swap(pass_on, "seq", 2).astype(F32)


def exchange_blocks(blocks):
    return [blocks[0]] + [swap(blocks[r], "seq", r) for r in (1, 2, 3)]


def params(mebibytes):
    return pltpu.CompilerParams(vmem_limit_bytes=mebibytes * 1024 * 1024)


def whole_spec():
    return pl.BlockSpec(memory_space=pltpu.VMEM)


def pack_heads_kernel(place_ref, q_ref, k_ref, v_ref, *head_refs):
    seq = place_ref[0]
    part = q_ref.shape[0]
    for c in range(4):
        for r in range(4):

            @pl.when(seq == c ^ r)
            def _(c=c, r=r):
                for i, ref in enumerate((q_ref, k_ref, v_ref)):
                    head_refs[r][:, i * part : (i + 1) * part] = ref[:, c * part : (c + 1) * part]


def pack_halves_kernel(place_ref, out_ref, up_ref, halves_ref, near_ref):
    bit = place_ref[1] % 2
    half = out_ref.shape[0] // 2
    wide = out_ref.shape[1]

    def cut(rows):
        blocks = [out_ref[rows, :]] + [up_ref[rows, j * wide : (j + 1) * wide] for j in range(4)]
        return jnp.concatenate(blocks, axis=0)

    for h in range(2):
        halves_ref[h] = cut(pl.ds(h * half, half))
    near_ref[...] = cut(pl.ds(pl.multiple_of(bit * half, half), half))


def pack(place_word, query, key, value, out, up):
    part, features = out.shape
    tall = part // 2 * 5
    heads = pl.pallas_call(
        pack_heads_kernel,
        in_specs=[pl.BlockSpec(memory_space=pltpu.SMEM)] + [whole_spec()] * 3,
        out_specs=[whole_spec()] * 4,
        out_shape=[shaped(part, 3 * part)] * 4,
        compiler_params=params(56),
        cost_estimate=pl.CostEstimate(flops=0, bytes_accessed=2 * 1024 * 1024, transcendentals=0),
        name="pack_heads",
    )(place_word, query, key, value)
    halves, near = pl.pallas_call(
        pack_halves_kernel,
        in_specs=[pl.BlockSpec(memory_space=pltpu.SMEM)] + [whole_spec()] * 2,
        out_specs=[whole_spec()] * 2,
        out_shape=[shaped(2, tall, features), shaped(tall, features)],
        compiler_params=params(56),
        cost_estimate=pl.CostEstimate(flops=0, bytes_accessed=4 * 1024 * 1024, transcendentals=0),
        name="pack_halves",
    )(place_word, out, up)
    return heads, halves, near


def attend_kernel(seq_ref, *refs, waits):
    x_refs, w_refs, bias_ref, refs = refs[:4], refs[4:8], refs[8], refs[9 + waits :]
    q_ref, k_ref, v_ref, wc_ref, out_refs = refs[0], refs[1], refs[2], refs[3], refs[4:]
    part = w_refs[0].shape[0]
    span = x_refs[0].shape[1]

    @pl.when(pl.program_id(0) == 0)
    def _():
        for r in range(4):
            at = pl.multiple_of((seq_ref[0] ^ r) * part, part)
            for i in range(3):
                wc_ref[i, pl.ds(at, part), :] = w_refs[r][:, i * part : (i + 1) * part]

    x = jnp.concatenate([ref[0] for ref in x_refs], axis=0)
    for i, ref in enumerate((q_ref, k_ref, v_ref)):
        ref[0] = (nn(x, wc_ref[i]) + bias_ref[i]).astype(BF16)
    q, k, v = q_ref[0], k_ref[0], v_ref[0]
    lane = lax.broadcasted_iota(jnp.int32, (1, part), 1) // HEAD_DIM
    for h in range(part // HEAD_DIM):
        pick = jnp.where(lane == h, 1.0 / math.sqrt(HEAD_DIM), 0.0).astype(BF16)
        scores = nt(k, q * pick)
        raised = jnp.exp(scores - jnp.max(scores, axis=0, keepdims=True))
        chances = (raised * (1.0 / jnp.sum(raised, axis=0, keepdims=True))).astype(BF16)
        attended = tn(v, chances)[h * HEAD_DIM : (h + 1) * HEAD_DIM].astype(BF16)
        for r in range(4):
            out_refs[r][h * HEAD_DIM : (h + 1) * HEAD_DIM, :] = attended[:, r * span : (r + 1) * span]


def attend(seq, x_blocks, w_blocks, bias, after):
    documents, span, features = x_blocks[0].shape
    part = w_blocks[0].shape[0]
    length = 4 * span
    flops = documents * (2 * length * features * 3 * part + 4 * length * length * part)
    per_doc = pl.BlockSpec((1, length, part), lambda d: (d, 0, 0))
    return pl.pallas_call(
        functools.partial(attend_kernel, waits=len(after)),
        grid=(documents,),
        in_specs=[pl.BlockSpec(memory_space=pltpu.SMEM)]
        + [pl.BlockSpec((1, span, features), lambda d: (d, 0, 0))] * 4
        + [pl.BlockSpec((part, 3 * part), lambda d: (0, 0))] * 4
        + [pl.BlockSpec((3, 1, part), lambda d: (0, 0, 0))]
        + [any_spec()] * len(after),
        out_specs=[per_doc] * 3
        + [pl.BlockSpec((3, features, part), lambda d: (0, 0, 0))]
        + [pl.BlockSpec((part, span), lambda d: (0, d))] * 4,
        out_shape=[jax.ShapeDtypeStruct((documents, length, part), BF16)] * 3
        + [jax.ShapeDtypeStruct((3, features, part), BF16)]
        + [jax.ShapeDtypeStruct((part, documents * span), BF16)] * 4,
        compiler_params=params(56),
        cost_estimate=pl.CostEstimate(
            flops=flops, bytes_accessed=8 * 1024 * 1024, transcendentals=documents * length * length * 3
        ),
        name="attend",
    )(seq, *x_blocks, *w_blocks, bias, *after)


def attend_back_kernel(place_ref, *refs, waits):
    g_refs, x_refs = refs[:4], refs[4:8]
    q_ref, k_ref, v_ref, wc_ref = refs[8:12]
    keep_ref, give_ref, dw_keep_ref, dw_give_ref, sums_ref, acc_ref = refs[12 + waits :]
    part = q_ref.shape[2]
    span = x_refs[0].shape[1]
    first = pl.program_id(0) == 0
    q, k, v = q_ref[0], k_ref[0], v_ref[0]
    g = jnp.concatenate([ref[...] for ref in g_refs], axis=1)
    lane = lax.broadcasted_iota(jnp.int32, (1, part), 1) // HEAD_DIM
    scale = 1.0 / math.sqrt(HEAD_DIM)
    dq = dk = dv = None
    for h in range(part // HEAD_DIM):
        on = lane == h
        pick = jnp.where(on, scale, 0.0).astype(BF16)
        mask = jnp.where(on, 1.0, 0.0)
        scores = nt(k, q * pick)
        raised = jnp.exp(scores - jnp.max(scores, axis=0, keepdims=True))
        chances = raised * (1.0 / jnp.sum(raised, axis=0, keepdims=True))
        grad = nn(v * mask.astype(BF16), g)
        both = chances * grad
        grad = (both - chances * jnp.sum(both, axis=0, keepdims=True)).astype(BF16)
        part_v = nt(chances.astype(BF16), g) * mask
        part_k = nn(grad, q) * (mask * scale)
        part_q = tn(grad, k) * (mask * scale)
        dq = part_q if dq is None else dq + part_q
        dk = part_k if dk is None else dk + part_k
        dv = part_v if dv is None else dv + part_v
    low = [t.astype(BF16) for t in (dq, dk, dv)]
    sums = jnp.concatenate(
        [jnp.sum(low[i].astype(F32), axis=0, keepdims=True) for i in (0, 2)], axis=0
    )
    x = jnp.concatenate([ref[0] for ref in x_refs], axis=0)
    x_t = x.T
    inner = nt(low[0], wc_ref[0]) + nt(low[1], wc_ref[1]) + nt(low[2], wc_ref[2])
    inner = inner.astype(BF16)
    for r in range(4):
        (give_ref if r % 2 else keep_ref)[r // 2, 0] = inner[r * span : (r + 1) * span]

    @pl.when(first)
    def _():
        sums_ref[...] = sums
        for i in range(3):
            acc_ref[i] = nn(x_t, low[i])

    @pl.when(jnp.logical_not(first))
    def _():
        sums_ref[...] += sums
        for i in range(3):
            acc_ref[i] += nn(x_t, low[i])

    @pl.when(pl.program_id(0) == pl.num_programs(0) - 1)
    def _():
        tall = part // PIECES
        dp = place_ref[1] % NEAR
        first = HEAD_ORDER[0]
        for p in range(PIECES):
            spot = place(p ^ dp, HEAD_ORDER[1:])
            for mine, ref in ((True, dw_keep_ref), (False, dw_give_ref)):

                @pl.when(((p ^ dp) // first % 2 == 0) == mine)
                def _(p=p, spot=spot, ref=ref):
                    for block in range(4):
                        at = block * part + p * tall
                        for i in range(3):
                            ref[spot, place_ref[0] ^ block, :, i * part : (i + 1) * part] = acc_ref[
                                i, at : at + tall, :
                            ].astype(BF16)


def attend_back(place_word, g_blocks, x_blocks, q, k, v, wc, after):
    documents, span, features = x_blocks[0].shape
    part = q.shape[2]
    length = 4 * span
    flops = documents * (4 * length * features * 3 * part + 10 * length * length * part)
    per_doc = pl.BlockSpec((1, length, part), lambda d: (d, 0, 0))
    pair = pl.BlockSpec((2, 1, span, features), lambda d: (0, d, 0, 0))
    return pl.pallas_call(
        functools.partial(attend_back_kernel, waits=len(after)),
        grid=(documents,),
        in_specs=[pl.BlockSpec(memory_space=pltpu.SMEM)]
        + [pl.BlockSpec((part, span), lambda d: (0, d))] * 4
        + [pl.BlockSpec((1, span, features), lambda d: (d, 0, 0))] * 4
        + [per_doc] * 3
        + [pl.BlockSpec((3, features, part), lambda d: (0, 0, 0))]
        + [any_spec()] * len(after),
        out_specs=[
            pair,
            pair,
            pl.BlockSpec((PIECES // 2, 4, part // PIECES, 3 * part), lambda d: (0, 0, 0, 0)),
            pl.BlockSpec((PIECES // 2, 4, part // PIECES, 3 * part), lambda d: (0, 0, 0, 0)),
            pl.BlockSpec((2, part), lambda d: (0, 0)),
        ],
        out_shape=[jax.ShapeDtypeStruct((2, documents, span, features), BF16)] * 2
        + [
            jax.ShapeDtypeStruct((PIECES // 2, 4, part // PIECES, 3 * part), BF16),
            jax.ShapeDtypeStruct((PIECES // 2, 4, part // PIECES, 3 * part), BF16),
            jax.ShapeDtypeStruct((2, part), F32),
        ],
        scratch_shapes=[pltpu.VMEM((3, features, part), F32)],
        compiler_params=params(56),
        cost_estimate=pl.CostEstimate(
            flops=flops, bytes_accessed=12 * 1024 * 1024, transcendentals=documents * length * length * 3
        ),
        name="attend_back",
    )(place_word, *g_blocks, *x_blocks, q, k, v, wc, *after)


def gelu_parts(x):
    square = x * x
    bend = jnp.tanh(GELU_IN * x * (1.0 + GELU_CUBE * square))
    gate = 0.5 * (1.0 + bend)
    rise = 0.5 * x * (1.0 - bend * bend) * (GELU_IN + 3.0 * GELU_IN * GELU_CUBE * square)
    return x * gate, gate + rise


def place(index, order):
    at = 0
    for by in order:
        at = 2 * at + (index // by) % 2
    return at


def weight_copies(place_ref, pieces, wo, up, down, sems):
    seq, dp = place_ref[0], place_ref[1]
    part = wo.shape[1]
    half = part // 2
    wo_copies, up_copies, down_copies = [], [[] for _ in range(4)], [[] for _ in range(4)]

    def bring(found, source, target):
        found.append(pltpu.make_async_copy(source, target, sems.at[sum(used)]))
        used.append(1)

    used = []
    own, near, far, one, near_one, far_one = pieces[:6]
    bit = dp % 2
    parts = [(own.at[h], 0, h) for h in range(2)] + [(one.at[h], 1, h) for h in range(2)]
    parts += [(near, 2, bit), (far, 2, 1 - bit), (near_one, 3, bit), (far_one, 3, 1 - bit)]
    for source, r, h in parts:
        at = pl.multiple_of(h * half, half)
        bring(wo_copies, source.at[pl.ds(0, half)], wo.at[r, pl.ds(at, half)])
        if up is None:
            continue
        at = pl.multiple_of((seq ^ r) * part + h * half, half)
        for i in range(4):
            start = pl.multiple_of(half * (1 + (seq ^ i)), half)
            bring(up_copies[i], source.at[pl.ds(start, half)], up.at[i, pl.ds(at, half)])
    for r in range(4 if down is not None else 0):
        bring(down_copies[r], pieces[6 + r], down.at[r])
    return wo_copies, up_copies, down_copies


def start_all(copies):
    for copy in copies:
        copy.start()


def wait_all(copies):
    for copy in copies:
        copy.wait()


def forward_kernel(place_ref, *refs):
    (a_refs, in_ref, cot_ref, vec_ref, upb_ref), refs = (refs[:4], *refs[4:8]), refs[8:]
    pieces, refs = refs[:10], refs[10:]
    out_ref, unit_ref, scale_ref, grad_ref, sums_ref, upsum_ref = refs[:6]
    outs = (refs[6:9], refs[9:12])
    wo, up, down, act, slope, low_t, spare, terms, sems, out_sems = refs[12:]
    seq, dp = place_ref[0], place_ref[1]
    part = wo.shape[1]
    half = part // 2
    size = terms.shape[3]

    wo_copies, up_copies, down_copies = weight_copies(place_ref, pieces, wo, up, down, sems)
    start_all(wo_copies + up_copies[0] + up_copies[1])
    out_bias, gain1, shift1, down_bias, gain2, shift2 = (vec_ref[i : i + 1, :] for i in range(6))
    residual = in_ref[...] + out_bias
    wait_all(wo_copies)
    joined = jnp.concatenate([ref[...] for ref in a_refs], axis=0)
    residual += tn(joined, wo[...].reshape(joined.shape[0], -1))
    unit1, scale1 = norm_parts(residual)
    unit_ref[...] = unit1
    scale_ref[...] = scale1
    first_out = unit1 * gain1 + shift1
    low = first_out.astype(BF16)
    for r in range(4):
        wait_all(up_copies[r])
        start_all(up_copies[r + 2] if r < 2 else down_copies[2 * r - 4] + down_copies[2 * r - 3])
        x = nn(low, up[r]) + upb_ref[pl.ds(seq ^ r, 1), :]
        value, rise = gelu_parts(x)
        act[r] = value.astype(BF16)
        slope[r] = rise
    second_in = first_out + down_bias
    for r in range(4):
        wait_all(down_copies[r])
        second_in += nn(act[r], down[r])
    unit2, scale2 = norm_parts(second_in)
    out_ref[...] = (unit2 * gain2 + shift2).astype(BF16)
    incoming = cot_ref[...].astype(F32)
    grad_first = norm_back(incoming, unit2, scale2, gain2)
    grad_down = grad_first.astype(BF16)
    sums_ref[0:1, :] = jnp.sum(incoming * unit2, axis=0, keepdims=True)
    sums_ref[1:2, :] = jnp.sum(incoming, axis=0, keepdims=True)
    sums_ref[2:3, :] = jnp.sum(grad_down.astype(F32), axis=0, keepdims=True)
    spare[...] = low.T
    for i in range(4):
        low_t[i * part : (i + 1) * part, :] = spare[pl.ds(pl.multiple_of((seq ^ i) * part, part), part), :]
    for r in range(4):
        grad_act = nt(grad_down, down[r]).astype(BF16).astype(F32)
        grad_up = (grad_act * slope[r]).astype(BF16)
        upsum_ref[pl.ds(seq ^ r, 1), :] = jnp.sum(grad_up.astype(F32), axis=0, keepdims=True)
        grad_first += nt(grad_up, up[r])
        value = nn(low_t[...], grad_up).astype(BF16)
        for i in range(4):
            for h in range(2):
                spot = place((2 * (seq ^ r) + h) ^ (dp % NEAR), UP_ORDER)
                at = i * part + h * half
                terms[1, i, spot] = value[at : at + half]
    grad_ref[...] = grad_first

    def send(which, r):
        keep_out, far_out, give_out = outs[which]
        target = (keep_out, give_out.at[0], far_out, give_out.at[1])[r]
        return pltpu.make_async_copy(terms.at[which, r], target, out_sems.at[which, r])

    start_all([send(1, r) for r in range(4)])
    for r in range(4):
        value = tn(act[r], grad_down)
        for p in range(PIECES):
            spot = place(p ^ (dp % NEAR), DOWN_ORDER)
            terms[0, r, spot] = value[p * size : (p + 1) * size].astype(BF16)
        send(0, r).start()
    wait_all([send(which, r) for which in range(2) for r in range(4)])


def backward_kernel(place_ref, *refs):
    (a_refs, unit_ref, scale_ref, grad_ref, vec_ref), refs = (refs[:4], *refs[4:8]), refs[8:]
    pieces, refs = refs[:6], refs[6:]
    res_ref, g_refs, sums_ref, keep_ref, far_ref, give_ref, wo, sems = refs[0], refs[1:5], *refs[5:]
    dp = place_ref[1]
    part = wo.shape[1]
    tall = part // PIECES
    copies = weight_copies(place_ref, pieces, wo, None, None, sems)[0]
    start_all(copies)
    unit1 = unit_ref[...]
    grad_first = grad_ref[...]
    grad_residual = norm_back(grad_first, unit1, scale_ref[...], vec_ref[1:2, :])
    res_ref[...] = grad_residual
    grad_out = grad_residual.astype(BF16)
    joined = jnp.concatenate([ref[...] for ref in a_refs], axis=0)
    value = nn(joined, grad_out)
    for r in range(4):
        for p in range(PIECES):
            spot = place(p ^ (dp % NEAR), DOWN_ORDER)
            piece = value[r * part + p * tall : r * part + (p + 1) * tall].astype(BF16)
            if r % 2:
                give_ref[r // 2, spot] = piece
            else:
                (far_ref if r else keep_ref)[spot] = piece
    sums_ref[0:1, :] = jnp.sum(grad_first * unit1, axis=0, keepdims=True)
    sums_ref[1:2, :] = jnp.sum(grad_first, axis=0, keepdims=True)
    sums_ref[2:3, :] = jnp.sum(grad_out.astype(F32), axis=0, keepdims=True)
    wait_all(copies)
    back = nt(wo[...].reshape(joined.shape[0], -1), grad_out).astype(BF16)
    for r in range(4):
        g_refs[r][...] = back[r * part : (r + 1) * part]


def shaped(*shape, dtype=BF16):
    return jax.ShapeDtypeStruct(shape, dtype)


def any_spec():
    return pl.BlockSpec(memory_space=pl.ANY)


def forward(place_word, attended, embedded, cotangent, vectors, up_bias, pieces):
    rows, features = embedded.shape
    part = attended[0].shape[0]
    size = features // PIECES
    term = [shaped(PIECES, size, features)] * 2 + [shaped(2, PIECES, size, features)]
    return pl.pallas_call(
        forward_kernel,
        in_specs=[pl.BlockSpec(memory_space=pltpu.SMEM)] + [whole_spec()] * 8 + [any_spec()] * 10,
        out_specs=[whole_spec()] * 6 + [any_spec()] * 6,
        out_shape=[
            shaped(rows, features),
            shaped(rows, features, dtype=F32),
            shaped(rows, 1, dtype=F32),
            shaped(rows, features, dtype=F32),
            shaped(3, features, dtype=F32),
            shaped(4, features, dtype=F32),
        ]
        + term
        + term,
        scratch_shapes=[
            pltpu.VMEM((4, part, features), BF16),
            pltpu.VMEM((4, features, features), BF16),
            pltpu.VMEM((4, features, features), BF16),
            pltpu.VMEM((4, rows, features), BF16),
            pltpu.VMEM((4, rows, features), F32),
            pltpu.VMEM((features, rows), BF16),
            pltpu.VMEM((features, rows), BF16),
            pltpu.VMEM((2, 4, PIECES, size, features), BF16),
            pltpu.SemaphoreType.DMA((44,)),
            pltpu.SemaphoreType.DMA((2, 4)),
        ],
        compiler_params=params(56),
        cost_estimate=pl.CostEstimate(
            flops=12 * rows * features * 4 * features,
            bytes_accessed=26 * 1024 * 1024,
            transcendentals=rows * 4 * features,
        ),
        name="forward",
    )(place_word, *attended, embedded, cotangent, vectors, up_bias, *pieces)


def backward(place_word, attended, unit, scale, grad, vectors, pieces):
    rows, features = unit.shape
    part = attended[0].shape[0]
    piece = (PIECES, part // PIECES, features)
    return pl.pallas_call(
        backward_kernel,
        in_specs=[pl.BlockSpec(memory_space=pltpu.SMEM)] + [whole_spec()] * 8 + [any_spec()] * 6,
        out_specs=[whole_spec()] * 9,
        out_shape=[shaped(rows, features, dtype=F32)]
        + [shaped(part, rows)] * 4
        + [shaped(3, features, dtype=F32), shaped(*piece), shaped(*piece), shaped(2, *piece)],
        scratch_shapes=[pltpu.VMEM((4, part, features), BF16), pltpu.SemaphoreType.DMA((44,))],
        compiler_params=params(56),
        cost_estimate=pl.CostEstimate(
            flops=4 * rows * features * features, bytes_accessed=6 * 1024 * 1024, transcendentals=rows
        ),
        name="backward",
    )(place_word, *attended, unit, scale, grad, vectors, *pieces)


def fold_kernel(*refs, body, inputs, waits):
    body(refs[:inputs], refs[inputs + waits :])


def fold(body, arrays, shapes, after, name):
    return pl.pallas_call(
        functools.partial(fold_kernel, body=body, inputs=len(arrays), waits=len(after)),
        in_specs=[whole_spec()] * len(arrays) + [any_spec()] * len(after),
        out_specs=[whole_spec()] * len(shapes),
        out_shape=[shaped(*shape) for shape in shapes],
        compiler_params=params(40),
        cost_estimate=pl.CostEstimate(flops=0, bytes_accessed=4 * 1024 * 1024, transcendentals=0),
        name=name,
    )(*arrays, *after)


def added(*values):
    return sum(v.astype(F32) for v in values[1:]) + values[0].astype(F32)


def fold_down_core(ins, outs):
    keeps, fars, gots = ins[0:2], ins[2:4], ins[4:6]
    size = keeps[0].shape[1]
    half = keeps[0].shape[0] // 2
    for i, mine in enumerate((keeps, fars)):
        for ref, got, rows in zip(mine, gots, (slice(0, size), slice(size, None))):
            total = added(ref[...], got[i]).astype(BF16)
            outs[0][:, i, rows] = total[:half]
            outs[1][:, i, rows] = total[half:]


def fold_up_core(ins, outs):
    keep, far, got = ins
    outs[0][...] = added(keep[...], got[0]).astype(BF16)
    outs[1][...] = added(far[...], got[1]).astype(BF16)


def fold_both(ins, outs):
    down, down_got, up, up_got = ins
    half = up.shape[0] // 2
    outs[0][...] = added(down[:, 0], down_got[:, 0]).astype(BF16)
    outs[1][...] = added(down[:, 1], down_got[:, 1]).astype(BF16)
    outs[2][...] = added(up[:half], up_got[:half]).astype(BF16)
    outs[3][...] = added(up[half:], up_got[half:]).astype(BF16)


def settle_kernel(place_ref, *refs, order, store):
    held, outs = refs[:2], refs[2:]
    seq, dp = place_ref[0], place_ref[1] % NEAR
    half = PIECES // 2
    for index in range(PIECES):
        spot = place(index, order)
        store(outs, held[spot // half].at[spot % half], index ^ dp, seq)


def store_down(outs, piece, p, seq):
    size, tall = (ref.shape[0] // PIECES for ref in outs)
    outs[0][pl.ds(pl.multiple_of(p * size, size), size), :] = piece[:size].astype(F32)
    outs[1][pl.ds(pl.multiple_of(p * tall, 8), tall), :] = piece[size:].astype(F32)


def store_up(outs, piece, p, seq):
    size, wide = piece.shape
    row, column = pl.multiple_of((p % 2) * size, size), pl.multiple_of((p // 2) * wide, wide)
    outs[0][pl.ds(row, size), pl.ds(column, wide)] = piece[...].astype(F32)


def store_heads(outs, piece, p, seq):
    tall, part = piece.shape[1], piece.shape[2] // 3
    rows = pl.ds(pl.multiple_of(p * tall, 8), tall)
    for c in range(4):
        columns = slice(c * part, (c + 1) * part)
        block = piece[seq ^ c].astype(F32)
        for i in range(3):
            outs[i][rows, columns] = block[:, i * part : (i + 1) * part]


def settle(place_word, held, order, store, shapes):
    return pl.pallas_call(
        functools.partial(settle_kernel, order=order, store=store),
        in_specs=[pl.BlockSpec(memory_space=pltpu.SMEM)] + [whole_spec()] * 2,
        out_specs=[whole_spec()] * len(shapes),
        out_shape=[jax.ShapeDtypeStruct(shape, F32) for shape in shapes],
        compiler_params=params(56),
        cost_estimate=pl.CostEstimate(flops=0, bytes_accessed=4 * 1024 * 1024, transcendentals=0),
        name="settle",
    )(place_word, *held)


def follow(x, *others):
    for other in others:
        x = x + jnp.minimum(jnp.abs(other[(0,) * other.ndim].astype(F32)), 0.0).astype(x.dtype)
    return x


def reduce_dp(x, orders):
    for by in orders:
        half = x.shape[0] // 2
        x = x[:half].astype(F32) + swap(x[half:].astype(BF16), "dp", by).astype(F32)
    return x


def reduce_rest(x, last):
    for by in (last, *bits("dp")[3:]):
        x = x.astype(BF16)
        x = x.astype(F32) + swap(x, "dp", by).astype(F32)
    return x.astype(BF16)


def spread_dp(x, order):
    for by in reversed(order[1:-1]):
        x = jnp.concatenate([x, swap(x, "dp", by)])
    return x, swap(x, "dp", order[0])


def body(
    text_embed,
    region_feature,
    token_mask,
    segment_mask,
    mask_vector,
    batch_gain,
    batch_shift,
    query_weight,
    query_bias,
    key_weight,
    value_weight,
    value_bias,
    output_weight,
    output_bias,
    first_gain,
    first_shift,
    up_weight,
    up_bias,
    down_weight,
    down_bias,
    second_gain,
    second_shift,
    cotangent,
):
    documents, span, features = text_embed.shape
    rows = documents * span
    seq, dp = lax.axis_index("seq"), lax.axis_index("dp")
    group = lax.axis_size("seq")
    population = rows * lax.axis_size("dp") * group
    score_scale = 1.0 / math.sqrt(HEAD_DIM)
    part = features // group
    heads = part // HEAD_DIM

    place_word = jnp.stack([seq, dp]).astype(jnp.int32)
    cut, halves, mine = pack(
        place_word, query_weight, key_weight, value_weight, output_weight, up_weight
    )

    region = region_feature.astype(F32).reshape(rows, features)
    sums = jnp.stack([jnp.sum(region, axis=0), jnp.sum(region * region, axis=0)])
    chip_sums = sums + swap(sums, "seq", 2)
    chip_sums = follow(chip_sums, cut[0], mine)
    sums = chip_sums + swap(chip_sums, "seq", 1)
    for by in bits("dp"):
        sums = sums + swap(sums, "dp", by)
    average = sums[0] / population
    inverse = lax.rsqrt(sums[1] / population - average * average + EPS_BATCH)

    head_blocks = exchange_blocks(cut)
    bias3 = jnp.stack([query_bias, jnp.zeros_like(query_bias), value_bias]).reshape(3, group, part)
    head_bias = lax.dynamic_slice_in_dim(bias3, seq, 1, 1)
    pieces = gather_weight(halves, mine, 1)

    standard = (region - average) * inverse
    token_hit = token_mask.astype(F32).reshape(rows, 1)
    segment_keep = 1.0 - segment_mask.astype(F32).reshape(rows, 1)
    embedded = (
        text_embed.astype(F32).reshape(rows, features) * (1.0 - token_hit)
        + token_hit * mask_vector
        + segment_keep * (standard * batch_gain + batch_shift)
    )
    low_in = follow(embedded, head_blocks[2], head_blocks[3]).astype(BF16).reshape(documents, span, features)
    x_blocks = gather_rows(low_in)
    far = swap(follow(down_weight, low_in, pieces[1]), "seq", 2)
    q, k, v, head_weight, *attended = attend(place_word, x_blocks, head_blocks, head_bias, [])
    attn_blocks = exchange_blocks(attended)
    far = follow(far, attended[0])
    pieces += [down_weight, swap(down_weight, "seq", 1), far, swap(far, "seq", 1)]
    vectors = jnp.stack([output_bias, first_gain, first_shift, down_bias, second_gain, second_shift])
    layer_output, unit, scale, grad_first, second_sums, up_sums, *terms = forward(
        place_word,
        attn_blocks,
        embedded,
        cotangent.reshape(rows, features),
        vectors,
        up_bias.reshape(group, features),
        pieces,
    )
    grad_residual, *rest = backward(place_word, attn_blocks, unit, scale, grad_first, vectors, pieces[:6])
    grad_attn, first_sums, (out_keep, out_far, out_give) = rest[:4], rest[4], rest[5:]
    down_keep, down_far, down_give = terms[:3]
    up_keep, up_far, up_give = terms[3:]

    half = PIECES // 2
    size, tall = features // PIECES, part // PIECES
    g_blocks = exchange_blocks(grad_attn)
    down, down_send = fold(
        fold_down_core,
        [down_keep, out_keep, down_far, out_far, swap(down_give, "seq", 1), swap(out_give, "seq", 1)],
        [(half, 2, size + tall, features)] * 2,
        [],
        "down_core",
    )
    up, up_send = fold(
        fold_up_core,
        [up_keep, up_far, swap(up_give, "seq", 1)],
        [(PIECES, size, features)] * 2,
        [g_blocks[2], g_blocks[3]],
        "up_core",
    )

    keep, give, heads, heads_send, head_sums = attend_back(
        place_word, g_blocks, x_blocks, q, k, v, head_weight, [down_send, up_send]
    )
    query_sums, value_sums = head_sums[0], head_sums[1]

    got = swap(give, "seq", 1)
    inner_send = (keep[1].astype(F32) + got[1].astype(F32)).astype(BF16)
    inner_own = keep[0].astype(F32) + got[0].astype(F32)

    down, down_send, up, up_send = fold(
        fold_both,
        [down, swap(down_send, "dp", DOWN_ORDER[0]), up, swap(up_send, "seq", 2)],
        [(half, size + tall, features)] * 2 + [(half, size, features)] * 2,
        [inner_send],
        "both",
    )
    own = up.astype(F32) + swap(up_send, "dp", UP_ORDER[0]).astype(F32)
    own = reduce_rest(reduce_dp(own, UP_ORDER[1:-1]), UP_ORDER[-1])
    (total_up,) = settle(place_word, spread_dp(own, UP_ORDER), UP_ORDER, store_up, [up_weight.shape])

    own = down.astype(F32) + swap(down_send, "seq", 2).astype(F32)
    own = reduce_rest(reduce_dp(own, DOWN_ORDER[1:-1]), DOWN_ORDER[-1])
    total_down, total_out = settle(
        place_word,
        spread_dp(own, DOWN_ORDER),
        DOWN_ORDER,
        store_down,
        [down_weight.shape, output_weight.shape],
    )

    inner = (inner_own + swap(inner_send, "seq", 2).astype(F32)).reshape(rows, features)
    heads = heads.astype(F32) + swap(heads_send, "dp", HEAD_ORDER[0]).astype(F32)
    own = reduce_rest(reduce_dp(heads, HEAD_ORDER[1:-1]), HEAD_ORDER[-1])
    own = jnp.stack(exchange_blocks([own[:, r] for r in range(group)]), axis=1)
    total_query, total_key, total_value = settle(
        place_word, spread_dp(own, HEAD_ORDER), HEAD_ORDER, store_heads, [query_weight.shape] * 3
    )

    grad_embedded = grad_residual + inner
    text_gradient = (grad_embedded * (1.0 - token_hit)).astype(BF16)
    grad_normed = grad_embedded * segment_keep

    def widen(x):
        return lax.dynamic_update_slice_in_dim(jnp.zeros((features,), F32), x, seq * part, 0)

    sums = sum_all(
        jnp.concatenate(
            [
                jnp.stack(
                    [
                        jnp.sum(grad_normed * standard, axis=0),
                        jnp.sum(grad_normed, axis=0),
                        jnp.sum(grad_embedded * token_hit, axis=0),
                        widen(query_sums),
                        widen(value_sums),
                    ]
                ),
                second_sums,
                first_sums,
                up_sums,
            ]
        )
    )
    (
        sum_gain,
        sum_shift,
        sum_mask,
        sum_query_bias,
        sum_value_bias,
        sum_second_gain,
        sum_second_shift,
        sum_down_bias,
        sum_first_gain,
        sum_first_shift,
        sum_output_bias,
    ) = sums[:11]
    sum_up_bias = sums[11:].reshape(-1)

    region_gradient = (
        batch_gain
        * inverse
        * (grad_normed - sum_shift / population - standard * (sum_gain / population))
    ).astype(BF16)
    shape = (documents, span, features)
    return (
        layer_output.reshape(shape),
        text_gradient.reshape(shape),
        region_gradient.reshape(shape),
        sum_mask,
        sum_gain,
        sum_shift,
        total_query,
        sum_query_bias,
        total_key,
        total_value,
        sum_value_bias,
        total_out,
        sum_output_bias,
        sum_first_gain,
        sum_first_shift,
        total_up,
        sum_up_bias,
        total_down,
        sum_down_bias,
        sum_second_gain,
        sum_second_shift,
    )


def solution(mesh):
    rows, weight, copied = P("dp", "seq", None), P("seq", None), P()
    mask = P("dp", "seq")
    in_specs = (
        (rows, rows, mask, mask, copied, copied, copied)
        + (weight, copied, weight, weight, copied, weight, copied, copied, copied)
        + (weight, copied, weight, copied, copied, copied, rows)
    )
    out_specs = (
        (rows, rows, rows, copied, copied, copied)
        + (weight, copied, weight, weight, copied, weight, copied, copied, copied)
        + (weight, copied, weight, copied, copied, copied)
    )
    return jax.shard_map(body, mesh=mesh, in_specs=in_specs, out_specs=out_specs, check_vma=False)
```

```python
import functools
import math

import jax
import jax.numpy as jnp
from jax import lax
from jax.experimental import pallas as pl
from jax.experimental.pallas import tpu as pltpu
from jax.sharding import PartitionSpec as P

HEAD_DIM = 64
EPS_NORM = 1e-12
EPS_BATCH = 1e-05
F32 = jnp.float32
BF16 = jnp.bfloat16
GELU_IN = math.sqrt(2.0 / math.pi)
GELU_CUBE = 0.044715
PIECES = 8
NEAR = 4
DOWN_ORDER = (2, 1, 4)
UP_ORDER = (1, 2, 4)
HEAD_ORDER = (1, 2, 4)


def swap(x, axis, by):
    return lax.ppermute(x, axis, [(i, i ^ by) for i in range(lax.axis_size(axis))])


def bits(axis):
    found, by = [], 1
    while by < lax.axis_size(axis):
        found.append(by)
        by *= 2
    return found


def nn(a, b):
    return jnp.dot(a, b, preferred_element_type=F32)


def tn(a, b):
    return lax.dot_general(a, b, (((0,), (0,)), ((), ())), preferred_element_type=F32)


def nt(a, b):
    return lax.dot_general(a, b, (((1,), (1,)), ((), ())), preferred_element_type=F32)


def norm_parts(x):
    centred = x - jnp.mean(x, axis=-1, keepdims=True)
    scale = lax.rsqrt(jnp.mean(centred * centred, axis=-1, keepdims=True) + EPS_NORM)
    return centred * scale, scale


def norm_back(grad, unit, scale, gain):
    g = grad * gain
    return scale * (
        g
        - jnp.mean(g, axis=-1, keepdims=True)
        - unit * jnp.mean(g * unit, axis=-1, keepdims=True)
    )


def gather_rows(x):
    two = swap(x, "seq", 2)
    one, three = swap(x, "seq", 1), swap(two, "seq", 1)
    return [x, one, two, three]


def gather_weight(halves, mine, by):
    near = swap(mine, "seq", 2)
    far = swap(near, "dp", by)
    return [halves, near, far, swap(halves, "seq", 1), swap(near, "seq", 1), swap(far, "seq", 1)]


def scatter_pairs(keep, give):
    got = swap(give, "seq", 1)
    pass_on = (keep[1].astype(F32) + got[1].astype(F32)).astype(BF16)
    own = keep[0].astype(F32) + got[0].astype(F32)
    return own + swap(pass_on, "seq", 2).astype(F32)


def exchange_blocks(blocks):
    return [blocks[0]] + [swap(blocks[r], "seq", r) for r in (1, 2, 3)]


def params(mebibytes):
    return pltpu.CompilerParams(vmem_limit_bytes=mebibytes * 1024 * 1024)


def whole_spec():
    return pl.BlockSpec(memory_space=pltpu.VMEM)


def pack_heads_kernel(place_ref, q_ref, k_ref, v_ref, *head_refs):
    seq = place_ref[0]
    part = q_ref.shape[0]
    for c in range(4):
        for r in range(4):

            @pl.when(seq == c ^ r)
            def _(c=c, r=r):
                for i, ref in enumerate((q_ref, k_ref, v_ref)):
                    head_refs[r][:, i * part : (i + 1) * part] = ref[:, c * part : (c + 1) * part]


def pack_halves_kernel(place_ref, out_ref, up_ref, halves_ref, near_ref):
    bit = place_ref[1] % 2
    half = out_ref.shape[0] // 2
    wide = out_ref.shape[1]

    def cut(rows):
        blocks = [out_ref[rows, :]] + [up_ref[rows, j * wide : (j + 1) * wide] for j in range(4)]
        return jnp.concatenate(blocks, axis=0)

    for h in range(2):
        halves_ref[h] = cut(pl.ds(h * half, half))
    near_ref[...] = cut(pl.ds(pl.multiple_of(bit * half, half), half))


def pack(place_word, query, key, value, out, up):
    part, features = out.shape
    tall = part // 2 * 5
    heads = pl.pallas_call(
        pack_heads_kernel,
        in_specs=[pl.BlockSpec(memory_space=pltpu.SMEM)] + [whole_spec()] * 3,
        out_specs=[whole_spec()] * 4,
        out_shape=[shaped(part, 3 * part)] * 4,
        compiler_params=params(56),
        cost_estimate=pl.CostEstimate(flops=0, bytes_accessed=2 * 1024 * 1024, transcendentals=0),
        name="pack_heads",
    )(place_word, query, key, value)
    halves, near = pl.pallas_call(
        pack_halves_kernel,
        in_specs=[pl.BlockSpec(memory_space=pltpu.SMEM)] + [whole_spec()] * 2,
        out_specs=[whole_spec()] * 2,
        out_shape=[shaped(2, tall, features), shaped(tall, features)],
        compiler_params=params(56),
        cost_estimate=pl.CostEstimate(flops=0, bytes_accessed=4 * 1024 * 1024, transcendentals=0),
        name="pack_halves",
    )(place_word, out, up)
    return heads, halves, near


def attend_kernel(seq_ref, *refs, waits):
    x_refs, w_refs, bias_ref, refs = refs[:4], refs[4:8], refs[8], refs[9 + waits :]
    q_ref, k_ref, v_ref, wc_ref, out_refs = refs[0], refs[1], refs[2], refs[3], refs[4:]
    part = w_refs[0].shape[0]
    span = x_refs[0].shape[1]

    @pl.when(pl.program_id(0) == 0)
    def _():
        for r in range(4):
            at = pl.multiple_of((seq_ref[0] ^ r) * part, part)
            for i in range(3):
                wc_ref[i, pl.ds(at, part), :] = w_refs[r][:, i * part : (i + 1) * part]

    x = jnp.concatenate([ref[0] for ref in x_refs], axis=0)
    for i, ref in enumerate((q_ref, k_ref, v_ref)):
        ref[0] = (nn(x, wc_ref[i]) + bias_ref[i]).astype(BF16)
    q, k, v = q_ref[0], k_ref[0], v_ref[0]
    lane = lax.broadcasted_iota(jnp.int32, (1, part), 1) // HEAD_DIM
    for h in range(part // HEAD_DIM):
        pick = jnp.where(lane == h, 1.0 / math.sqrt(HEAD_DIM), 0.0).astype(BF16)
        scores = nt(k, q * pick)
        raised = jnp.exp(scores - jnp.max(scores, axis=0, keepdims=True))
        chances = (raised * (1.0 / jnp.sum(raised, axis=0, keepdims=True))).astype(BF16)
        attended = tn(v, chances)[h * HEAD_DIM : (h + 1) * HEAD_DIM].astype(BF16)
        for r in range(4):
            out_refs[r][h * HEAD_DIM : (h + 1) * HEAD_DIM, :] = attended[:, r * span : (r + 1) * span]


def attend(seq, x_blocks, w_blocks, bias, after):
    documents, span, features = x_blocks[0].shape
    part = w_blocks[0].shape[0]
    length = 4 * span
    flops = documents * (2 * length * features * 3 * part + 4 * length * length * part)
    per_doc = pl.BlockSpec((1, length, part), lambda d: (d, 0, 0))
    return pl.pallas_call(
        functools.partial(attend_kernel, waits=len(after)),
        grid=(documents,),
        in_specs=[pl.BlockSpec(memory_space=pltpu.SMEM)]
        + [pl.BlockSpec((1, span, features), lambda d: (d, 0, 0))] * 4
        + [pl.BlockSpec((part, 3 * part), lambda d: (0, 0))] * 4
        + [pl.BlockSpec((3, 1, part), lambda d: (0, 0, 0))]
        + [any_spec()] * len(after),
        out_specs=[per_doc] * 3
        + [pl.BlockSpec((3, features, part), lambda d: (0, 0, 0))]
        + [pl.BlockSpec((part, span), lambda d: (0, d))] * 4,
        out_shape=[jax.ShapeDtypeStruct((documents, length, part), BF16)] * 3
        + [jax.ShapeDtypeStruct((3, features, part), BF16)]
        + [jax.ShapeDtypeStruct((part, documents * span), BF16)] * 4,
        compiler_params=params(56),
        cost_estimate=pl.CostEstimate(
            flops=flops, bytes_accessed=8 * 1024 * 1024, transcendentals=documents * length * length * 3
        ),
        name="attend",
    )(seq, *x_blocks, *w_blocks, bias, *after)


def attend_back_kernel(place_ref, *refs, waits):
    g_refs, x_refs = refs[:4], refs[4:8]
    q_ref, k_ref, v_ref, wc_ref = refs[8:12]
    keep_ref, give_ref, dw_keep_ref, dw_give_ref, sums_ref, acc_ref = refs[12 + waits :]
    part = q_ref.shape[2]
    span = x_refs[0].shape[1]
    first = pl.program_id(0) == 0
    q, k, v = q_ref[0], k_ref[0], v_ref[0]
    g = jnp.concatenate([ref[...] for ref in g_refs], axis=1)
    lane = lax.broadcasted_iota(jnp.int32, (1, part), 1) // HEAD_DIM
    scale = 1.0 / math.sqrt(HEAD_DIM)
    dq = dk = dv = None
    for h in range(part // HEAD_DIM):
        on = lane == h
        pick = jnp.where(on, scale, 0.0).astype(BF16)
        mask = jnp.where(on, 1.0, 0.0)
        scores = nt(k, q * pick)
        raised = jnp.exp(scores - jnp.max(scores, axis=0, keepdims=True))
        chances = raised * (1.0 / jnp.sum(raised, axis=0, keepdims=True))
        grad = nn(v * mask.astype(BF16), g)
        both = chances * grad
        grad = (both - chances * jnp.sum(both, axis=0, keepdims=True)).astype(BF16)
        part_v = nt(chances.astype(BF16), g) * mask
        part_k = nn(grad, q) * (mask * scale)
        part_q = tn(grad, k) * (mask * scale)
        dq = part_q if dq is None else dq + part_q
        dk = part_k if dk is None else dk + part_k
        dv = part_v if dv is None else dv + part_v
    low = [t.astype(BF16) for t in (dq, dk, dv)]
    sums = jnp.concatenate(
        [jnp.sum(low[i].astype(F32), axis=0, keepdims=True) for i in (0, 2)], axis=0
    )
    x = jnp.concatenate([ref[0] for ref in x_refs], axis=0)
    x_t = x.T
    inner = nt(low[0], wc_ref[0]) + nt(low[1], wc_ref[1]) + nt(low[2], wc_ref[2])
    inner = inner.astype(BF16)
    for r in range(4):
        (give_ref if r % 2 else keep_ref)[r // 2, 0] = inner[r * span : (r + 1) * span]

    @pl.when(first)
    def _():
        sums_ref[...] = sums
        for i in range(3):
            acc_ref[i] = nn(x_t, low[i])

    @pl.when(jnp.logical_not(first))
    def _():
        sums_ref[...] += sums
        for i in range(3):
            acc_ref[i] += nn(x_t, low[i])

    @pl.when(pl.program_id(0) == pl.num_programs(0) - 1)
    def _():
        tall = part // PIECES
        dp = place_ref[1] % NEAR
        first = HEAD_ORDER[0]
        for p in range(PIECES):
            spot = place(p ^ dp, HEAD_ORDER[1:])
            for mine, ref in ((True, dw_keep_ref), (False, dw_give_ref)):

                @pl.when(((p ^ dp) // first % 2 == 0) == mine)
                def _(p=p, spot=spot, ref=ref):
                    for block in range(4):
                        at = block * part + p * tall
                        for i in range(3):
                            ref[spot, place_ref[0] ^ block, :, i * part : (i + 1) * part] = acc_ref[
                                i, at : at + tall, :
                            ].astype(BF16)


def attend_back(place_word, g_blocks, x_blocks, q, k, v, wc, after):
    documents, span, features = x_blocks[0].shape
    part = q.shape[2]
    length = 4 * span
    flops = documents * (4 * length * features * 3 * part + 10 * length * length * part)
    per_doc = pl.BlockSpec((1, length, part), lambda d: (d, 0, 0))
    pair = pl.BlockSpec((2, 1, span, features), lambda d: (0, d, 0, 0))
    return pl.pallas_call(
        functools.partial(attend_back_kernel, waits=len(after)),
        grid=(documents,),
        in_specs=[pl.BlockSpec(memory_space=pltpu.SMEM)]
        + [pl.BlockSpec((part, span), lambda d: (0, d))] * 4
        + [pl.BlockSpec((1, span, features), lambda d: (d, 0, 0))] * 4
        + [per_doc] * 3
        + [pl.BlockSpec((3, features, part), lambda d: (0, 0, 0))]
        + [any_spec()] * len(after),
        out_specs=[
            pair,
            pair,
            pl.BlockSpec((PIECES // 2, 4, part // PIECES, 3 * part), lambda d: (0, 0, 0, 0)),
            pl.BlockSpec((PIECES // 2, 4, part // PIECES, 3 * part), lambda d: (0, 0, 0, 0)),
            pl.BlockSpec((2, part), lambda d: (0, 0)),
        ],
        out_shape=[jax.ShapeDtypeStruct((2, documents, span, features), BF16)] * 2
        + [
            jax.ShapeDtypeStruct((PIECES // 2, 4, part // PIECES, 3 * part), BF16),
            jax.ShapeDtypeStruct((PIECES // 2, 4, part // PIECES, 3 * part), BF16),
            jax.ShapeDtypeStruct((2, part), F32),
        ],
        scratch_shapes=[pltpu.VMEM((3, features, part), F32)],
        compiler_params=params(56),
        cost_estimate=pl.CostEstimate(
            flops=flops, bytes_accessed=12 * 1024 * 1024, transcendentals=documents * length * length * 3
        ),
        name="attend_back",
    )(place_word, *g_blocks, *x_blocks, q, k, v, wc, *after)


def gelu_parts(x):
    square = x * x
    bend = jnp.tanh(GELU_IN * x * (1.0 + GELU_CUBE * square))
    gate = 0.5 * (1.0 + bend)
    rise = 0.5 * x * (1.0 - bend * bend) * (GELU_IN + 3.0 * GELU_IN * GELU_CUBE * square)
    return x * gate, gate + rise


def place(index, order):
    at = 0
    for by in order:
        at = 2 * at + (index // by) % 2
    return at


def weight_copies(place_ref, pieces, wo, up, down, sems):
    seq, dp = place_ref[0], place_ref[1]
    part = wo.shape[1]
    half = part // 2
    wo_copies, up_copies, down_copies = [], [[] for _ in range(4)], [[] for _ in range(4)]

    def bring(found, source, target):
        found.append(pltpu.make_async_copy(source, target, sems.at[sum(used)]))
        used.append(1)

    used = []
    own, near, far, one, near_one, far_one = pieces[:6]
    bit = dp % 2
    parts = [(own.at[h], 0, h) for h in range(2)] + [(one.at[h], 1, h) for h in range(2)]
    parts += [(near, 2, bit), (far, 2, 1 - bit), (near_one, 3, bit), (far_one, 3, 1 - bit)]
    for source, r, h in parts:
        at = pl.multiple_of(h * half, half)
        bring(wo_copies, source.at[pl.ds(0, half)], wo.at[r, pl.ds(at, half)])
        if up is None:
            continue
        at = pl.multiple_of((seq ^ r) * part + h * half, half)
        for i in range(4):
            start = pl.multiple_of(half * (1 + (seq ^ i)), half)
            bring(up_copies[i], source.at[pl.ds(start, half)], up.at[i, pl.ds(at, half)])
    for r in range(4 if down is not None else 0):
        bring(down_copies[r], pieces[6 + r], down.at[r])
    return wo_copies, up_copies, down_copies


def start_all(copies):
    for copy in copies:
        copy.start()


def wait_all(copies):
    for copy in copies:
        copy.wait()


def forward_kernel(place_ref, *refs):
    (a_refs, in_ref, cot_ref, vec_ref, upb_ref), refs = (refs[:4], *refs[4:8]), refs[8:]
    pieces, refs = refs[:10], refs[10:]
    out_ref, unit_ref, scale_ref, grad_ref, sums_ref, upsum_ref = refs[:6]
    outs = (refs[6:9], refs[9:12])
    wo, up, down, act, slope, low_t, spare, terms, sems, out_sems = refs[12:]
    seq, dp = place_ref[0], place_ref[1]
    part = wo.shape[1]
    half = part // 2
    size = terms.shape[3]

    wo_copies, up_copies, down_copies = weight_copies(place_ref, pieces, wo, up, down, sems)
    start_all(wo_copies + up_copies[0] + up_copies[1])
    out_bias, gain1, shift1, down_bias, gain2, shift2 = (vec_ref[i : i + 1, :] for i in range(6))
    residual = in_ref[...] + out_bias
    wait_all(wo_copies)
    joined = jnp.concatenate([ref[...] for ref in a_refs], axis=0)
    residual += tn(joined, wo[...].reshape(joined.shape[0], -1))
    unit1, scale1 = norm_parts(residual)
    unit_ref[...] = unit1
    scale_ref[...] = scale1
    first_out = unit1 * gain1 + shift1
    low = first_out.astype(BF16)
    for r in range(4):
        wait_all(up_copies[r])
        start_all(up_copies[r + 2] if r < 2 else down_copies[2 * r - 4] + down_copies[2 * r - 3])
        x = nn(low, up[r]) + upb_ref[pl.ds(seq ^ r, 1), :]
        value, rise = gelu_parts(x)
        act[r] = value.astype(BF16)
        slope[r] = rise
    second_in = first_out + down_bias
    for r in range(4):
        wait_all(down_copies[r])
        second_in += nn(act[r], down[r])
    unit2, scale2 = norm_parts(second_in)
    out_ref[...] = (unit2 * gain2 + shift2).astype(BF16)
    incoming = cot_ref[...].astype(F32)
    grad_first = norm_back(incoming, unit2, scale2, gain2)
    grad_down = grad_first.astype(BF16)
    sums_ref[0:1, :] = jnp.sum(incoming * unit2, axis=0, keepdims=True)
    sums_ref[1:2, :] = jnp.sum(incoming, axis=0, keepdims=True)
    sums_ref[2:3, :] = jnp.sum(grad_down.astype(F32), axis=0, keepdims=True)
    spare[...] = low.T
    for i in range(4):
        low_t[i * part : (i + 1) * part, :] = spare[pl.ds(pl.multiple_of((seq ^ i) * part, part), part), :]
    for r in range(4):
        grad_act = nt(grad_down, down[r]).astype(BF16).astype(F32)
        grad_up = (grad_act * slope[r]).astype(BF16)
        upsum_ref[pl.ds(seq ^ r, 1), :] = jnp.sum(grad_up.astype(F32), axis=0, keepdims=True)
        grad_first += nt(grad_up, up[r])
        value = nn(low_t[...], grad_up).astype(BF16)
        for i in range(4):
            for h in range(2):
                spot = place((2 * (seq ^ r) + h) ^ (dp % NEAR), UP_ORDER)
                at = i * part + h * half
                terms[1, i, spot] = value[at : at + half]
    grad_ref[...] = grad_first

    def send(which, r):
        keep_out, far_out, give_out = outs[which]
        target = (keep_out, give_out.at[0], far_out, give_out.at[1])[r]
        return pltpu.make_async_copy(terms.at[which, r], target, out_sems.at[which, r])

    start_all([send(1, r) for r in range(4)])
    for r in range(4):
        value = tn(act[r], grad_down)
        for p in range(PIECES):
            spot = place(p ^ (dp % NEAR), DOWN_ORDER)
            terms[0, r, spot] = value[p * size : (p + 1) * size].astype(BF16)
        send(0, r).start()
    wait_all([send(which, r) for which in range(2) for r in range(4)])


def backward_kernel(place_ref, *refs):
    (a_refs, unit_ref, scale_ref, grad_ref, vec_ref), refs = (refs[:4], *refs[4:8]), refs[8:]
    pieces, refs = refs[:6], refs[6:]
    res_ref, g_refs, sums_ref, keep_ref, far_ref, give_ref, wo, sems = refs[0], refs[1:5], *refs[5:]
    dp = place_ref[1]
    part = wo.shape[1]
    tall = part // PIECES
    copies = weight_copies(place_ref, pieces, wo, None, None, sems)[0]
    start_all(copies)
    unit1 = unit_ref[...]
    grad_first = grad_ref[...]
    grad_residual = norm_back(grad_first, unit1, scale_ref[...], vec_ref[1:2, :])
    res_ref[...] = grad_residual
    grad_out = grad_residual.astype(BF16)
    joined = jnp.concatenate([ref[...] for ref in a_refs], axis=0)
    value = nn(joined, grad_out)
    for r in range(4):
        for p in range(PIECES):
            spot = place(p ^ (dp % NEAR), UP_ORDER)
            piece = value[r * part + p * tall : r * part + (p + 1) * tall].astype(BF16)
            if r % 2:
                give_ref[r // 2, spot] = piece
            else:
                (far_ref if r else keep_ref)[spot] = piece
    sums_ref[0:1, :] = jnp.sum(grad_first * unit1, axis=0, keepdims=True)
    sums_ref[1:2, :] = jnp.sum(grad_first, axis=0, keepdims=True)
    sums_ref[2:3, :] = jnp.sum(grad_out.astype(F32), axis=0, keepdims=True)
    wait_all(copies)
    back = nt(wo[...].reshape(joined.shape[0], -1), grad_out).astype(BF16)
    for r in range(4):
        g_refs[r][...] = back[r * part : (r + 1) * part]


def shaped(*shape, dtype=BF16):
    return jax.ShapeDtypeStruct(shape, dtype)


def any_spec():
    return pl.BlockSpec(memory_space=pl.ANY)


def forward(place_word, attended, embedded, cotangent, vectors, up_bias, pieces):
    rows, features = embedded.shape
    part = attended[0].shape[0]
    size = features // PIECES
    term = [shaped(PIECES, size, features)] * 2 + [shaped(2, PIECES, size, features)]
    return pl.pallas_call(
        forward_kernel,
        in_specs=[pl.BlockSpec(memory_space=pltpu.SMEM)] + [whole_spec()] * 8 + [any_spec()] * 10,
        out_specs=[whole_spec()] * 6 + [any_spec()] * 6,
        out_shape=[
            shaped(rows, features),
            shaped(rows, features, dtype=F32),
            shaped(rows, 1, dtype=F32),
            shaped(rows, features, dtype=F32),
            shaped(3, features, dtype=F32),
            shaped(4, features, dtype=F32),
        ]
        + term
        + term,
        scratch_shapes=[
            pltpu.VMEM((4, part, features), BF16),
            pltpu.VMEM((4, features, features), BF16),
            pltpu.VMEM((4, features, features), BF16),
            pltpu.VMEM((4, rows, features), BF16),
            pltpu.VMEM((4, rows, features), F32),
            pltpu.VMEM((features, rows), BF16),
            pltpu.VMEM((features, rows), BF16),
            pltpu.VMEM((2, 4, PIECES, size, features), BF16),
            pltpu.SemaphoreType.DMA((44,)),
            pltpu.SemaphoreType.DMA((2, 4)),
        ],
        compiler_params=params(56),
        cost_estimate=pl.CostEstimate(
            flops=12 * rows * features * 4 * features,
            bytes_accessed=26 * 1024 * 1024,
            transcendentals=rows * 4 * features,
        ),
        name="forward",
    )(place_word, *attended, embedded, cotangent, vectors, up_bias, *pieces)


def backward(place_word, attended, unit, scale, grad, vectors, pieces):
    rows, features = unit.shape
    part = attended[0].shape[0]
    piece = (PIECES, part // PIECES, features)
    return pl.pallas_call(
        backward_kernel,
        in_specs=[pl.BlockSpec(memory_space=pltpu.SMEM)] + [whole_spec()] * 8 + [any_spec()] * 6,
        out_specs=[whole_spec()] * 9,
        out_shape=[shaped(rows, features, dtype=F32)]
        + [shaped(part, rows)] * 4
        + [shaped(3, features, dtype=F32), shaped(*piece), shaped(*piece), shaped(2, *piece)],
        scratch_shapes=[pltpu.VMEM((4, part, features), BF16), pltpu.SemaphoreType.DMA((44,))],
        compiler_params=params(56),
        cost_estimate=pl.CostEstimate(
            flops=4 * rows * features * features, bytes_accessed=6 * 1024 * 1024, transcendentals=rows
        ),
        name="backward",
    )(place_word, *attended, unit, scale, grad, vectors, *pieces)


def fold_kernel(*refs, body, inputs, waits):
    body(refs[:inputs], refs[inputs + waits :])


def fold(body, arrays, shapes, after, name):
    return pl.pallas_call(
        functools.partial(fold_kernel, body=body, inputs=len(arrays), waits=len(after)),
        in_specs=[whole_spec()] * len(arrays) + [any_spec()] * len(after),
        out_specs=[whole_spec()] * len(shapes),
        out_shape=[shaped(*shape) for shape in shapes],
        compiler_params=params(40),
        cost_estimate=pl.CostEstimate(flops=0, bytes_accessed=4 * 1024 * 1024, transcendentals=0),
        name=name,
    )(*arrays, *after)


def added(*values):
    return sum(v.astype(F32) for v in values[1:]) + values[0].astype(F32)


def fold_down_core(ins, outs):
    keeps, got = ins[:2], ins[2]
    half = got.shape[1] // 2
    for i, mine in enumerate(keeps):
        outs[0][:, i] = added(mine[:half], got[i, :half]).astype(BF16)
        outs[1][:, i] = added(mine[half:], got[i, half:]).astype(BF16)


def fold_up_core(ins, outs):
    size = ins[0].shape[1]
    for keep, far, got, rows in ((*ins[:3], slice(0, size)), (*ins[3:], slice(size, None))):
        outs[0][:, rows] = added(keep[...], got[0]).astype(BF16)
        outs[1][:, rows] = added(far[...], got[1]).astype(BF16)


def fold_both(ins, outs):
    down, down_got, up, up_got = ins
    half = up.shape[0] // 2
    outs[0][...] = added(down[:, 0], down_got[:, 0]).astype(BF16)
    outs[1][...] = added(down[:, 1], down_got[:, 1]).astype(BF16)
    outs[2][...] = added(up[:half], up_got[:half]).astype(BF16)
    outs[3][...] = added(up[half:], up_got[half:]).astype(BF16)


def fold_half(ins, outs):
    mine, got = ins
    half = mine.shape[0] // 2
    outs[0][...] = added(mine[:half], got[:half]).astype(BF16)
    outs[1][...] = added(mine[half:], got[half:]).astype(BF16)


def fold_inner(ins, outs):
    mine, got = ins
    for i in range(2):
        outs[i][...] = added(mine[i], got[i]).astype(BF16)


def settle_kernel(place_ref, *refs, order, store):
    held, outs = refs[:2], refs[2:]
    seq, dp = place_ref[0], place_ref[1] % NEAR
    half = PIECES // 2
    for index in range(PIECES):
        spot = place(index, order)
        store(outs, held[spot // half].at[spot % half], index ^ dp, seq)


def store_down(outs, piece, p, seq):
    size = piece.shape[0]
    outs[0][pl.ds(pl.multiple_of(p * size, size), size), :] = piece[...].astype(F32)


def store_up(outs, piece, p, seq):
    size, wide = outs[0].shape[0] // 2, piece.shape[1]
    tall = piece.shape[0] - size
    row, column = pl.multiple_of((p % 2) * size, size), pl.multiple_of((p // 2) * wide, wide)
    outs[0][pl.ds(row, size), pl.ds(column, wide)] = piece[:size].astype(F32)
    outs[1][pl.ds(pl.multiple_of(p * tall, 8), tall), :] = piece[size:].astype(F32)


def store_heads(outs, piece, p, seq):
    tall, part = piece.shape[1], piece.shape[2] // 3
    rows = pl.ds(pl.multiple_of(p * tall, 8), tall)
    for c in range(4):
        columns = slice(c * part, (c + 1) * part)
        block = piece[seq ^ c].astype(F32)
        for i in range(3):
            outs[i][rows, columns] = block[:, i * part : (i + 1) * part]


def settle(place_word, held, order, store, shapes):
    return pl.pallas_call(
        functools.partial(settle_kernel, order=order, store=store),
        in_specs=[pl.BlockSpec(memory_space=pltpu.SMEM)] + [whole_spec()] * 2,
        out_specs=[whole_spec()] * len(shapes),
        out_shape=[jax.ShapeDtypeStruct(shape, F32) for shape in shapes],
        compiler_params=params(56),
        cost_estimate=pl.CostEstimate(flops=0, bytes_accessed=4 * 1024 * 1024, transcendentals=0),
        name="settle",
    )(place_word, *held)


def gate_kernel(*refs):
    pass


def gate(x, *after):
    return pl.pallas_call(
        gate_kernel,
        in_specs=[any_spec()] * (1 + len(after)),
        out_specs=any_spec(),
        out_shape=shaped(*x.shape, dtype=x.dtype),
        input_output_aliases={0: 0},
        cost_estimate=pl.CostEstimate(flops=0, bytes_accessed=0, transcendentals=0),
        name="gate",
    )(x, *after)


def reduce_dp(x, orders):
    for by in orders:
        half = x.shape[0] // 2
        x = x[:half].astype(F32) + swap(x[half:].astype(BF16), "dp", by).astype(F32)
    return x


def reduce_rest(x, last, *after):
    for by in (last, *bits("dp")[3:]):
        x = x.astype(BF16)
        got = swap(x, "dp", by)
        if after and by == last:
            got = gate(got, *after)
        x = x.astype(F32) + got.astype(F32)
    return x.astype(BF16)


def spread_dp(x, first, last, *after):
    got = swap(x, "dp", first)
    x = jnp.concatenate([x, gate(got, *after) if after else got])
    return x, swap(x, "dp", last)


def body(
    text_embed,
    region_feature,
    token_mask,
    segment_mask,
    mask_vector,
    batch_gain,
    batch_shift,
    query_weight,
    query_bias,
    key_weight,
    value_weight,
    value_bias,
    output_weight,
    output_bias,
    first_gain,
    first_shift,
    up_weight,
    up_bias,
    down_weight,
    down_bias,
    second_gain,
    second_shift,
    cotangent,
):
    documents, span, features = text_embed.shape
    rows = documents * span
    seq, dp = lax.axis_index("seq"), lax.axis_index("dp")
    group = lax.axis_size("seq")
    population = rows * lax.axis_size("dp") * group
    score_scale = 1.0 / math.sqrt(HEAD_DIM)
    part = features // group
    heads = part // HEAD_DIM

    place_word = jnp.stack([seq, dp]).astype(jnp.int32)
    cut, halves, mine = pack(
        place_word, query_weight, key_weight, value_weight, output_weight, up_weight
    )

    region = region_feature.astype(F32).reshape(rows, features)
    sums = jnp.stack([jnp.sum(region, axis=0), jnp.sum(region * region, axis=0)])
    chip_sums = sums + swap(sums, "seq", 2)
    chip_sums = gate(chip_sums, cut[0])
    sums = chip_sums + swap(chip_sums, "seq", 1)
    head_blocks = exchange_blocks(cut)
    for by in bits("dp"):
        if by == 4:
            sums = gate(sums, head_blocks[2], head_blocks[3])
        sums = sums + swap(sums, "dp", by)
    average = sums[0] / population
    inverse = lax.rsqrt(sums[1] / population - average * average + EPS_BATCH)

    bias3 = jnp.stack([query_bias, jnp.zeros_like(query_bias), value_bias]).reshape(3, group, part)
    head_bias = lax.dynamic_slice_in_dim(bias3, seq, 1, 1)
    pieces = gather_weight(halves, mine, 1)

    standard = (region - average) * inverse
    token_hit = token_mask.astype(F32).reshape(rows, 1)
    segment_keep = 1.0 - segment_mask.astype(F32).reshape(rows, 1)
    embedded = (
        text_embed.astype(F32).reshape(rows, features) * (1.0 - token_hit)
        + token_hit * mask_vector
        + segment_keep * (standard * batch_gain + batch_shift)
    )
    low_in = embedded.astype(BF16).reshape(documents, span, features)
    x_blocks = gather_rows(low_in)
    far = swap(gate(down_weight, low_in, pieces[1]), "seq", 2)
    q, k, v, head_weight, *attended = attend(place_word, x_blocks, head_blocks, head_bias, [])
    attn_blocks = exchange_blocks(attended)
    far = gate(far, attn_blocks[3])
    pieces += [down_weight, swap(down_weight, "seq", 1), far, swap(far, "seq", 1)]
    vectors = jnp.stack([output_bias, first_gain, first_shift, down_bias, second_gain, second_shift])
    layer_output, unit, scale, grad_first, second_sums, up_sums, *terms = forward(
        place_word,
        attn_blocks,
        embedded,
        cotangent.reshape(rows, features),
        vectors,
        up_bias.reshape(group, features),
        pieces,
    )
    grad_residual, *rest = backward(place_word, attn_blocks, unit, scale, grad_first, vectors, pieces[:6])
    grad_attn, first_sums, (out_keep, out_far, out_give) = rest[:4], rest[4], rest[5:]
    down_keep, down_far, down_give = terms[:3]
    up_keep, up_far, up_give = terms[3:]

    half = PIECES // 2
    size, tall = features // PIECES, part // PIECES
    g_blocks = exchange_blocks(grad_attn)
    down, down_send = fold(
        fold_down_core,
        [down_keep, down_far, swap(down_give, "seq", 1)],
        [(half, 2, size, features)] * 2,
        [g_blocks[2], g_blocks[3]],
        "down_core",
    )
    up, up_send = fold(
        fold_up_core,
        [up_keep, up_far, swap(up_give, "seq", 1), out_keep, out_far, swap(out_give, "seq", 1)],
        [(PIECES, size + tall, features)] * 2,
        [down_send],
        "up_core",
    )

    keep, give, heads, heads_send, head_sums = attend_back(
        place_word, g_blocks, x_blocks, q, k, v, head_weight, [up_send]
    )
    query_sums, value_sums = head_sums[0], head_sums[1]

    heads_got = swap(heads_send, "dp", HEAD_ORDER[0])
    down, down_send, up, up_send = fold(
        fold_both,
        [down, swap(down_send, "dp", DOWN_ORDER[0]), up, swap(up_send, "seq", 2)],
        [(half, size, features)] * 2 + [(half, size + tall, features)] * 2,
        [heads_got],
        "both",
    )
    inner_own, inner_send = fold(
        fold_inner, [keep, swap(give, "seq", 1)], [keep.shape[1:]] * 2, [up_send], "inner"
    )
    heads, heads_send = fold(
        fold_half,
        [heads, heads_got],
        [(half // 2, group, tall, 3 * part)] * 2,
        [inner_send],
        "heads",
    )
    up = up.astype(F32) + gate(swap(up_send, "dp", UP_ORDER[0]), heads_send).astype(F32)
    down = down.astype(F32) + gate(swap(down_send, "seq", 2), up).astype(F32)
    heads = heads.astype(F32) + gate(swap(heads_send, "dp", HEAD_ORDER[1]), up).astype(F32)
    inner_got = swap(inner_send, "seq", 2)
    quarter = half // 2
    got = gate(swap(up[quarter:].astype(BF16), "dp", UP_ORDER[1]), inner_got, down)
    up = up[:quarter] + got.astype(F32)
    down = reduce_dp(down, DOWN_ORDER[1:-1])

    inner = inner_own.astype(F32) + inner_got.astype(F32)
    grad_embedded = grad_residual + inner.reshape(rows, features)
    text_gradient = (grad_embedded * (1.0 - token_hit)).astype(BF16)
    grad_normed = grad_embedded * segment_keep

    def widen(x):
        return lax.dynamic_update_slice_in_dim(jnp.zeros((features,), F32), x, seq * part, 0)

    sums = jnp.concatenate(
        [
            jnp.stack(
                [
                    jnp.sum(grad_normed * standard, axis=0),
                    jnp.sum(grad_normed, axis=0),
                    jnp.sum(grad_embedded * token_hit, axis=0),
                    widen(query_sums),
                    widen(value_sums),
                ]
            ),
            second_sums,
            first_sums,
            up_sums,
        ]
    )
    for by in bits("seq"):
        sums = sums + swap(sums, "seq", by)

    own = reduce_rest(heads, HEAD_ORDER[-1], up, down)
    own = jnp.stack(exchange_blocks([own[:, r] for r in range(group)]), axis=1)
    held_heads = spread_dp(own, 1, 2)
    total_query, total_key, total_value = settle(
        place_word, held_heads, (2, 1, 4), store_heads, [query_weight.shape] * 3
    )

    up = reduce_rest(up, UP_ORDER[-1], sums)
    sums = sums + swap(sums, "dp", 1)
    down = reduce_rest(down, DOWN_ORDER[-1], up, sums)
    total_up, total_out = settle(
        place_word, spread_dp(up, 2, 1, down), (1, 2, 4), store_up, [up_weight.shape, output_weight.shape]
    )
    (total_down,) = settle(
        place_word, spread_dp(down, 1, 2, held_heads[1]), (2, 1, 4), store_down, [down_weight.shape]
    )

    for by, ready in zip(bits("dp")[1:], (total_query, total_up)):
        sums = sums + gate(swap(sums, "dp", by), ready)
    for by in bits("dp")[3:]:
        sums = sums + swap(sums, "dp", by)
    (
        sum_gain,
        sum_shift,
        sum_mask,
        sum_query_bias,
        sum_value_bias,
        sum_second_gain,
        sum_second_shift,
        sum_down_bias,
        sum_first_gain,
        sum_first_shift,
        sum_output_bias,
    ) = sums[:11]
    sum_up_bias = sums[11:].reshape(-1)

    region_gradient = (
        batch_gain
        * inverse
        * (grad_normed - sum_shift / population - standard * (sum_gain / population))
    ).astype(BF16)
    shape = (documents, span, features)
    return (
        layer_output.reshape(shape),
        text_gradient.reshape(shape),
        region_gradient.reshape(shape),
        sum_mask,
        sum_gain,
        sum_shift,
        total_query,
        sum_query_bias,
        total_key,
        total_value,
        sum_value_bias,
        total_out,
        sum_output_bias,
        sum_first_gain,
        sum_first_shift,
        total_up,
        sum_up_bias,
        total_down,
        sum_down_bias,
        sum_second_gain,
        sum_second_shift,
    )


def solution(mesh):
    rows, weight, copied = P("dp", "seq", None), P("seq", None), P()
    mask = P("dp", "seq")
    in_specs = (
        (rows, rows, mask, mask, copied, copied, copied)
        + (weight, copied, weight, weight, copied, weight, copied, copied, copied)
        + (weight, copied, weight, copied, copied, copied, rows)
    )
    out_specs = (
        (rows, rows, rows, copied, copied, copied)
        + (weight, copied, weight, weight, copied, weight, copied, copied, copied)
        + (weight, copied, weight, copied, copied, copied)
    )
    return jax.shard_map(body, mesh=mesh, in_specs=in_specs, out_specs=out_specs, check_vma=False)
```

```python
import functools
import math

import jax
import jax.numpy as jnp
from jax import lax
from jax.experimental import pallas as pl
from jax.experimental.pallas import tpu as pltpu
from jax.sharding import PartitionSpec as P

HEAD_DIM = 64
EPS_NORM = 1e-12
EPS_BATCH = 1e-05
F32 = jnp.float32
BF16 = jnp.bfloat16
GELU_IN = math.sqrt(2.0 / math.pi)
GELU_CUBE = 0.044715
PIECES = 8
NEAR = 4
DOWN_ORDER = (2, 1, 4)
UP_ORDER = (1, 2, 4)
HEAD_ORDER = (1, 2, 4)


def swap(x, axis, by):
    return lax.ppermute(x, axis, [(i, i ^ by) for i in range(lax.axis_size(axis))])


def bits(axis):
    found, by = [], 1
    while by < lax.axis_size(axis):
        found.append(by)
        by *= 2
    return found


def nn(a, b):
    return jnp.dot(a, b, preferred_element_type=F32)


def tn(a, b):
    return lax.dot_general(a, b, (((0,), (0,)), ((), ())), preferred_element_type=F32)


def nt(a, b):
    return lax.dot_general(a, b, (((1,), (1,)), ((), ())), preferred_element_type=F32)


def norm_parts(x):
    centred = x - jnp.mean(x, axis=-1, keepdims=True)
    scale = lax.rsqrt(jnp.mean(centred * centred, axis=-1, keepdims=True) + EPS_NORM)
    return centred * scale, scale


def norm_back(grad, unit, scale, gain):
    g = grad * gain
    return scale * (
        g
        - jnp.mean(g, axis=-1, keepdims=True)
        - unit * jnp.mean(g * unit, axis=-1, keepdims=True)
    )


def gather_rows(x):
    two = swap(x, "seq", 2)
    one, three = swap(x, "seq", 1), swap(two, "seq", 1)
    return [x, one, two, three]


def gather_weight(halves, mine, by):
    near = swap(mine, "seq", 2)
    far = swap(near, "dp", by)
    return [halves, near, far, swap(halves, "seq", 1), swap(near, "seq", 1), swap(far, "seq", 1)]


def scatter_pairs(keep, give):
    got = swap(give, "seq", 1)
    pass_on = (keep[1].astype(F32) + got[1].astype(F32)).astype(BF16)
    own = keep[0].astype(F32) + got[0].astype(F32)
    return own + swap(pass_on, "seq", 2).astype(F32)


def exchange_blocks(blocks):
    return [blocks[0]] + [swap(blocks[r], "seq", r) for r in (1, 2, 3)]


def params(mebibytes):
    return pltpu.CompilerParams(vmem_limit_bytes=mebibytes * 1024 * 1024)


def whole_spec():
    return pl.BlockSpec(memory_space=pltpu.VMEM)


def pack_heads_kernel(place_ref, q_ref, k_ref, v_ref, *head_refs):
    seq = place_ref[0]
    part = q_ref.shape[0]
    for c in range(4):
        for r in range(4):

            @pl.when(seq == c ^ r)
            def _(c=c, r=r):
                for i, ref in enumerate((q_ref, k_ref, v_ref)):
                    head_refs[r][:, i * part : (i + 1) * part] = ref[:, c * part : (c + 1) * part]


def pack_halves_kernel(place_ref, out_ref, up_ref, halves_ref, near_ref):
    bit = place_ref[1] % 2
    half = out_ref.shape[0] // 2
    wide = out_ref.shape[1]

    def cut(rows):
        blocks = [out_ref[rows, :]] + [up_ref[rows, j * wide : (j + 1) * wide] for j in range(4)]
        return jnp.concatenate(blocks, axis=0)

    for h in range(2):
        halves_ref[h] = cut(pl.ds(h * half, half))
    near_ref[...] = cut(pl.ds(pl.multiple_of(bit * half, half), half))


def pack(place_word, query, key, value, out, up):
    part, features = out.shape
    tall = part // 2 * 5
    heads = pl.pallas_call(
        pack_heads_kernel,
        in_specs=[pl.BlockSpec(memory_space=pltpu.SMEM)] + [whole_spec()] * 3,
        out_specs=[whole_spec()] * 4,
        out_shape=[shaped(part, 3 * part)] * 4,
        compiler_params=params(56),
        cost_estimate=pl.CostEstimate(flops=0, bytes_accessed=2 * 1024 * 1024, transcendentals=0),
        name="pack_heads",
    )(place_word, query, key, value)
    halves, near = pl.pallas_call(
        pack_halves_kernel,
        in_specs=[pl.BlockSpec(memory_space=pltpu.SMEM)] + [whole_spec()] * 2,
        out_specs=[whole_spec()] * 2,
        out_shape=[shaped(2, tall, features), shaped(tall, features)],
        compiler_params=params(56),
        cost_estimate=pl.CostEstimate(flops=0, bytes_accessed=4 * 1024 * 1024, transcendentals=0),
        name="pack_halves",
    )(place_word, out, up)
    return heads, halves, near


def attend_kernel(seq_ref, *refs, waits):
    x_refs, w_refs, bias_ref, refs = refs[:4], refs[4:8], refs[8], refs[9 + waits :]
    q_ref, k_ref, v_ref, wc_ref, log_ref, out_refs = refs[0], refs[1], refs[2], refs[3], refs[4], refs[5:]
    part = w_refs[0].shape[0]
    span = x_refs[0].shape[1]

    @pl.when(pl.program_id(0) == 0)
    def _():
        for r in range(4):
            at = pl.multiple_of((seq_ref[0] ^ r) * part, part)
            for i in range(3):
                wc_ref[i, pl.ds(at, part), :] = w_refs[r][:, i * part : (i + 1) * part]

    x = jnp.concatenate([ref[0] for ref in x_refs], axis=0)
    for i, ref in enumerate((q_ref, k_ref, v_ref)):
        ref[0] = (nn(x, wc_ref[i]) + bias_ref[i]).astype(BF16)
    q, k, v = q_ref[0], k_ref[0], v_ref[0]
    lane = lax.broadcasted_iota(jnp.int32, (1, part), 1) // HEAD_DIM
    for h in range(part // HEAD_DIM):
        pick = jnp.where(lane == h, 1.0 / math.sqrt(HEAD_DIM), 0.0).astype(BF16)
        scores = nt(k, q * pick)
        top = jnp.max(scores, axis=0, keepdims=True)
        raised = jnp.exp(scores - top)
        total = jnp.sum(raised, axis=0, keepdims=True)
        log_ref[0, h : h + 1, :] = top + jnp.log(total)
        attended = tn(v, raised.astype(BF16))[h * HEAD_DIM : (h + 1) * HEAD_DIM]
        attended = (attended * (1.0 / total)).astype(BF16)
        for r in range(4):
            out_refs[r][h * HEAD_DIM : (h + 1) * HEAD_DIM, :] = attended[:, r * span : (r + 1) * span]


def attend(seq, x_blocks, w_blocks, bias, after):
    documents, span, features = x_blocks[0].shape
    part = w_blocks[0].shape[0]
    length = 4 * span
    flops = documents * (2 * length * features * 3 * part + 4 * length * length * part)
    per_doc = pl.BlockSpec((1, length, part), lambda d: (d, 0, 0))
    return pl.pallas_call(
        functools.partial(attend_kernel, waits=len(after)),
        grid=(documents,),
        in_specs=[pl.BlockSpec(memory_space=pltpu.SMEM)]
        + [pl.BlockSpec((1, span, features), lambda d: (d, 0, 0))] * 4
        + [pl.BlockSpec((part, 3 * part), lambda d: (0, 0))] * 4
        + [pl.BlockSpec((3, 1, part), lambda d: (0, 0, 0))]
        + [any_spec()] * len(after),
        out_specs=[per_doc] * 3
        + [pl.BlockSpec((3, features, part), lambda d: (0, 0, 0))]
        + [pl.BlockSpec((1, part // HEAD_DIM, length), lambda d: (d, 0, 0))]
        + [pl.BlockSpec((part, span), lambda d: (0, d))] * 4,
        out_shape=[jax.ShapeDtypeStruct((documents, length, part), BF16)] * 3
        + [jax.ShapeDtypeStruct((3, features, part), BF16)]
        + [jax.ShapeDtypeStruct((documents, part // HEAD_DIM, length), F32)]
        + [jax.ShapeDtypeStruct((part, documents * span), BF16)] * 4,
        compiler_params=params(56),
        cost_estimate=pl.CostEstimate(
            flops=flops, bytes_accessed=8 * 1024 * 1024, transcendentals=documents * length * length * 3
        ),
        name="attend",
    )(seq, *x_blocks, *w_blocks, bias, *after)


def attend_back_kernel(place_ref, *refs, waits):
    g_refs, x_refs, a_refs = refs[:4], refs[4:8], refs[8:12]
    q_ref, k_ref, v_ref, wc_ref, log_ref = refs[12:17]
    keep_ref, give_ref, dw_keep_ref, dw_give_ref, sums_ref, acc_ref = refs[17 + waits :]
    part = q_ref.shape[2]
    span = x_refs[0].shape[1]
    first = pl.program_id(0) == 0
    q, k, v = q_ref[0], k_ref[0], v_ref[0]
    g = jnp.concatenate([ref[...] for ref in g_refs], axis=1)
    product = g.astype(F32) * jnp.concatenate([ref[...] for ref in a_refs], axis=1).astype(F32)
    lane = lax.broadcasted_iota(jnp.int32, (1, part), 1) // HEAD_DIM
    scale = 1.0 / math.sqrt(HEAD_DIM)
    k_t = k.T
    dq, dk, dv = [], None, None
    for h in range(part // HEAD_DIM):
        on = lane == h
        pick = jnp.where(on, scale, 0.0).astype(BF16)
        mask = jnp.where(on, 1.0, 0.0)
        chances = jnp.exp(nt(k, q * pick) - log_ref[0, h : h + 1, :])
        drift = jnp.sum(product[h * HEAD_DIM : (h + 1) * HEAD_DIM], axis=0, keepdims=True)
        grad = (chances * (nn(v * mask.astype(BF16), g) - drift)).astype(BF16)
        part_v = nt(chances.astype(BF16), g) * mask
        part_k = nn(grad, q) * (mask * scale)
        dq.append(nn(k_t[h * HEAD_DIM : (h + 1) * HEAD_DIM], grad) * scale)
        dk = part_k if dk is None else dk + part_k
        dv = part_v if dv is None else dv + part_v
    low = [t.astype(BF16) for t in (jnp.concatenate(dq, axis=0).T, dk, dv)]
    sums = jnp.concatenate(
        [jnp.sum(low[i].astype(F32), axis=0, keepdims=True) for i in (0, 2)], axis=0
    )
    x = jnp.concatenate([ref[0] for ref in x_refs], axis=0)
    x_t = x.T
    inner = nt(low[0], wc_ref[0]) + nt(low[1], wc_ref[1]) + nt(low[2], wc_ref[2])
    inner = inner.astype(BF16)
    for r in range(4):
        (give_ref if r % 2 else keep_ref)[r // 2, 0] = inner[r * span : (r + 1) * span]

    @pl.when(first)
    def _():
        sums_ref[...] = sums
        for i in range(3):
            acc_ref[i] = nn(x_t, low[i])

    @pl.when(jnp.logical_not(first))
    def _():
        sums_ref[...] += sums
        for i in range(3):
            acc_ref[i] += nn(x_t, low[i])

    @pl.when(pl.program_id(0) == pl.num_programs(0) - 1)
    def _():
        tall = part // PIECES
        dp = place_ref[1] % NEAR
        first = HEAD_ORDER[0]
        for p in range(PIECES):
            spot = place(p ^ dp, HEAD_ORDER[1:])
            for mine, ref in ((True, dw_keep_ref), (False, dw_give_ref)):

                @pl.when(((p ^ dp) // first % 2 == 0) == mine)
                def _(p=p, spot=spot, ref=ref):
                    for block in range(4):
                        at = block * part + p * tall
                        for i in range(3):
                            ref[spot, place_ref[0] ^ block, :, i * part : (i + 1) * part] = acc_ref[
                                i, at : at + tall, :
                            ].astype(BF16)


def attend_back(place_word, g_blocks, x_blocks, attended, q, k, v, wc, logs, after):
    documents, span, features = x_blocks[0].shape
    part = q.shape[2]
    length = 4 * span
    flops = documents * (4 * length * features * 3 * part + 10 * length * length * part)
    per_doc = pl.BlockSpec((1, length, part), lambda d: (d, 0, 0))
    pair = pl.BlockSpec((2, 1, span, features), lambda d: (0, d, 0, 0))
    return pl.pallas_call(
        functools.partial(attend_back_kernel, waits=len(after)),
        grid=(documents,),
        in_specs=[pl.BlockSpec(memory_space=pltpu.SMEM)]
        + [pl.BlockSpec((part, span), lambda d: (0, d))] * 4
        + [pl.BlockSpec((1, span, features), lambda d: (d, 0, 0))] * 4
        + [pl.BlockSpec((part, span), lambda d: (0, d))] * 4
        + [per_doc] * 3
        + [pl.BlockSpec((3, features, part), lambda d: (0, 0, 0))]
        + [pl.BlockSpec((1, part // HEAD_DIM, length), lambda d: (d, 0, 0))]
        + [any_spec()] * len(after),
        out_specs=[
            pair,
            pair,
            pl.BlockSpec((PIECES // 2, 4, part // PIECES, 3 * part), lambda d: (0, 0, 0, 0)),
            pl.BlockSpec((PIECES // 2, 4, part // PIECES, 3 * part), lambda d: (0, 0, 0, 0)),
            pl.BlockSpec((2, part), lambda d: (0, 0)),
        ],
        out_shape=[jax.ShapeDtypeStruct((2, documents, span, features), BF16)] * 2
        + [
            jax.ShapeDtypeStruct((PIECES // 2, 4, part // PIECES, 3 * part), BF16),
            jax.ShapeDtypeStruct((PIECES // 2, 4, part // PIECES, 3 * part), BF16),
            jax.ShapeDtypeStruct((2, part), F32),
        ],
        scratch_shapes=[pltpu.VMEM((3, features, part), F32)],
        compiler_params=params(56),
        cost_estimate=pl.CostEstimate(
            flops=flops, bytes_accessed=12 * 1024 * 1024, transcendentals=documents * length * length * 3
        ),
        name="attend_back",
    )(place_word, *g_blocks, *x_blocks, *attended, q, k, v, wc, logs, *after)


def gelu_parts(x):
    square = x * x
    bend = jnp.tanh(GELU_IN * x * (1.0 + GELU_CUBE * square))
    gate = 0.5 * (1.0 + bend)
    rise = 0.5 * x * (1.0 - bend * bend) * (GELU_IN + 3.0 * GELU_IN * GELU_CUBE * square)
    return x * gate, gate + rise


def place(index, order):
    at = 0
    for by in order:
        at = 2 * at + (index // by) % 2
    return at


def weight_copies(place_ref, pieces, wo, up, down, sems):
    seq, dp = place_ref[0], place_ref[1]
    part = wo.shape[1]
    half = part // 2
    wo_copies, up_copies, down_copies = [], [[] for _ in range(4)], [[] for _ in range(4)]

    def bring(found, source, target):
        found.append(pltpu.make_async_copy(source, target, sems.at[sum(used)]))
        used.append(1)

    used = []
    own, near, far, one, near_one, far_one = pieces[:6]
    bit = dp % 2
    parts = [(own.at[h], 0, h) for h in range(2)] + [(one.at[h], 1, h) for h in range(2)]
    parts += [(near, 2, bit), (far, 2, 1 - bit), (near_one, 3, bit), (far_one, 3, 1 - bit)]
    for source, r, h in parts:
        at = pl.multiple_of(h * half, half)
        bring(wo_copies, source.at[pl.ds(0, half)], wo.at[r, pl.ds(at, half)])
        if up is None:
            continue
        at = pl.multiple_of((seq ^ r) * part + h * half, half)
        for i in range(4):
            start = pl.multiple_of(half * (1 + (seq ^ i)), half)
            bring(up_copies[i], source.at[pl.ds(start, half)], up.at[i, pl.ds(at, half)])
    for r in range(4 if down is not None else 0):
        bring(down_copies[r], pieces[6 + r], down.at[r])
    return wo_copies, up_copies, down_copies


def start_all(copies):
    for copy in copies:
        copy.start()


def wait_all(copies):
    for copy in copies:
        copy.wait()


def forward_kernel(place_ref, *refs):
    (a_refs, in_ref, cot_ref, vec_ref, upb_ref), refs = (refs[:4], *refs[4:8]), refs[8:]
    pieces, refs = refs[:10], refs[10:]
    out_ref, unit_ref, scale_ref, grad_ref, sums_ref, upsum_ref = refs[:6]
    outs = (refs[6:9], refs[9:12])
    wo, up, down, act, slope, low_t, spare, terms, sems, out_sems = refs[12:]
    seq, dp = place_ref[0], place_ref[1]
    part = wo.shape[1]
    half = part // 2
    size = terms.shape[3]

    wo_copies, up_copies, down_copies = weight_copies(place_ref, pieces, wo, up, down, sems)
    start_all(wo_copies + up_copies[0] + up_copies[1])
    out_bias, gain1, shift1, down_bias, gain2, shift2 = (vec_ref[i : i + 1, :] for i in range(6))
    residual = in_ref[...] + out_bias
    wait_all(wo_copies)
    joined = jnp.concatenate([ref[...] for ref in a_refs], axis=0)
    residual += tn(joined, wo[...].reshape(joined.shape[0], -1))
    unit1, scale1 = norm_parts(residual)
    unit_ref[...] = unit1
    scale_ref[...] = scale1
    first_out = unit1 * gain1 + shift1
    low = first_out.astype(BF16)
    for r in range(4):
        wait_all(up_copies[r])
        start_all(up_copies[r + 2] if r < 2 else down_copies[2 * r - 4] + down_copies[2 * r - 3])
        x = nn(low, up[r]) + upb_ref[pl.ds(seq ^ r, 1), :]
        value, rise = gelu_parts(x)
        act[r] = value.astype(BF16)
        slope[r] = rise
    second_in = first_out + down_bias
    for r in range(4):
        wait_all(down_copies[r])
        second_in += nn(act[r], down[r])
    unit2, scale2 = norm_parts(second_in)
    out_ref[...] = (unit2 * gain2 + shift2).astype(BF16)
    incoming = cot_ref[...].astype(F32)
    grad_first = norm_back(incoming, unit2, scale2, gain2)
    grad_down = grad_first.astype(BF16)
    sums_ref[0:1, :] = jnp.sum(incoming * unit2, axis=0, keepdims=True)
    sums_ref[1:2, :] = jnp.sum(incoming, axis=0, keepdims=True)
    sums_ref[2:3, :] = jnp.sum(grad_down.astype(F32), axis=0, keepdims=True)
    spare[...] = low.T
    for i in range(4):
        low_t[i * part : (i + 1) * part, :] = spare[pl.ds(pl.multiple_of((seq ^ i) * part, part), part), :]
    for r in range(4):
        grad_act = nt(grad_down, down[r]).astype(BF16).astype(F32)
        grad_up = (grad_act * slope[r]).astype(BF16)
        upsum_ref[pl.ds(seq ^ r, 1), :] = jnp.sum(grad_up.astype(F32), axis=0, keepdims=True)
        grad_first += nt(grad_up, up[r])
        value = nn(low_t[...], grad_up).astype(BF16)
        for i in range(4):
            for h in range(2):
                spot = place((2 * (seq ^ r) + h) ^ (dp % NEAR), UP_ORDER)
                at = i * part + h * half
                terms[1, i, spot] = value[at : at + half]
    grad_ref[...] = grad_first

    def send(which, r):
        keep_out, far_out, give_out = outs[which]
        target = (keep_out, give_out.at[0], far_out, give_out.at[1])[r]
        return pltpu.make_async_copy(terms.at[which, r], target, out_sems.at[which, r])

    start_all([send(1, r) for r in range(4)])
    for r in range(4):
        value = tn(act[r], grad_down)
        for p in range(PIECES):
            spot = place(p ^ (dp % NEAR), DOWN_ORDER)
            terms[0, r, spot] = value[p * size : (p + 1) * size].astype(BF16)
        send(0, r).start()
    wait_all([send(which, r) for which in range(2) for r in range(4)])


def backward_kernel(place_ref, *refs):
    (a_refs, unit_ref, scale_ref, grad_ref, vec_ref), refs = (refs[:4], *refs[4:8]), refs[8:]
    pieces, refs = refs[:6], refs[6:]
    res_ref, g_refs, sums_ref, keep_ref, far_ref, give_ref, wo, sems = refs[0], refs[1:5], *refs[5:]
    dp = place_ref[1]
    part = wo.shape[1]
    tall = part // PIECES
    copies = weight_copies(place_ref, pieces, wo, None, None, sems)[0]
    start_all(copies)
    unit1 = unit_ref[...]
    grad_first = grad_ref[...]
    grad_residual = norm_back(grad_first, unit1, scale_ref[...], vec_ref[1:2, :])
    res_ref[...] = grad_residual
    grad_out = grad_residual.astype(BF16)
    joined = jnp.concatenate([ref[...] for ref in a_refs], axis=0)
    value = nn(joined, grad_out)
    for r in range(4):
        for p in range(PIECES):
            spot = place(p ^ (dp % NEAR), UP_ORDER)
            piece = value[r * part + p * tall : r * part + (p + 1) * tall].astype(BF16)
            if r % 2:
                give_ref[r // 2, spot] = piece
            else:
                (far_ref if r else keep_ref)[spot] = piece
    sums_ref[0:1, :] = jnp.sum(grad_first * unit1, axis=0, keepdims=True)
    sums_ref[1:2, :] = jnp.sum(grad_first, axis=0, keepdims=True)
    sums_ref[2:3, :] = jnp.sum(grad_out.astype(F32), axis=0, keepdims=True)
    wait_all(copies)
    back = nt(wo[...].reshape(joined.shape[0], -1), grad_out).astype(BF16)
    for r in range(4):
        g_refs[r][...] = back[r * part : (r + 1) * part]


def shaped(*shape, dtype=BF16):
    return jax.ShapeDtypeStruct(shape, dtype)


def any_spec():
    return pl.BlockSpec(memory_space=pl.ANY)


def forward(place_word, attended, embedded, cotangent, vectors, up_bias, pieces):
    rows, features = embedded.shape
    part = attended[0].shape[0]
    size = features // PIECES
    term = [shaped(PIECES, size, features)] * 2 + [shaped(2, PIECES, size, features)]
    return pl.pallas_call(
        forward_kernel,
        in_specs=[pl.BlockSpec(memory_space=pltpu.SMEM)] + [whole_spec()] * 8 + [any_spec()] * 10,
        out_specs=[whole_spec()] * 6 + [any_spec()] * 6,
        out_shape=[
            shaped(rows, features),
            shaped(rows, features, dtype=F32),
            shaped(rows, 1, dtype=F32),
            shaped(rows, features, dtype=F32),
            shaped(3, features, dtype=F32),
            shaped(4, features, dtype=F32),
        ]
        + term
        + term,
        scratch_shapes=[
            pltpu.VMEM((4, part, features), BF16),
            pltpu.VMEM((4, features, features), BF16),
            pltpu.VMEM((4, features, features), BF16),
            pltpu.VMEM((4, rows, features), BF16),
            pltpu.VMEM((4, rows, features), F32),
            pltpu.VMEM((features, rows), BF16),
            pltpu.VMEM((features, rows), BF16),
            pltpu.VMEM((2, 4, PIECES, size, features), BF16),
            pltpu.SemaphoreType.DMA((44,)),
            pltpu.SemaphoreType.DMA((2, 4)),
        ],
        compiler_params=params(56),
        cost_estimate=pl.CostEstimate(
            flops=12 * rows * features * 4 * features,
            bytes_accessed=26 * 1024 * 1024,
            transcendentals=rows * 4 * features,
        ),
        name="forward",
    )(place_word, *attended, embedded, cotangent, vectors, up_bias, *pieces)


def backward(place_word, attended, unit, scale, grad, vectors, pieces):
    rows, features = unit.shape
    part = attended[0].shape[0]
    piece = (PIECES, part // PIECES, features)
    return pl.pallas_call(
        backward_kernel,
        in_specs=[pl.BlockSpec(memory_space=pltpu.SMEM)] + [whole_spec()] * 8 + [any_spec()] * 6,
        out_specs=[whole_spec()] * 9,
        out_shape=[shaped(rows, features, dtype=F32)]
        + [shaped(part, rows)] * 4
        + [shaped(3, features, dtype=F32), shaped(*piece), shaped(*piece), shaped(2, *piece)],
        scratch_shapes=[pltpu.VMEM((4, part, features), BF16), pltpu.SemaphoreType.DMA((44,))],
        compiler_params=params(56),
        cost_estimate=pl.CostEstimate(
            flops=4 * rows * features * features, bytes_accessed=6 * 1024 * 1024, transcendentals=rows
        ),
        name="backward",
    )(place_word, *attended, unit, scale, grad, vectors, *pieces)


def fold_kernel(*refs, body, inputs, waits):
    body(refs[:inputs], refs[inputs + waits :])


def fold(body, arrays, shapes, after, name):
    return pl.pallas_call(
        functools.partial(fold_kernel, body=body, inputs=len(arrays), waits=len(after)),
        in_specs=[whole_spec()] * len(arrays) + [any_spec()] * len(after),
        out_specs=[whole_spec()] * len(shapes),
        out_shape=[shaped(*shape) for shape in shapes],
        compiler_params=params(40),
        cost_estimate=pl.CostEstimate(flops=0, bytes_accessed=4 * 1024 * 1024, transcendentals=0),
        name=name,
    )(*arrays, *after)


def added(*values):
    return sum(v.astype(F32) for v in values[1:]) + values[0].astype(F32)


def fold_down_core(ins, outs):
    keeps, got = ins[:2], ins[2]
    half = got.shape[1] // 2
    for i, mine in enumerate(keeps):
        outs[i][...] = added(mine[:half], got[i, :half]).astype(BF16)
        outs[2 + i][...] = added(mine[half:], got[i, half:]).astype(BF16)


def fold_up_core(ins, outs):
    size = ins[0].shape[1]
    half = ins[0].shape[0] // 2
    for keep, far, got, rows in ((*ins[:3], slice(0, size)), (*ins[3:], slice(size, None))):
        for i, part in enumerate((slice(0, half), slice(half, None))):
            outs[i][:, rows] = added(keep[part], got[0, part]).astype(BF16)
            outs[2 + i][:, rows] = added(far[part], got[1, part]).astype(BF16)


def fold_both(ins, outs):
    down, down_got, up, up_got = ins
    outs[0][...] = added(down[...], down_got[...]).astype(BF16)
    half = up.shape[0] // 2
    outs[1][...] = added(up[:half], up_got[:half]).astype(BF16)
    outs[2][...] = added(up[half:], up_got[half:]).astype(BF16)


def fold_half(ins, outs):
    mine, got = ins
    half = mine.shape[0] // 2
    outs[0][...] = added(mine[:half], got[:half]).astype(BF16)
    outs[1][...] = added(mine[half:], got[half:]).astype(BF16)


def fold_sum(ins, outs):
    outs[0][...] = added(ins[0][...], ins[1][...]).astype(BF16)


def fold_inner(ins, outs):
    mine, got = ins
    for i in range(2):
        outs[i][...] = added(mine[i], got[i]).astype(BF16)


def settle_kernel(place_ref, *refs, order, store, waits):
    held, outs = refs[:4], refs[4 + waits :]
    seq, dp = place_ref[0], place_ref[1] % NEAR
    for index in range(PIECES):
        spot = place(index, order)
        store(outs, held[spot // 2].at[spot % 2], index ^ dp, seq)


def store_down(outs, piece, p, seq):
    size = piece.shape[0]
    outs[0][pl.ds(pl.multiple_of(p * size, size), size), :] = piece[...].astype(F32)


def store_up(outs, piece, p, seq):
    size, wide = outs[0].shape[0] // 2, piece.shape[1]
    tall = piece.shape[0] - size
    row, column = pl.multiple_of((p % 2) * size, size), pl.multiple_of((p // 2) * wide, wide)
    outs[0][pl.ds(row, size), pl.ds(column, wide)] = piece[:size].astype(F32)
    outs[1][pl.ds(pl.multiple_of(p * tall, 8), tall), :] = piece[size:].astype(F32)


def store_heads(outs, piece, p, seq):
    tall, part = piece.shape[1], piece.shape[2] // 3
    rows = pl.ds(pl.multiple_of(p * tall, 8), tall)
    for c in range(4):
        columns = slice(c * part, (c + 1) * part)
        block = piece[seq ^ c].astype(F32)
        for i in range(3):
            outs[i][rows, columns] = block[:, i * part : (i + 1) * part]


def settle(place_word, held, order, store, shapes, after=()):
    return pl.pallas_call(
        functools.partial(settle_kernel, order=order, store=store, waits=len(after)),
        in_specs=[pl.BlockSpec(memory_space=pltpu.SMEM)] + [whole_spec()] * 4 + [any_spec()] * len(after),
        out_specs=[whole_spec()] * len(shapes),
        out_shape=[jax.ShapeDtypeStruct(shape, F32) for shape in shapes],
        compiler_params=params(56),
        cost_estimate=pl.CostEstimate(flops=0, bytes_accessed=4 * 1024 * 1024, transcendentals=0),
        name="settle",
    )(place_word, *held, *after)


def gate_kernel(*refs):
    pass


def gate(x, *after):
    return pl.pallas_call(
        gate_kernel,
        in_specs=[any_spec()] * (1 + len(after)),
        out_specs=any_spec(),
        out_shape=shaped(*x.shape, dtype=x.dtype),
        input_output_aliases={0: 0},
        cost_estimate=pl.CostEstimate(flops=0, bytes_accessed=0, transcendentals=0),
        name="gate",
    )(x, *after)


def reduce_dp(x, orders):
    for by in orders:
        half = x.shape[0] // 2
        x = x[:half].astype(F32) + swap(x[half:].astype(BF16), "dp", by).astype(F32)
    return x


def reduce_rest(x, last, *after):
    for by in (last, *bits("dp")[3:]):
        x = x.astype(BF16)
        got = swap(x, "dp", by)
        if after and by == last:
            (x,) = fold(fold_sum, [x, got], [x.shape], after, "sum")
        else:
            x = x.astype(F32) + got.astype(F32)
    return x.astype(BF16)


def spread_dp(x, first, last, *after):
    got = swap(x, "dp", first)
    if after:
        got = gate(got, *after)
    return x, got, swap(x, "dp", last), swap(got, "dp", last)


def body(
    text_embed,
    region_feature,
    token_mask,
    segment_mask,
    mask_vector,
    batch_gain,
    batch_shift,
    query_weight,
    query_bias,
    key_weight,
    value_weight,
    value_bias,
    output_weight,
    output_bias,
    first_gain,
    first_shift,
    up_weight,
    up_bias,
    down_weight,
    down_bias,
    second_gain,
    second_shift,
    cotangent,
):
    documents, span, features = text_embed.shape
    rows = documents * span
    seq, dp = lax.axis_index("seq"), lax.axis_index("dp")
    group = lax.axis_size("seq")
    population = rows * lax.axis_size("dp") * group
    score_scale = 1.0 / math.sqrt(HEAD_DIM)
    part = features // group
    heads = part // HEAD_DIM

    place_word = jnp.stack([seq, dp]).astype(jnp.int32)
    cut, halves, mine = pack(
        place_word, query_weight, key_weight, value_weight, output_weight, up_weight
    )

    region = region_feature.astype(F32).reshape(rows, features)
    sums = jnp.stack([jnp.sum(region, axis=0), jnp.sum(region * region, axis=0)])
    chip_sums = sums + swap(sums, "seq", 2)
    chip_sums = gate(chip_sums, cut[0])
    sums = chip_sums + swap(chip_sums, "seq", 1)
    head_blocks = exchange_blocks(cut)
    for by in bits("dp"):
        if by == 4:
            sums = gate(sums, head_blocks[2], head_blocks[3])
        sums = sums + swap(sums, "dp", by)
    average = sums[0] / population
    inverse = lax.rsqrt(sums[1] / population - average * average + EPS_BATCH)

    bias3 = jnp.stack([query_bias, jnp.zeros_like(query_bias), value_bias]).reshape(3, group, part)
    head_bias = lax.dynamic_slice_in_dim(bias3, seq, 1, 1)
    pieces = gather_weight(halves, mine, 1)

    standard = (region - average) * inverse
    token_hit = token_mask.astype(F32).reshape(rows, 1)
    segment_keep = 1.0 - segment_mask.astype(F32).reshape(rows, 1)
    embedded = (
        text_embed.astype(F32).reshape(rows, features) * (1.0 - token_hit)
        + token_hit * mask_vector
        + segment_keep * (standard * batch_gain + batch_shift)
    )
    low_in = embedded.astype(BF16).reshape(documents, span, features)
    x_blocks = gather_rows(low_in)
    far = swap(gate(down_weight, low_in, pieces[1]), "seq", 2)
    q, k, v, head_weight, logs, *attended = attend(place_word, x_blocks, head_blocks, head_bias, [])
    attn_blocks = exchange_blocks(attended)
    far = gate(far, attn_blocks[3])
    pieces += [down_weight, swap(down_weight, "seq", 1), far, swap(far, "seq", 1)]
    vectors = jnp.stack([output_bias, first_gain, first_shift, down_bias, second_gain, second_shift])
    layer_output, unit, scale, grad_first, second_sums, up_sums, *terms = forward(
        place_word,
        attn_blocks,
        embedded,
        cotangent.reshape(rows, features),
        vectors,
        up_bias.reshape(group, features),
        pieces,
    )
    grad_residual, *rest = backward(place_word, attn_blocks, unit, scale, grad_first, vectors, pieces[:6])
    grad_attn, first_sums, (out_keep, out_far, out_give) = rest[:4], rest[4], rest[5:]
    down_keep, down_far, down_give = terms[:3]
    up_keep, up_far, up_give = terms[3:]

    half = PIECES // 2
    size, tall = features // PIECES, part // PIECES
    g_blocks = exchange_blocks(grad_attn)
    down, down_far, down_near_send, down_far_send = fold(
        fold_down_core,
        [down_keep, down_far, swap(down_give, "seq", 1)],
        [(half, size, features)] * 4,
        [g_blocks[2], g_blocks[3]],
        "down_core",
    )
    up, up_more, up_send, up_more_send = fold(
        fold_up_core,
        [up_keep, up_far, swap(up_give, "seq", 1), out_keep, out_far, swap(out_give, "seq", 1)],
        [(half, size + tall, features)] * 4,
        [down_far_send],
        "up_core",
    )
    down_far_got = swap(down_far_send, "dp", DOWN_ORDER[0])
    down_near_got = swap(down_near_send, "dp", DOWN_ORDER[0])
    up_more_got = swap(up_more_send, "seq", 2)
    up_got = swap(up_send, "seq", 2)

    keep, give, heads, heads_send, head_sums = attend_back(
        place_word, g_blocks, x_blocks, attended, q, k, v, head_weight, logs, [up_more_send]
    )
    query_sums, value_sums = head_sums[0], head_sums[1]

    quarter = half // 2
    down_send, up_send, up_more_send = fold(
        fold_both,
        [down_far, down_far_got, up_more, up_more_got],
        [(half, size, features)] + [(quarter, size + tall, features)] * 2,
        [head_sums],
        "both",
    )
    inner_own, inner_send = fold(
        fold_inner, [keep, swap(gate(give, up_more_send), "seq", 1)], [keep.shape[1:]] * 2, [up_send, down_near_got], "inner"
    )
    heads, heads_send = fold(
        fold_half,
        [heads, swap(gate(heads_send, up_more_send), "dp", HEAD_ORDER[0])],
        [(half // 2, group, tall, 3 * part)] * 2,
        [up_send, up_got],
        "heads",
    )
    inner_got = swap(inner_send, "seq", 2)
    got = gate(swap(up_more_send, "dp", UP_ORDER[0]), heads_send)
    up_more = up[quarter:].astype(F32) + up_got[quarter:].astype(F32) + got.astype(F32)
    got = swap(up_send, "dp", UP_ORDER[0])
    up = up[:quarter].astype(F32) + up_got[:quarter].astype(F32) + got.astype(F32)
    got = gate(swap(down_send, "seq", 2), up_more)
    down = down.astype(F32) + down_near_got.astype(F32) + got.astype(F32)
    heads = heads.astype(F32) + gate(swap(heads_send, "dp", HEAD_ORDER[1]), down).astype(F32)
    got = gate(swap(up_more.astype(BF16), "dp", UP_ORDER[1]), inner_got, down)
    up = up + got.astype(F32)
    down = reduce_dp(down, DOWN_ORDER[1:-1])

    inner = inner_own.astype(F32) + inner_got.astype(F32)
    grad_embedded = grad_residual + inner.reshape(rows, features)
    text_gradient = (grad_embedded * (1.0 - token_hit)).astype(BF16)
    grad_normed = grad_embedded * segment_keep

    def widen(x):
        return lax.dynamic_update_slice_in_dim(jnp.zeros((features,), F32), x, seq * part, 0)

    sums = jnp.concatenate(
        [
            jnp.stack(
                [
                    jnp.sum(grad_normed * standard, axis=0),
                    jnp.sum(grad_normed, axis=0),
                    jnp.sum(grad_embedded * token_hit, axis=0),
                    widen(query_sums),
                    widen(value_sums),
                ]
            ),
            second_sums,
            first_sums,
            up_sums,
        ]
    )
    for by in bits("seq"):
        sums = sums + swap(sums, "seq", by)

    own = reduce_rest(heads, HEAD_ORDER[-1], up, down)
    own = jnp.stack(exchange_blocks([own[:, r] for r in range(group)]), axis=1)
    held_heads = spread_dp(own, 1, 2)
    total_query, total_key, total_value = settle(
        place_word, held_heads, (2, 1, 4), store_heads, [query_weight.shape] * 3
    )

    up = reduce_rest(up, UP_ORDER[-1], sums)
    sums = sums + swap(sums, "dp", 1)
    down = reduce_rest(down, DOWN_ORDER[-1], up, sums)
    held_up = spread_dp(up, 2, 1, down)
    held_down = spread_dp(down, 1, 2, held_heads[3])
    for by in bits("dp")[1:]:
        sums = sums + swap(sums, "dp", by)
    (total_down,) = settle(place_word, held_down, (2, 1, 4), store_down, [down_weight.shape], [sums])
    total_up, total_out = settle(
        place_word, held_up, (1, 2, 4), store_up, [up_weight.shape, output_weight.shape], [sums]
    )

    (
        sum_gain,
        sum_shift,
        sum_mask,
        sum_query_bias,
        sum_value_bias,
        sum_second_gain,
        sum_second_shift,
        sum_down_bias,
        sum_first_gain,
        sum_first_shift,
        sum_output_bias,
    ) = sums[:11]
    sum_up_bias = sums[11:].reshape(-1)

    region_gradient = (
        batch_gain
        * inverse
        * (grad_normed - sum_shift / population - standard * (sum_gain / population))
    ).astype(BF16)
    shape = (documents, span, features)
    return (
        layer_output.reshape(shape),
        text_gradient.reshape(shape),
        region_gradient.reshape(shape),
        sum_mask,
        sum_gain,
        sum_shift,
        total_query,
        sum_query_bias,
        total_key,
        total_value,
        sum_value_bias,
        total_out,
        sum_output_bias,
        sum_first_gain,
        sum_first_shift,
        total_up,
        sum_up_bias,
        total_down,
        sum_down_bias,
        sum_second_gain,
        sum_second_shift,
    )


def solution(mesh):
    rows, weight, copied = P("dp", "seq", None), P("seq", None), P()
    mask = P("dp", "seq")
    in_specs = (
        (rows, rows, mask, mask, copied, copied, copied)
        + (weight, copied, weight, weight, copied, weight, copied, copied, copied)
        + (weight, copied, weight, copied, copied, copied, rows)
    )
    out_specs = (
        (rows, rows, rows, copied, copied, copied)
        + (weight, copied, weight, weight, copied, weight, copied, copied, copied)
        + (weight, copied, weight, copied, copied, copied)
    )
    return jax.shard_map(body, mesh=mesh, in_specs=in_specs, out_specs=out_specs, check_vma=False)
```

```python
import functools
import math

import jax
import jax.numpy as jnp
from jax import lax
from jax.experimental import pallas as pl
from jax.experimental.pallas import tpu as pltpu
from jax.sharding import PartitionSpec as P

HEAD_DIM = 64
EPS_NORM = 1e-12
EPS_BATCH = 1e-05
F32 = jnp.float32
BF16 = jnp.bfloat16
GELU_IN = math.sqrt(2.0 / math.pi)
GELU_CUBE = 0.044715
PIECES = 8
NEAR = 4
DOWN_ORDER = (2, 1, 4)
UP_ORDER = (1, 2, 4)
HEAD_ORDER = (1, 2, 4)


def swap(x, axis, by):
    return lax.ppermute(x, axis, [(i, i ^ by) for i in range(lax.axis_size(axis))])


def bits(axis):
    found, by = [], 1
    while by < lax.axis_size(axis):
        found.append(by)
        by *= 2
    return found


def nn(a, b):
    return jnp.dot(a, b, preferred_element_type=F32)


def tn(a, b):
    return lax.dot_general(a, b, (((0,), (0,)), ((), ())), preferred_element_type=F32)


def nt(a, b):
    return lax.dot_general(a, b, (((1,), (1,)), ((), ())), preferred_element_type=F32)


def norm_parts(x):
    centred = x - jnp.mean(x, axis=-1, keepdims=True)
    scale = lax.rsqrt(jnp.mean(centred * centred, axis=-1, keepdims=True) + EPS_NORM)
    return centred * scale, scale


def norm_back(grad, unit, scale, gain):
    g = grad * gain
    return scale * (
        g
        - jnp.mean(g, axis=-1, keepdims=True)
        - unit * jnp.mean(g * unit, axis=-1, keepdims=True)
    )


def gather_rows(x):
    two = swap(x, "seq", 2)
    one, three = swap(x, "seq", 1), swap(two, "seq", 1)
    return [x, one, two, three]


def gather_weight(halves, mine, by):
    near = swap(mine, "seq", 2)
    far = swap(near, "dp", by)
    return [halves, near, far, swap(halves, "seq", 1), swap(near, "seq", 1), swap(far, "seq", 1)]


def scatter_pairs(keep, give):
    got = swap(give, "seq", 1)
    pass_on = (keep[1].astype(F32) + got[1].astype(F32)).astype(BF16)
    own = keep[0].astype(F32) + got[0].astype(F32)
    return own + swap(pass_on, "seq", 2).astype(F32)


def exchange_blocks(blocks):
    return [blocks[0]] + [swap(blocks[r], "seq", r) for r in (1, 2, 3)]


def params(mebibytes):
    return pltpu.CompilerParams(vmem_limit_bytes=mebibytes * 1024 * 1024)


def whole_spec():
    return pl.BlockSpec(memory_space=pltpu.VMEM)


def pack_heads_kernel(place_ref, q_ref, k_ref, v_ref, *head_refs):
    seq = place_ref[0]
    part = q_ref.shape[0]
    for c in range(4):
        for r in range(4):

            @pl.when(seq == c ^ r)
            def _(c=c, r=r):
                for i, ref in enumerate((q_ref, k_ref, v_ref)):
                    head_refs[r][:, i * part : (i + 1) * part] = ref[:, c * part : (c + 1) * part]


def pack_halves_kernel(place_ref, out_ref, up_ref, halves_ref, near_ref):
    bit = place_ref[1] % 2
    half = out_ref.shape[0] // 2
    wide = out_ref.shape[1]

    def cut(rows):
        blocks = [out_ref[rows, :]] + [up_ref[rows, j * wide : (j + 1) * wide] for j in range(4)]
        return jnp.concatenate(blocks, axis=0)

    for h in range(2):
        halves_ref[h] = cut(pl.ds(h * half, half))
    near_ref[...] = cut(pl.ds(pl.multiple_of(bit * half, half), half))


def pack(place_word, query, key, value, out, up):
    part, features = out.shape
    tall = part // 2 * 5
    heads = pl.pallas_call(
        pack_heads_kernel,
        in_specs=[pl.BlockSpec(memory_space=pltpu.SMEM)] + [whole_spec()] * 3,
        out_specs=[whole_spec()] * 4,
        out_shape=[shaped(part, 3 * part)] * 4,
        compiler_params=params(56),
        cost_estimate=pl.CostEstimate(flops=0, bytes_accessed=2 * 1024 * 1024, transcendentals=0),
        name="pack_heads",
    )(place_word, query, key, value)
    halves, near = pl.pallas_call(
        pack_halves_kernel,
        in_specs=[pl.BlockSpec(memory_space=pltpu.SMEM)] + [whole_spec()] * 2,
        out_specs=[whole_spec()] * 2,
        out_shape=[shaped(2, tall, features), shaped(tall, features)],
        compiler_params=params(56),
        cost_estimate=pl.CostEstimate(flops=0, bytes_accessed=4 * 1024 * 1024, transcendentals=0),
        name="pack_halves",
    )(place_word, out, up)
    return heads, halves, near


def attend_kernel(seq_ref, *refs, waits):
    x_refs, w_refs, bias_ref, refs = refs[:4], refs[4:8], refs[8], refs[9 + waits :]
    q_ref, k_ref, v_ref, wc_ref, log_ref, out_refs = refs[0], refs[1], refs[2], refs[3], refs[4], refs[5:]
    part = w_refs[0].shape[0]
    span = x_refs[0].shape[1]

    @pl.when(pl.program_id(0) == 0)
    def _():
        for r in range(4):
            at = pl.multiple_of((seq_ref[0] ^ r) * part, part)
            for i in range(3):
                wc_ref[i, pl.ds(at, part), :] = w_refs[r][:, i * part : (i + 1) * part]

    x = jnp.concatenate([ref[0] for ref in x_refs], axis=0)
    for i, ref in enumerate((q_ref, k_ref, v_ref)):
        ref[0] = (nn(x, wc_ref[i]) + bias_ref[i]).astype(BF16)
    q, k, v = q_ref[0], k_ref[0], v_ref[0]
    lane = lax.broadcasted_iota(jnp.int32, (1, part), 1) // HEAD_DIM
    for h in range(part // HEAD_DIM):
        pick = jnp.where(lane == h, 1.0 / math.sqrt(HEAD_DIM), 0.0).astype(BF16)
        scores = nt(k, q * pick)
        top = jnp.max(scores, axis=0, keepdims=True)
        raised = jnp.exp(scores - top)
        total = jnp.sum(raised, axis=0, keepdims=True)
        log_ref[0, h : h + 1, :] = top + jnp.log(total)
        attended = tn(v, raised.astype(BF16))[h * HEAD_DIM : (h + 1) * HEAD_DIM]
        attended = (attended * (1.0 / total)).astype(BF16)
        for r in range(4):
            out_refs[r][h * HEAD_DIM : (h + 1) * HEAD_DIM, :] = attended[:, r * span : (r + 1) * span]


def attend(seq, x_blocks, w_blocks, bias, after):
    documents, span, features = x_blocks[0].shape
    part = w_blocks[0].shape[0]
    length = 4 * span
    flops = documents * (2 * length * features * 3 * part + 4 * length * length * part)
    per_doc = pl.BlockSpec((1, length, part), lambda d: (d, 0, 0))
    return pl.pallas_call(
        functools.partial(attend_kernel, waits=len(after)),
        grid=(documents,),
        in_specs=[pl.BlockSpec(memory_space=pltpu.SMEM)]
        + [pl.BlockSpec((1, span, features), lambda d: (d, 0, 0))] * 4
        + [pl.BlockSpec((part, 3 * part), lambda d: (0, 0))] * 4
        + [pl.BlockSpec((3, 1, part), lambda d: (0, 0, 0))]
        + [any_spec()] * len(after),
        out_specs=[per_doc] * 3
        + [pl.BlockSpec((3, features, part), lambda d: (0, 0, 0))]
        + [pl.BlockSpec((1, part // HEAD_DIM, length), lambda d: (d, 0, 0))]
        + [pl.BlockSpec((part, span), lambda d: (0, d))] * 4,
        out_shape=[jax.ShapeDtypeStruct((documents, length, part), BF16)] * 3
        + [jax.ShapeDtypeStruct((3, features, part), BF16)]
        + [jax.ShapeDtypeStruct((documents, part // HEAD_DIM, length), F32)]
        + [jax.ShapeDtypeStruct((part, documents * span), BF16)] * 4,
        compiler_params=params(56),
        cost_estimate=pl.CostEstimate(
            flops=flops, bytes_accessed=8 * 1024 * 1024, transcendentals=documents * length * length * 3
        ),
        name="attend",
    )(seq, *x_blocks, *w_blocks, bias, *after)


def attend_back_kernel(place_ref, *refs, waits):
    g_refs, x_refs, a_refs = refs[:4], refs[4:8], refs[8:12]
    q_ref, k_ref, v_ref, wc_ref, log_ref = refs[12:17]
    keep_ref, give_ref, dw_keep_ref, dw_give_ref, sums_ref, acc_ref = refs[17 + waits :]
    part = q_ref.shape[2]
    span = x_refs[0].shape[1]
    first = pl.program_id(0) == 0
    q, k, v = q_ref[0], k_ref[0], v_ref[0]
    g = jnp.concatenate([ref[...] for ref in g_refs], axis=1)
    product = g.astype(F32) * jnp.concatenate([ref[...] for ref in a_refs], axis=1).astype(F32)
    lane = lax.broadcasted_iota(jnp.int32, (1, part), 1) // HEAD_DIM
    scale = 1.0 / math.sqrt(HEAD_DIM)
    k_t = k.T
    dq, dk, dv = [], None, None
    for h in range(part // HEAD_DIM):
        on = lane == h
        pick = jnp.where(on, scale, 0.0).astype(BF16)
        mask = jnp.where(on, 1.0, 0.0)
        chances = jnp.exp(nt(k, q * pick) - log_ref[0, h : h + 1, :])
        drift = jnp.sum(product[h * HEAD_DIM : (h + 1) * HEAD_DIM], axis=0, keepdims=True)
        grad = (chances * (nn(v * mask.astype(BF16), g) - drift)).astype(BF16)
        part_v = nt(chances.astype(BF16), g) * mask
        part_k = nn(grad, q) * (mask * scale)
        dq.append(nn(k_t[h * HEAD_DIM : (h + 1) * HEAD_DIM], grad) * scale)
        dk = part_k if dk is None else dk + part_k
        dv = part_v if dv is None else dv + part_v
    low = [t.astype(BF16) for t in (jnp.concatenate(dq, axis=0).T, dk, dv)]
    sums = jnp.concatenate(
        [jnp.sum(low[i].astype(F32), axis=0, keepdims=True) for i in (0, 2)], axis=0
    )
    x = jnp.concatenate([ref[0] for ref in x_refs], axis=0)
    x_t = x.T
    inner = nt(low[0], wc_ref[0]) + nt(low[1], wc_ref[1]) + nt(low[2], wc_ref[2])
    inner = inner.astype(BF16)
    for r in range(4):
        (give_ref if r % 2 else keep_ref)[r // 2, 0] = inner[r * span : (r + 1) * span]

    @pl.when(first)
    def _():
        sums_ref[...] = sums
        for i in range(3):
            acc_ref[i] = nn(x_t, low[i])

    @pl.when(jnp.logical_not(first))
    def _():
        sums_ref[...] += sums
        for i in range(3):
            acc_ref[i] += nn(x_t, low[i])

    @pl.when(pl.program_id(0) == pl.num_programs(0) - 1)
    def _():
        tall = part // PIECES
        dp = place_ref[1] % NEAR
        first = HEAD_ORDER[0]
        for p in range(PIECES):
            spot = place(p ^ dp, HEAD_ORDER[1:])
            for mine, ref in ((True, dw_keep_ref), (False, dw_give_ref)):

                @pl.when(((p ^ dp) // first % 2 == 0) == mine)
                def _(p=p, spot=spot, ref=ref):
                    for block in range(4):
                        at = block * part + p * tall
                        for i in range(3):
                            ref[spot, place_ref[0] ^ block, :, i * part : (i + 1) * part] = acc_ref[
                                i, at : at + tall, :
                            ].astype(BF16)


def attend_back(place_word, g_blocks, x_blocks, attended, q, k, v, wc, logs, after):
    documents, span, features = x_blocks[0].shape
    part = q.shape[2]
    length = 4 * span
    flops = documents * (4 * length * features * 3 * part + 10 * length * length * part)
    per_doc = pl.BlockSpec((1, length, part), lambda d: (d, 0, 0))
    pair = pl.BlockSpec((2, 1, span, features), lambda d: (0, d, 0, 0))
    return pl.pallas_call(
        functools.partial(attend_back_kernel, waits=len(after)),
        grid=(documents,),
        in_specs=[pl.BlockSpec(memory_space=pltpu.SMEM)]
        + [pl.BlockSpec((part, span), lambda d: (0, d))] * 4
        + [pl.BlockSpec((1, span, features), lambda d: (d, 0, 0))] * 4
        + [pl.BlockSpec((part, span), lambda d: (0, d))] * 4
        + [per_doc] * 3
        + [pl.BlockSpec((3, features, part), lambda d: (0, 0, 0))]
        + [pl.BlockSpec((1, part // HEAD_DIM, length), lambda d: (d, 0, 0))]
        + [any_spec()] * len(after),
        out_specs=[
            pair,
            pair,
            pl.BlockSpec((PIECES // 2, 4, part // PIECES, 3 * part), lambda d: (0, 0, 0, 0)),
            pl.BlockSpec((PIECES // 2, 4, part // PIECES, 3 * part), lambda d: (0, 0, 0, 0)),
            pl.BlockSpec((2, part), lambda d: (0, 0)),
        ],
        out_shape=[jax.ShapeDtypeStruct((2, documents, span, features), BF16)] * 2
        + [
            jax.ShapeDtypeStruct((PIECES // 2, 4, part // PIECES, 3 * part), BF16),
            jax.ShapeDtypeStruct((PIECES // 2, 4, part // PIECES, 3 * part), BF16),
            jax.ShapeDtypeStruct((2, part), F32),
        ],
        scratch_shapes=[pltpu.VMEM((3, features, part), F32)],
        compiler_params=params(56),
        cost_estimate=pl.CostEstimate(
            flops=flops, bytes_accessed=12 * 1024 * 1024, transcendentals=documents * length * length * 3
        ),
        name="attend_back",
    )(place_word, *g_blocks, *x_blocks, *attended, q, k, v, wc, logs, *after)


def gelu_parts(x):
    square = x * x
    bend = jnp.tanh(GELU_IN * x * (1.0 + GELU_CUBE * square))
    gate = 0.5 * (1.0 + bend)
    rise = 0.5 * x * (1.0 - bend * bend) * (GELU_IN + 3.0 * GELU_IN * GELU_CUBE * square)
    return x * gate, gate + rise


def place(index, order):
    at = 0
    for by in order:
        at = 2 * at + (index // by) % 2
    return at


def weight_copies(place_ref, pieces, wo, up, down, sems):
    seq, dp = place_ref[0], place_ref[1]
    part = wo.shape[1]
    half = part // 2
    wo_copies, up_copies, down_copies = [], [[] for _ in range(4)], [[] for _ in range(4)]

    def bring(found, source, target):
        found.append(pltpu.make_async_copy(source, target, sems.at[sum(used)]))
        used.append(1)

    used = []
    own, near, far, one, near_one, far_one = pieces[:6]
    bit = dp % 2
    parts = [(own.at[h], 0, h) for h in range(2)] + [(one.at[h], 1, h) for h in range(2)]
    parts += [(near, 2, bit), (far, 2, 1 - bit), (near_one, 3, bit), (far_one, 3, 1 - bit)]
    for source, r, h in parts:
        at = pl.multiple_of(h * half, half)
        bring(wo_copies, source.at[pl.ds(0, half)], wo.at[r, pl.ds(at, half)])
        if up is None:
            continue
        at = pl.multiple_of((seq ^ r) * part + h * half, half)
        for i in range(4):
            start = pl.multiple_of(half * (1 + (seq ^ i)), half)
            bring(up_copies[i], source.at[pl.ds(start, half)], up.at[i, pl.ds(at, half)])
    for r in range(4 if down is not None else 0):
        bring(down_copies[r], pieces[6 + r], down.at[r])
    return wo_copies, up_copies, down_copies


def start_all(copies):
    for copy in copies:
        copy.start()


def wait_all(copies):
    for copy in copies:
        copy.wait()


def forward_kernel(place_ref, *refs):
    (a_refs, in_ref, cot_ref, vec_ref, upb_ref), refs = (refs[:4], *refs[4:8]), refs[8:]
    pieces, refs = refs[:10], refs[10:]
    out_ref, unit_ref, scale_ref, grad_ref, sums_ref, upsum_ref = refs[:6]
    outs = (refs[6:9], refs[9:12])
    wo, up, down, act, slope, low_t, spare, terms, sems, out_sems = refs[12:]
    seq, dp = place_ref[0], place_ref[1]
    part = wo.shape[1]
    half = part // 2
    size = terms.shape[3]

    wo_copies, up_copies, down_copies = weight_copies(place_ref, pieces, wo, up, down, sems)
    start_all(wo_copies + sum(up_copies, []) + sum(down_copies, []))
    out_bias, gain1, shift1, down_bias, gain2, shift2 = (vec_ref[i : i + 1, :] for i in range(6))
    residual = in_ref[...] + out_bias
    wait_all(wo_copies)
    joined = jnp.concatenate([ref[...] for ref in a_refs], axis=0)
    residual += tn(joined, wo[...].reshape(joined.shape[0], -1))
    unit1, scale1 = norm_parts(residual)
    unit_ref[...] = unit1
    scale_ref[...] = scale1
    first_out = unit1 * gain1 + shift1
    low = first_out.astype(BF16)
    wait_all(sum(up_copies, []))
    wait_all(sum(down_copies, []))
    second_in = first_out + down_bias
    for r in range(4):
        x = nn(low, up[r]) + upb_ref[pl.ds(seq ^ r, 1), :]
        value, rise = gelu_parts(x)
        act[r] = value.astype(BF16)
        slope[r] = rise
        second_in += nn(act[r], down[r])
    unit2, scale2 = norm_parts(second_in)
    out_ref[...] = (unit2 * gain2 + shift2).astype(BF16)
    incoming = cot_ref[...].astype(F32)
    grad_first = norm_back(incoming, unit2, scale2, gain2)
    grad_down = grad_first.astype(BF16)
    sums_ref[0:1, :] = jnp.sum(incoming * unit2, axis=0, keepdims=True)
    sums_ref[1:2, :] = jnp.sum(incoming, axis=0, keepdims=True)
    sums_ref[2:3, :] = jnp.sum(grad_down.astype(F32), axis=0, keepdims=True)
    spare[...] = low.T
    for i in range(4):
        low_t[i * part : (i + 1) * part, :] = spare[pl.ds(pl.multiple_of((seq ^ i) * part, part), part), :]
    for r in range(4):
        grad_act = nt(grad_down, down[r]).astype(BF16).astype(F32)
        grad_up = (grad_act * slope[r]).astype(BF16)
        upsum_ref[pl.ds(seq ^ r, 1), :] = jnp.sum(grad_up.astype(F32), axis=0, keepdims=True)
        grad_first += nt(grad_up, up[r])
        value = nn(low_t[...], grad_up).astype(BF16)
        for i in range(4):
            for h in range(2):
                spot = place((2 * (seq ^ r) + h) ^ (dp % NEAR), UP_ORDER)
                at = i * part + h * half
                terms[1, i, spot] = value[at : at + half]
    grad_ref[...] = grad_first

    def send(which, r):
        keep_out, far_out, give_out = outs[which]
        target = (keep_out, give_out.at[0], far_out, give_out.at[1])[r]
        return pltpu.make_async_copy(terms.at[which, r], target, out_sems.at[which, r])

    start_all([send(1, r) for r in range(4)])
    for r in range(4):
        value = tn(act[r], grad_down)
        for p in range(PIECES):
            spot = place(p ^ (dp % NEAR), DOWN_ORDER)
            terms[0, r, spot] = value[p * size : (p + 1) * size].astype(BF16)
        send(0, r).start()
    wait_all([send(which, r) for which in range(2) for r in range(4)])


def backward_kernel(place_ref, *refs):
    (a_refs, unit_ref, scale_ref, grad_ref, vec_ref), refs = (refs[:4], *refs[4:8]), refs[8:]
    pieces, refs = refs[:6], refs[6:]
    res_ref, g_refs, sums_ref, keep_ref, far_ref, give_ref, wo, sems = refs[0], refs[1:5], *refs[5:]
    dp = place_ref[1]
    part = wo.shape[1]
    tall = part // PIECES
    copies = weight_copies(place_ref, pieces, wo, None, None, sems)[0]
    start_all(copies)
    unit1 = unit_ref[...]
    grad_first = grad_ref[...]
    grad_residual = norm_back(grad_first, unit1, scale_ref[...], vec_ref[1:2, :])
    res_ref[...] = grad_residual
    grad_out = grad_residual.astype(BF16)
    joined = jnp.concatenate([ref[...] for ref in a_refs], axis=0)
    value = nn(joined, grad_out)
    for r in range(4):
        for p in range(PIECES):
            spot = place(p ^ (dp % NEAR), UP_ORDER)
            piece = value[r * part + p * tall : r * part + (p + 1) * tall].astype(BF16)
            if r % 2:
                give_ref[r // 2, spot] = piece
            else:
                (far_ref if r else keep_ref)[spot] = piece
    sums_ref[0:1, :] = jnp.sum(grad_first * unit1, axis=0, keepdims=True)
    sums_ref[1:2, :] = jnp.sum(grad_first, axis=0, keepdims=True)
    sums_ref[2:3, :] = jnp.sum(grad_out.astype(F32), axis=0, keepdims=True)
    wait_all(copies)
    back = nt(wo[...].reshape(joined.shape[0], -1), grad_out).astype(BF16)
    for r in range(4):
        g_refs[r][...] = back[r * part : (r + 1) * part]


def shaped(*shape, dtype=BF16):
    return jax.ShapeDtypeStruct(shape, dtype)


def any_spec():
    return pl.BlockSpec(memory_space=pl.ANY)


def forward(place_word, attended, embedded, cotangent, vectors, up_bias, pieces):
    rows, features = embedded.shape
    part = attended[0].shape[0]
    size = features // PIECES
    term = [shaped(PIECES, size, features)] * 2 + [shaped(2, PIECES, size, features)]
    return pl.pallas_call(
        forward_kernel,
        in_specs=[pl.BlockSpec(memory_space=pltpu.SMEM)] + [whole_spec()] * 8 + [any_spec()] * 10,
        out_specs=[whole_spec()] * 6 + [any_spec()] * 6,
        out_shape=[
            shaped(rows, features),
            shaped(rows, features, dtype=F32),
            shaped(rows, 1, dtype=F32),
            shaped(rows, features, dtype=F32),
            shaped(3, features, dtype=F32),
            shaped(4, features, dtype=F32),
        ]
        + term
        + term,
        scratch_shapes=[
            pltpu.VMEM((4, part, features), BF16),
            pltpu.VMEM((4, features, features), BF16),
            pltpu.VMEM((4, features, features), BF16),
            pltpu.VMEM((4, rows, features), BF16),
            pltpu.VMEM((4, rows, features), F32),
            pltpu.VMEM((features, rows), BF16),
            pltpu.VMEM((features, rows), BF16),
            pltpu.VMEM((2, 4, PIECES, size, features), BF16),
            pltpu.SemaphoreType.DMA((44,)),
            pltpu.SemaphoreType.DMA((2, 4)),
        ],
        compiler_params=params(56),
        cost_estimate=pl.CostEstimate(
            flops=12 * rows * features * 4 * features,
            bytes_accessed=26 * 1024 * 1024,
            transcendentals=rows * 4 * features,
        ),
        name="forward",
    )(place_word, *attended, embedded, cotangent, vectors, up_bias, *pieces)


def backward(place_word, attended, unit, scale, grad, vectors, pieces):
    rows, features = unit.shape
    part = attended[0].shape[0]
    piece = (PIECES, part // PIECES, features)
    return pl.pallas_call(
        backward_kernel,
        in_specs=[pl.BlockSpec(memory_space=pltpu.SMEM)] + [whole_spec()] * 8 + [any_spec()] * 6,
        out_specs=[whole_spec()] * 9,
        out_shape=[shaped(rows, features, dtype=F32)]
        + [shaped(part, rows)] * 4
        + [shaped(3, features, dtype=F32), shaped(*piece), shaped(*piece), shaped(2, *piece)],
        scratch_shapes=[pltpu.VMEM((4, part, features), BF16), pltpu.SemaphoreType.DMA((44,))],
        compiler_params=params(56),
        cost_estimate=pl.CostEstimate(
            flops=4 * rows * features * features, bytes_accessed=6 * 1024 * 1024, transcendentals=rows
        ),
        name="backward",
    )(place_word, *attended, unit, scale, grad, vectors, *pieces)


def fold_kernel(*refs, body, inputs, waits):
    body(refs[:inputs], refs[inputs + waits :])


def fold(body, arrays, shapes, after, name):
    return pl.pallas_call(
        functools.partial(fold_kernel, body=body, inputs=len(arrays), waits=len(after)),
        in_specs=[whole_spec()] * len(arrays) + [any_spec()] * len(after),
        out_specs=[whole_spec()] * len(shapes),
        out_shape=[shaped(*shape) for shape in shapes],
        compiler_params=params(40),
        cost_estimate=pl.CostEstimate(flops=0, bytes_accessed=4 * 1024 * 1024, transcendentals=0),
        name=name,
    )(*arrays, *after)


def added(*values):
    return sum(v.astype(F32) for v in values[1:]) + values[0].astype(F32)


def fold_down_core(ins, outs):
    keeps, got = ins[:2], ins[2]
    half = got.shape[1] // 2
    for i, mine in enumerate(keeps):
        outs[i][...] = added(mine[:half], got[i, :half]).astype(BF16)
        outs[2 + i][...] = added(mine[half:], got[i, half:]).astype(BF16)


def fold_up_core(ins, outs):
    size = ins[0].shape[1]
    half = ins[0].shape[0] // 2
    for keep, far, got, rows in ((*ins[:3], slice(0, size)), (*ins[3:], slice(size, None))):
        for i, part in enumerate((slice(0, half), slice(half, None))):
            outs[i][:, rows] = added(keep[part], got[0, part]).astype(BF16)
            outs[2 + i][:, rows] = added(far[part], got[1, part]).astype(BF16)


def fold_both(ins, outs):
    down, down_got, up, up_got = ins
    outs[0][...] = added(down[...], down_got[...]).astype(BF16)
    half = up.shape[0] // 2
    outs[1][...] = added(up[:half], up_got[:half]).astype(BF16)
    outs[2][...] = added(up[half:], up_got[half:]).astype(BF16)


def fold_half(ins, outs):
    mine, got = ins
    half = mine.shape[0] // 2
    outs[0][...] = added(mine[:half], got[:half]).astype(BF16)
    outs[1][...] = added(mine[half:], got[half:]).astype(BF16)


def fold_sum(ins, outs):
    outs[0][...] = added(ins[0][...], ins[1][...]).astype(BF16)


def fold_inner(ins, outs):
    mine, got = ins
    for i in range(2):
        outs[i][...] = added(mine[i], got[i]).astype(BF16)


def settle_kernel(place_ref, *refs, order, store, waits):
    held, outs = refs[:4], refs[4 + waits :]
    seq, dp = place_ref[0], place_ref[1] % NEAR
    for index in range(PIECES):
        spot = place(index, order)
        store(outs, held[spot // 2].at[spot % 2], index ^ dp, seq)


def store_down(outs, piece, p, seq):
    size = piece.shape[0]
    outs[0][pl.ds(pl.multiple_of(p * size, size), size), :] = piece[...].astype(F32)


def store_up(outs, piece, p, seq):
    size, wide = outs[0].shape[0] // 2, piece.shape[1]
    tall = piece.shape[0] - size
    row, column = pl.multiple_of((p % 2) * size, size), pl.multiple_of((p // 2) * wide, wide)
    outs[0][pl.ds(row, size), pl.ds(column, wide)] = piece[:size].astype(F32)
    outs[1][pl.ds(pl.multiple_of(p * tall, 8), tall), :] = piece[size:].astype(F32)


def store_heads(outs, piece, p, seq):
    tall, part = piece.shape[1], piece.shape[2] // 3
    rows = pl.ds(pl.multiple_of(p * tall, 8), tall)
    for c in range(4):
        columns = slice(c * part, (c + 1) * part)
        block = piece[seq ^ c].astype(F32)
        for i in range(3):
            outs[i][rows, columns] = block[:, i * part : (i + 1) * part]


def settle(place_word, held, order, store, shapes, after=()):
    return pl.pallas_call(
        functools.partial(settle_kernel, order=order, store=store, waits=len(after)),
        in_specs=[pl.BlockSpec(memory_space=pltpu.SMEM)] + [whole_spec()] * 4 + [any_spec()] * len(after),
        out_specs=[whole_spec()] * len(shapes),
        out_shape=[jax.ShapeDtypeStruct(shape, F32) for shape in shapes],
        compiler_params=params(56),
        cost_estimate=pl.CostEstimate(flops=0, bytes_accessed=4 * 1024 * 1024, transcendentals=0),
        name="settle",
    )(place_word, *held, *after)


def gate_kernel(*refs):
    pass


def gate(x, *after):
    return pl.pallas_call(
        gate_kernel,
        in_specs=[any_spec()] * (1 + len(after)),
        out_specs=any_spec(),
        out_shape=shaped(*x.shape, dtype=x.dtype),
        input_output_aliases={0: 0},
        cost_estimate=pl.CostEstimate(flops=0, bytes_accessed=0, transcendentals=0),
        name="gate",
    )(x, *after)


def reduce_dp(x, orders):
    for by in orders:
        half = x.shape[0] // 2
        x = x[:half].astype(F32) + swap(x[half:].astype(BF16), "dp", by).astype(F32)
    return x


def reduce_rest(x, last, *after):
    for by in (last, *bits("dp")[3:]):
        x = x.astype(BF16)
        got = swap(x, "dp", by)
        if after and by == last:
            (x,) = fold(fold_sum, [x, got], [x.shape], after, "sum")
        else:
            x = x.astype(F32) + got.astype(F32)
    return x.astype(BF16)


def spread_dp(x, first, last, *after):
    got = swap(x, "dp", first)
    if after:
        got = gate(got, *after)
    return x, got, swap(x, "dp", last), swap(got, "dp", last)


def body(
    text_embed,
    region_feature,
    token_mask,
    segment_mask,
    mask_vector,
    batch_gain,
    batch_shift,
    query_weight,
    query_bias,
    key_weight,
    value_weight,
    value_bias,
    output_weight,
    output_bias,
    first_gain,
    first_shift,
    up_weight,
    up_bias,
    down_weight,
    down_bias,
    second_gain,
    second_shift,
    cotangent,
):
    documents, span, features = text_embed.shape
    rows = documents * span
    seq, dp = lax.axis_index("seq"), lax.axis_index("dp")
    group = lax.axis_size("seq")
    population = rows * lax.axis_size("dp") * group
    score_scale = 1.0 / math.sqrt(HEAD_DIM)
    part = features // group
    heads = part // HEAD_DIM

    place_word = jnp.stack([seq, dp]).astype(jnp.int32)
    cut, halves, mine = pack(
        place_word, query_weight, key_weight, value_weight, output_weight, up_weight
    )

    region = region_feature.astype(F32).reshape(rows, features)
    sums = jnp.stack([jnp.sum(region, axis=0), jnp.sum(region * region, axis=0)])
    chip_sums = sums + swap(sums, "seq", 2)
    chip_sums = gate(chip_sums, cut[0])
    sums = chip_sums + swap(chip_sums, "seq", 1)
    head_blocks = exchange_blocks(cut)
    for by in bits("dp"):
        if by == 4:
            sums = gate(sums, head_blocks[2], head_blocks[3])
        sums = sums + swap(sums, "dp", by)
    average = sums[0] / population
    inverse = lax.rsqrt(sums[1] / population - average * average + EPS_BATCH)

    bias3 = jnp.stack([query_bias, jnp.zeros_like(query_bias), value_bias]).reshape(3, group, part)
    head_bias = lax.dynamic_slice_in_dim(bias3, seq, 1, 1)
    pieces = gather_weight(halves, mine, 1)

    standard = (region - average) * inverse
    token_hit = token_mask.astype(F32).reshape(rows, 1)
    segment_keep = 1.0 - segment_mask.astype(F32).reshape(rows, 1)
    embedded = (
        text_embed.astype(F32).reshape(rows, features) * (1.0 - token_hit)
        + token_hit * mask_vector
        + segment_keep * (standard * batch_gain + batch_shift)
    )
    low_in = embedded.astype(BF16).reshape(documents, span, features)
    x_blocks = gather_rows(low_in)
    far = swap(gate(down_weight, low_in, pieces[1]), "seq", 2)
    q, k, v, head_weight, logs, *attended = attend(place_word, x_blocks, head_blocks, head_bias, [])
    attn_blocks = exchange_blocks(attended)
    far = gate(far, attn_blocks[3])
    pieces += [down_weight, swap(down_weight, "seq", 1), far, swap(far, "seq", 1)]
    vectors = jnp.stack([output_bias, first_gain, first_shift, down_bias, second_gain, second_shift])
    layer_output, unit, scale, grad_first, second_sums, up_sums, *terms = forward(
        place_word,
        attn_blocks,
        embedded,
        cotangent.reshape(rows, features),
        vectors,
        up_bias.reshape(group, features),
        pieces,
    )
    grad_residual, *rest = backward(place_word, attn_blocks, unit, scale, grad_first, vectors, pieces[:6])
    grad_attn, first_sums, (out_keep, out_far, out_give) = rest[:4], rest[4], rest[5:]
    down_keep, down_far, down_give = terms[:3]
    up_keep, up_far, up_give = terms[3:]

    half = PIECES // 2
    size, tall = features // PIECES, part // PIECES
    g_blocks = exchange_blocks(grad_attn)
    down, down_far, down_near_send, down_far_send = fold(
        fold_down_core,
        [down_keep, down_far, swap(down_give, "seq", 1)],
        [(half, size, features)] * 4,
        [g_blocks[2], g_blocks[3]],
        "down_core",
    )
    up, up_more, up_send, up_more_send = fold(
        fold_up_core,
        [up_keep, up_far, swap(up_give, "seq", 1), out_keep, out_far, swap(out_give, "seq", 1)],
        [(half, size + tall, features)] * 4,
        [down_far_send],
        "up_core",
    )
    down_far_got = swap(down_far_send, "dp", DOWN_ORDER[0])
    down_near_got = swap(down_near_send, "dp", DOWN_ORDER[0])
    up_more_got = swap(up_more_send, "seq", 2)
    up_got = swap(up_send, "seq", 2)

    keep, give, heads, heads_send, head_sums = attend_back(
        place_word, g_blocks, x_blocks, attended, q, k, v, head_weight, logs, [up_more_send]
    )
    query_sums, value_sums = head_sums[0], head_sums[1]

    quarter = half // 2
    down_send, up_send, up_more_send = fold(
        fold_both,
        [down_far, down_far_got, up_more, up_more_got],
        [(half, size, features)] + [(quarter, size + tall, features)] * 2,
        [head_sums],
        "both",
    )
    inner_own, inner_send = fold(
        fold_inner, [keep, swap(gate(give, up_more_send), "seq", 1)], [keep.shape[1:]] * 2, [up_send, down_near_got], "inner"
    )
    heads, heads_send = fold(
        fold_half,
        [heads, swap(gate(heads_send, up_more_send), "dp", HEAD_ORDER[0])],
        [(half // 2, group, tall, 3 * part)] * 2,
        [up_send, up_got],
        "heads",
    )
    inner_got = swap(inner_send, "seq", 2)
    got = gate(swap(up_more_send, "dp", UP_ORDER[0]), heads_send)
    up_more = up[quarter:].astype(F32) + up_got[quarter:].astype(F32) + got.astype(F32)
    got = swap(up_send, "dp", UP_ORDER[0])
    up = up[:quarter].astype(F32) + up_got[:quarter].astype(F32) + got.astype(F32)
    got = gate(swap(down_send, "seq", 2), up_more)
    down = down.astype(F32) + down_near_got.astype(F32) + got.astype(F32)
    heads = heads.astype(F32) + gate(swap(heads_send, "dp", HEAD_ORDER[1]), down).astype(F32)
    got = gate(swap(up_more.astype(BF16), "dp", UP_ORDER[1]), inner_got, down)
    up = up + got.astype(F32)
    down = reduce_dp(down, DOWN_ORDER[1:-1])

    inner = inner_own.astype(F32) + inner_got.astype(F32)
    grad_embedded = grad_residual + inner.reshape(rows, features)
    text_gradient = (grad_embedded * (1.0 - token_hit)).astype(BF16)
    grad_normed = grad_embedded * segment_keep

    def widen(x):
        return lax.dynamic_update_slice_in_dim(jnp.zeros((features,), F32), x, seq * part, 0)

    sums = jnp.concatenate(
        [
            jnp.stack(
                [
                    jnp.sum(grad_normed * standard, axis=0),
                    jnp.sum(grad_normed, axis=0),
                    jnp.sum(grad_embedded * token_hit, axis=0),
                    widen(query_sums),
                    widen(value_sums),
                ]
            ),
            second_sums,
            first_sums,
            up_sums,
        ]
    )
    for by in bits("seq"):
        sums = sums + swap(sums, "seq", by)

    own = reduce_rest(heads, HEAD_ORDER[-1], up, down)
    own = jnp.stack(exchange_blocks([own[:, r] for r in range(group)]), axis=1)
    held_heads = spread_dp(own, 1, 2)
    total_query, total_key, total_value = settle(
        place_word, held_heads, (2, 1, 4), store_heads, [query_weight.shape] * 3
    )

    up = reduce_rest(up, UP_ORDER[-1], sums)
    sums = sums + swap(sums, "dp", 1)
    down = reduce_rest(down, DOWN_ORDER[-1], up, sums)
    held_up = spread_dp(up, 2, 1, down)
    held_down = spread_dp(down, 1, 2, held_heads[3])
    for by in bits("dp")[1:]:
        sums = sums + swap(sums, "dp", by)
    (total_down,) = settle(place_word, held_down, (2, 1, 4), store_down, [down_weight.shape], [sums])
    total_up, total_out = settle(
        place_word, held_up, (1, 2, 4), store_up, [up_weight.shape, output_weight.shape], [sums]
    )

    (
        sum_gain,
        sum_shift,
        sum_mask,
        sum_query_bias,
        sum_value_bias,
        sum_second_gain,
        sum_second_shift,
        sum_down_bias,
        sum_first_gain,
        sum_first_shift,
        sum_output_bias,
    ) = sums[:11]
    sum_up_bias = sums[11:].reshape(-1)

    region_gradient = (
        batch_gain
        * inverse
        * (grad_normed - sum_shift / population - standard * (sum_gain / population))
    ).astype(BF16)
    shape = (documents, span, features)
    return (
        layer_output.reshape(shape),
        text_gradient.reshape(shape),
        region_gradient.reshape(shape),
        sum_mask,
        sum_gain,
        sum_shift,
        total_query,
        sum_query_bias,
        total_key,
        total_value,
        sum_value_bias,
        total_out,
        sum_output_bias,
        sum_first_gain,
        sum_first_shift,
        total_up,
        sum_up_bias,
        total_down,
        sum_down_bias,
        sum_second_gain,
        sum_second_shift,
    )


def solution(mesh):
    rows, weight, copied = P("dp", "seq", None), P("seq", None), P()
    mask = P("dp", "seq")
    in_specs = (
        (rows, rows, mask, mask, copied, copied, copied)
        + (weight, copied, weight, weight, copied, weight, copied, copied, copied)
        + (weight, copied, weight, copied, copied, copied, rows)
    )
    out_specs = (
        (rows, rows, rows, copied, copied, copied)
        + (weight, copied, weight, weight, copied, weight, copied, copied, copied)
        + (weight, copied, weight, copied, copied, copied)
    )
    return jax.shard_map(body, mesh=mesh, in_specs=in_specs, out_specs=out_specs, check_vma=False)
```

```python
import functools
import math

import jax
import jax.numpy as jnp
from jax import lax
from jax.experimental import pallas as pl
from jax.experimental.pallas import tpu as pltpu
from jax.sharding import PartitionSpec as P

HEAD_DIM = 64
EPS_NORM = 1e-12
EPS_BATCH = 1e-05
F32 = jnp.float32
BF16 = jnp.bfloat16
GELU_IN = math.sqrt(2.0 / math.pi)
GELU_CUBE = 0.044715
PIECES = 8
NEAR = 4
DOWN_ORDER = (2, 1, 4)
UP_ORDER = (1, 2, 4)
HEAD_ORDER = (1, 2, 4)


def swap(x, axis, by):
    return lax.ppermute(x, axis, [(i, i ^ by) for i in range(lax.axis_size(axis))])


def bits(axis):
    found, by = [], 1
    while by < lax.axis_size(axis):
        found.append(by)
        by *= 2
    return found


def nn(a, b):
    return jnp.dot(a, b, preferred_element_type=F32)


def tn(a, b):
    return lax.dot_general(a, b, (((0,), (0,)), ((), ())), preferred_element_type=F32)


def nt(a, b):
    return lax.dot_general(a, b, (((1,), (1,)), ((), ())), preferred_element_type=F32)


def norm_parts(x):
    centred = x - jnp.mean(x, axis=-1, keepdims=True)
    scale = lax.rsqrt(jnp.mean(centred * centred, axis=-1, keepdims=True) + EPS_NORM)
    return centred * scale, scale


def norm_back(grad, unit, scale, gain):
    g = grad * gain
    return scale * (
        g
        - jnp.mean(g, axis=-1, keepdims=True)
        - unit * jnp.mean(g * unit, axis=-1, keepdims=True)
    )


def gather_rows(x):
    two = swap(x, "seq", 2)
    one, three = swap(x, "seq", 1), swap(two, "seq", 1)
    return [x, one, two, three]


def gather_weight(halves, mine, by):
    near = swap(mine, "seq", 2)
    far = swap(near, "dp", by)
    return [halves, near, far, swap(halves, "seq", 1), swap(near, "seq", 1), swap(far, "seq", 1)]


def scatter_pairs(keep, give):
    got = swap(give, "seq", 1)
    pass_on = (keep[1].astype(F32) + got[1].astype(F32)).astype(BF16)
    own = keep[0].astype(F32) + got[0].astype(F32)
    return own + swap(pass_on, "seq", 2).astype(F32)


def exchange_blocks(blocks):
    return [blocks[0]] + [swap(blocks[r], "seq", r) for r in (1, 2, 3)]


def params(mebibytes):
    return pltpu.CompilerParams(vmem_limit_bytes=mebibytes * 1024 * 1024)


def whole_spec():
    return pl.BlockSpec(memory_space=pltpu.VMEM)


def pack_heads_kernel(place_ref, q_ref, k_ref, v_ref, *head_refs):
    seq = place_ref[0]
    part = q_ref.shape[0]
    for c in range(4):
        for r in range(4):

            @pl.when(seq == c ^ r)
            def _(c=c, r=r):
                for i, ref in enumerate((q_ref, k_ref, v_ref)):
                    head_refs[r][:, i * part : (i + 1) * part] = ref[:, c * part : (c + 1) * part]


def pack_halves_kernel(place_ref, out_ref, up_ref, halves_ref, near_ref):
    bit = place_ref[1] % 2
    half = out_ref.shape[0] // 2
    wide = out_ref.shape[1]

    def cut(rows):
        blocks = [out_ref[rows, :]] + [up_ref[rows, j * wide : (j + 1) * wide] for j in range(4)]
        return jnp.concatenate(blocks, axis=0)

    for h in range(2):
        halves_ref[h] = cut(pl.ds(h * half, half))
    near_ref[...] = cut(pl.ds(pl.multiple_of(bit * half, half), half))


def pack(place_word, query, key, value, out, up):
    part, features = out.shape
    tall = part // 2 * 5
    heads = pl.pallas_call(
        pack_heads_kernel,
        in_specs=[pl.BlockSpec(memory_space=pltpu.SMEM)] + [whole_spec()] * 3,
        out_specs=[whole_spec()] * 4,
        out_shape=[shaped(part, 3 * part)] * 4,
        compiler_params=params(56),
        cost_estimate=pl.CostEstimate(flops=0, bytes_accessed=2 * 1024 * 1024, transcendentals=0),
        name="pack_heads",
    )(place_word, query, key, value)
    halves, near = pl.pallas_call(
        pack_halves_kernel,
        in_specs=[pl.BlockSpec(memory_space=pltpu.SMEM)] + [whole_spec()] * 2,
        out_specs=[whole_spec()] * 2,
        out_shape=[shaped(2, tall, features), shaped(tall, features)],
        compiler_params=params(56),
        cost_estimate=pl.CostEstimate(flops=0, bytes_accessed=4 * 1024 * 1024, transcendentals=0),
        name="pack_halves",
    )(place_word, out, up)
    return heads, halves, near


def attend_kernel(seq_ref, *refs, waits):
    x_refs, w_refs, bias_ref, refs = refs[:4], refs[4:8], refs[8], refs[9 + waits :]
    q_ref, k_ref, v_ref, wc_ref, log_ref, out_refs = refs[0], refs[1], refs[2], refs[3], refs[4], refs[5:]
    part = w_refs[0].shape[0]
    span = x_refs[0].shape[1]

    @pl.when(pl.program_id(0) == 0)
    def _():
        for r in range(4):
            at = pl.multiple_of((seq_ref[0] ^ r) * part, part)
            for i in range(3):
                wc_ref[i, pl.ds(at, part), :] = w_refs[r][:, i * part : (i + 1) * part]

    x = jnp.concatenate([ref[0] for ref in x_refs], axis=0)
    for i, ref in enumerate((q_ref, k_ref, v_ref)):
        ref[0] = (nn(x, wc_ref[i]) + bias_ref[i]).astype(BF16)
    q, k, v = q_ref[0], k_ref[0], v_ref[0]
    lane = lax.broadcasted_iota(jnp.int32, (1, part), 1) // HEAD_DIM
    for h in range(part // HEAD_DIM):
        pick = jnp.where(lane == h, 1.0 / math.sqrt(HEAD_DIM), 0.0).astype(BF16)
        scores = nt(k, q * pick)
        top = jnp.max(scores, axis=0, keepdims=True)
        raised = jnp.exp(scores - top)
        total = jnp.sum(raised, axis=0, keepdims=True)
        log_ref[0, h : h + 1, :] = top + jnp.log(total)
        attended = tn(v, raised.astype(BF16))[h * HEAD_DIM : (h + 1) * HEAD_DIM]
        attended = (attended * (1.0 / total)).astype(BF16)
        for r in range(4):
            out_refs[r][h * HEAD_DIM : (h + 1) * HEAD_DIM, :] = attended[:, r * span : (r + 1) * span]


def attend(seq, x_blocks, w_blocks, bias, after):
    documents, span, features = x_blocks[0].shape
    part = w_blocks[0].shape[0]
    length = 4 * span
    flops = documents * (2 * length * features * 3 * part + 4 * length * length * part)
    per_doc = pl.BlockSpec((1, length, part), lambda d: (d, 0, 0))
    return pl.pallas_call(
        functools.partial(attend_kernel, waits=len(after)),
        grid=(documents,),
        in_specs=[pl.BlockSpec(memory_space=pltpu.SMEM)]
        + [pl.BlockSpec((1, span, features), lambda d: (d, 0, 0))] * 4
        + [pl.BlockSpec((part, 3 * part), lambda d: (0, 0))] * 4
        + [pl.BlockSpec((3, 1, part), lambda d: (0, 0, 0))]
        + [any_spec()] * len(after),
        out_specs=[per_doc] * 3
        + [pl.BlockSpec((3, features, part), lambda d: (0, 0, 0))]
        + [pl.BlockSpec((1, part // HEAD_DIM, length), lambda d: (d, 0, 0))]
        + [pl.BlockSpec((part, span), lambda d: (0, d))] * 4,
        out_shape=[jax.ShapeDtypeStruct((documents, length, part), BF16)] * 3
        + [jax.ShapeDtypeStruct((3, features, part), BF16)]
        + [jax.ShapeDtypeStruct((documents, part // HEAD_DIM, length), F32)]
        + [jax.ShapeDtypeStruct((part, documents * span), BF16)] * 4,
        compiler_params=params(56),
        cost_estimate=pl.CostEstimate(
            flops=flops, bytes_accessed=8 * 1024 * 1024, transcendentals=documents * length * length * 3
        ),
        name="attend",
    )(seq, *x_blocks, *w_blocks, bias, *after)


def attend_back_kernel(place_ref, *refs, waits):
    g_refs, x_refs, a_refs = refs[:4], refs[4:8], refs[8:12]
    q_ref, k_ref, v_ref, wc_ref, log_ref = refs[12:17]
    keep_ref, give_ref, dw_keep_ref, dw_give_ref, sums_ref, acc_ref = refs[17 + waits :]
    part = q_ref.shape[2]
    span = x_refs[0].shape[1]
    first = pl.program_id(0) == 0
    q, k, v = q_ref[0], k_ref[0], v_ref[0]
    g = jnp.concatenate([ref[...] for ref in g_refs], axis=1)
    product = g.astype(F32) * jnp.concatenate([ref[...] for ref in a_refs], axis=1).astype(F32)
    lane = lax.broadcasted_iota(jnp.int32, (1, part), 1) // HEAD_DIM
    scale = 1.0 / math.sqrt(HEAD_DIM)
    k_t = k.T
    dq, dk, dv = [], None, None
    for h in range(part // HEAD_DIM):
        on = lane == h
        pick = jnp.where(on, scale, 0.0).astype(BF16)
        mask = jnp.where(on, 1.0, 0.0)
        chances = jnp.exp(nt(k, q * pick) - log_ref[0, h : h + 1, :])
        drift = jnp.sum(product[h * HEAD_DIM : (h + 1) * HEAD_DIM], axis=0, keepdims=True)
        grad = (chances * (nn(v * mask.astype(BF16), g) - drift)).astype(BF16)
        part_v = nt(chances.astype(BF16), g) * mask
        part_k = nn(grad, q) * (mask * scale)
        dq.append(nn(k_t[h * HEAD_DIM : (h + 1) * HEAD_DIM], grad) * scale)
        dk = part_k if dk is None else dk + part_k
        dv = part_v if dv is None else dv + part_v
    low = [t.astype(BF16) for t in (jnp.concatenate(dq, axis=0).T, dk, dv)]
    sums = jnp.concatenate(
        [jnp.sum(low[i].astype(F32), axis=0, keepdims=True) for i in (0, 2)], axis=0
    )
    x = jnp.concatenate([ref[0] for ref in x_refs], axis=0)
    x_t = x.T
    inner = nt(low[0], wc_ref[0]) + nt(low[1], wc_ref[1]) + nt(low[2], wc_ref[2])
    inner = inner.astype(BF16)
    for r in range(4):
        (give_ref if r % 2 else keep_ref)[r // 2, 0] = inner[r * span : (r + 1) * span]

    @pl.when(first)
    def _():
        sums_ref[...] = sums
        for i in range(3):
            acc_ref[i] = nn(x_t, low[i])

    @pl.when(jnp.logical_not(first))
    def _():
        sums_ref[...] += sums
        for i in range(3):
            acc_ref[i] += nn(x_t, low[i])

    @pl.when(pl.program_id(0) == pl.num_programs(0) - 1)
    def _():
        tall = part // PIECES
        dp = place_ref[1] % NEAR
        first = HEAD_ORDER[0]
        for p in range(PIECES):
            spot = place(p ^ dp, HEAD_ORDER[1:])
            for mine, ref in ((True, dw_keep_ref), (False, dw_give_ref)):

                @pl.when(((p ^ dp) // first % 2 == 0) == mine)
                def _(p=p, spot=spot, ref=ref):
                    for block in range(4):
                        at = block * part + p * tall
                        for i in range(3):
                            ref[spot, place_ref[0] ^ block, :, i * part : (i + 1) * part] = acc_ref[
                                i, at : at + tall, :
                            ].astype(BF16)


def attend_back(place_word, g_blocks, x_blocks, attended, q, k, v, wc, logs, after):
    documents, span, features = x_blocks[0].shape
    part = q.shape[2]
    length = 4 * span
    flops = documents * (4 * length * features * 3 * part + 10 * length * length * part)
    per_doc = pl.BlockSpec((1, length, part), lambda d: (d, 0, 0))
    pair = pl.BlockSpec((2, 1, span, features), lambda d: (0, d, 0, 0))
    return pl.pallas_call(
        functools.partial(attend_back_kernel, waits=len(after)),
        grid=(documents,),
        in_specs=[pl.BlockSpec(memory_space=pltpu.SMEM)]
        + [pl.BlockSpec((part, span), lambda d: (0, d))] * 4
        + [pl.BlockSpec((1, span, features), lambda d: (d, 0, 0))] * 4
        + [pl.BlockSpec((part, span), lambda d: (0, d))] * 4
        + [per_doc] * 3
        + [pl.BlockSpec((3, features, part), lambda d: (0, 0, 0))]
        + [pl.BlockSpec((1, part // HEAD_DIM, length), lambda d: (d, 0, 0))]
        + [any_spec()] * len(after),
        out_specs=[
            pair,
            pair,
            pl.BlockSpec((PIECES // 2, 4, part // PIECES, 3 * part), lambda d: (0, 0, 0, 0)),
            pl.BlockSpec((PIECES // 2, 4, part // PIECES, 3 * part), lambda d: (0, 0, 0, 0)),
            pl.BlockSpec((2, part), lambda d: (0, 0)),
        ],
        out_shape=[jax.ShapeDtypeStruct((2, documents, span, features), BF16)] * 2
        + [
            jax.ShapeDtypeStruct((PIECES // 2, 4, part // PIECES, 3 * part), BF16),
            jax.ShapeDtypeStruct((PIECES // 2, 4, part // PIECES, 3 * part), BF16),
            jax.ShapeDtypeStruct((2, part), F32),
        ],
        scratch_shapes=[pltpu.VMEM((3, features, part), F32)],
        compiler_params=params(56),
        cost_estimate=pl.CostEstimate(
            flops=flops, bytes_accessed=12 * 1024 * 1024, transcendentals=documents * length * length * 3
        ),
        name="attend_back",
    )(place_word, *g_blocks, *x_blocks, *attended, q, k, v, wc, logs, *after)


def gelu_parts(x):
    square = x * x
    bend = jnp.tanh(GELU_IN * x * (1.0 + GELU_CUBE * square))
    gate = 0.5 * (1.0 + bend)
    rise = 0.5 * x * (1.0 - bend * bend) * (GELU_IN + 3.0 * GELU_IN * GELU_CUBE * square)
    return x * gate, gate + rise


def place(index, order):
    at = 0
    for by in order:
        at = 2 * at + (index // by) % 2
    return at


def weight_copies(place_ref, pieces, wo, up, down, sems):
    seq, dp = place_ref[0], place_ref[1]
    part = wo.shape[1]
    half = part // 2
    wo_copies, up_copies, down_copies = [], [[] for _ in range(4)], [[] for _ in range(4)]

    def bring(found, source, target):
        found.append(pltpu.make_async_copy(source, target, sems.at[sum(used)]))
        used.append(1)

    used = []
    own, near, far, one, near_one, far_one = pieces[:6]
    bit = dp % 2
    parts = [(own.at[h], 0, h) for h in range(2)] + [(one.at[h], 1, h) for h in range(2)]
    parts += [(near, 2, bit), (far, 2, 1 - bit), (near_one, 3, bit), (far_one, 3, 1 - bit)]
    for source, r, h in parts:
        at = pl.multiple_of(h * half, half)
        bring(wo_copies, source.at[pl.ds(0, half)], wo.at[r, pl.ds(at, half)])
        if up is None:
            continue
        at = pl.multiple_of((seq ^ r) * part + h * half, half)
        for i in range(4):
            start = pl.multiple_of(half * (1 + (seq ^ i)), half)
            bring(up_copies[i], source.at[pl.ds(start, half)], up.at[i, pl.ds(at, half)])
    for r in range(4 if down is not None else 0):
        bring(down_copies[r], pieces[6 + r], down.at[r])
    return wo_copies, up_copies, down_copies


def start_all(copies):
    for copy in copies:
        copy.start()


def wait_all(copies):
    for copy in copies:
        copy.wait()


def forward_kernel(place_ref, *refs):
    (a_refs, in_ref, cot_ref, vec_ref, upb_ref), refs = (refs[:4], *refs[4:8]), refs[8:]
    pieces, refs = refs[:10], refs[10:]
    out_ref, unit_ref, scale_ref, grad_ref, sums_ref, upsum_ref = refs[:6]
    outs = (refs[6:9], refs[9:12])
    wo, up, down, act, slope, low_t, spare, terms, out_held, unit_held, sems, out_sems, early_sems = refs[12:]
    seq, dp = place_ref[0], place_ref[1]
    part = wo.shape[1]
    half = part // 2
    size = terms.shape[3]

    wo_copies, up_copies, down_copies = weight_copies(place_ref, pieces, wo, up, down, sems)
    start_all(wo_copies + sum(up_copies, []) + sum(down_copies, []))
    out_bias, gain1, shift1, down_bias, gain2, shift2 = (vec_ref[i : i + 1, :] for i in range(6))
    residual = in_ref[...] + out_bias
    wait_all(wo_copies)
    joined = jnp.concatenate([ref[...] for ref in a_refs], axis=0)
    residual += tn(joined, wo[...].reshape(joined.shape[0], -1))
    unit1, scale1 = norm_parts(residual)
    early = [
        pltpu.make_async_copy(unit_held, unit_ref, early_sems.at[0]),
        pltpu.make_async_copy(out_held, out_ref, early_sems.at[1]),
    ]
    unit_held[...] = unit1
    early[0].start()
    scale_ref[...] = scale1
    first_out = unit1 * gain1 + shift1
    low = first_out.astype(BF16)
    wait_all(sum(up_copies, []))
    wait_all(sum(down_copies, []))
    second_in = first_out + down_bias
    for r in range(4):
        x = nn(low, up[r]) + upb_ref[pl.ds(seq ^ r, 1), :]
        value, rise = gelu_parts(x)
        act[r] = value.astype(BF16)
        slope[r] = rise
        second_in += nn(act[r], down[r])
    unit2, scale2 = norm_parts(second_in)
    out_held[...] = (unit2 * gain2 + shift2).astype(BF16)
    early[1].start()
    incoming = cot_ref[...].astype(F32)
    grad_first = norm_back(incoming, unit2, scale2, gain2)
    grad_down = grad_first.astype(BF16)
    sums_ref[0:1, :] = jnp.sum(incoming * unit2, axis=0, keepdims=True)
    sums_ref[1:2, :] = jnp.sum(incoming, axis=0, keepdims=True)
    sums_ref[2:3, :] = jnp.sum(grad_down.astype(F32), axis=0, keepdims=True)
    spare[...] = low.T
    for i in range(4):
        low_t[i * part : (i + 1) * part, :] = spare[pl.ds(pl.multiple_of((seq ^ i) * part, part), part), :]
    for r in range(4):
        grad_act = nt(grad_down, down[r]).astype(BF16).astype(F32)
        grad_up = (grad_act * slope[r]).astype(BF16)
        upsum_ref[pl.ds(seq ^ r, 1), :] = jnp.sum(grad_up.astype(F32), axis=0, keepdims=True)
        grad_first += nt(grad_up, up[r])
        value = nn(low_t[...], grad_up).astype(BF16)
        for i in range(4):
            for h in range(2):
                spot = place((2 * (seq ^ r) + h) ^ (dp % NEAR), UP_ORDER)
                at = i * part + h * half
                terms[1, i, spot] = value[at : at + half]
    grad_ref[...] = grad_first

    def send(which, r):
        keep_out, far_out, give_out = outs[which]
        target = (keep_out, give_out.at[0], far_out, give_out.at[1])[r]
        return pltpu.make_async_copy(terms.at[which, r], target, out_sems.at[which, r])

    start_all([send(1, r) for r in range(4)])
    for r in range(4):
        value = tn(act[r], grad_down)
        for p in range(PIECES):
            spot = place(p ^ (dp % NEAR), DOWN_ORDER)
            terms[0, r, spot] = value[p * size : (p + 1) * size].astype(BF16)
        send(0, r).start()
    wait_all(early + [send(which, r) for which in range(2) for r in range(4)])


def backward_kernel(place_ref, *refs):
    (a_refs, unit_ref, scale_ref, grad_ref, vec_ref), refs = (refs[:4], *refs[4:8]), refs[8:]
    pieces, refs = refs[:6], refs[6:]
    res_ref, g_refs, sums_ref, keep_ref, far_ref, give_ref, wo, sems = refs[0], refs[1:5], *refs[5:]
    dp = place_ref[1]
    part = wo.shape[1]
    tall = part // PIECES
    copies = weight_copies(place_ref, pieces, wo, None, None, sems)[0]
    start_all(copies)
    unit1 = unit_ref[...]
    grad_first = grad_ref[...]
    grad_residual = norm_back(grad_first, unit1, scale_ref[...], vec_ref[1:2, :])
    res_ref[...] = grad_residual
    grad_out = grad_residual.astype(BF16)
    joined = jnp.concatenate([ref[...] for ref in a_refs], axis=0)
    value = nn(joined, grad_out)
    for r in range(4):
        for p in range(PIECES):
            spot = place(p ^ (dp % NEAR), UP_ORDER)
            piece = value[r * part + p * tall : r * part + (p + 1) * tall].astype(BF16)
            if r % 2:
                give_ref[r // 2, spot] = piece
            else:
                (far_ref if r else keep_ref)[spot] = piece
    sums_ref[0:1, :] = jnp.sum(grad_first * unit1, axis=0, keepdims=True)
    sums_ref[1:2, :] = jnp.sum(grad_first, axis=0, keepdims=True)
    sums_ref[2:3, :] = jnp.sum(grad_out.astype(F32), axis=0, keepdims=True)
    wait_all(copies)
    back = nt(wo[...].reshape(joined.shape[0], -1), grad_out).astype(BF16)
    for r in range(4):
        g_refs[r][...] = back[r * part : (r + 1) * part]


def shaped(*shape, dtype=BF16):
    return jax.ShapeDtypeStruct(shape, dtype)


def any_spec():
    return pl.BlockSpec(memory_space=pl.ANY)


def forward(place_word, attended, embedded, cotangent, vectors, up_bias, pieces):
    rows, features = embedded.shape
    part = attended[0].shape[0]
    size = features // PIECES
    term = [shaped(PIECES, size, features)] * 2 + [shaped(2, PIECES, size, features)]
    return pl.pallas_call(
        forward_kernel,
        in_specs=[pl.BlockSpec(memory_space=pltpu.SMEM)] + [whole_spec()] * 8 + [any_spec()] * 10,
        out_specs=[any_spec()] * 2 + [whole_spec()] * 4 + [any_spec()] * 6,
        out_shape=[
            shaped(rows, features),
            shaped(rows, features, dtype=F32),
            shaped(rows, 1, dtype=F32),
            shaped(rows, features, dtype=F32),
            shaped(3, features, dtype=F32),
            shaped(4, features, dtype=F32),
        ]
        + term
        + term,
        scratch_shapes=[
            pltpu.VMEM((4, part, features), BF16),
            pltpu.VMEM((4, features, features), BF16),
            pltpu.VMEM((4, features, features), BF16),
            pltpu.VMEM((4, rows, features), BF16),
            pltpu.VMEM((4, rows, features), F32),
            pltpu.VMEM((features, rows), BF16),
            pltpu.VMEM((features, rows), BF16),
            pltpu.VMEM((2, 4, PIECES, size, features), BF16),
            pltpu.VMEM((rows, features), BF16),
            pltpu.VMEM((rows, features), F32),
            pltpu.SemaphoreType.DMA((44,)),
            pltpu.SemaphoreType.DMA((2, 4)),
            pltpu.SemaphoreType.DMA((2,)),
        ],
        compiler_params=params(56),
        cost_estimate=pl.CostEstimate(
            flops=12 * rows * features * 4 * features,
            bytes_accessed=26 * 1024 * 1024,
            transcendentals=rows * 4 * features,
        ),
        name="forward",
    )(place_word, *attended, embedded, cotangent, vectors, up_bias, *pieces)


def backward(place_word, attended, unit, scale, grad, vectors, pieces):
    rows, features = unit.shape
    part = attended[0].shape[0]
    piece = (PIECES, part // PIECES, features)
    return pl.pallas_call(
        backward_kernel,
        in_specs=[pl.BlockSpec(memory_space=pltpu.SMEM)] + [whole_spec()] * 8 + [any_spec()] * 6,
        out_specs=[whole_spec()] * 9,
        out_shape=[shaped(rows, features, dtype=F32)]
        + [shaped(part, rows)] * 4
        + [shaped(3, features, dtype=F32), shaped(*piece), shaped(*piece), shaped(2, *piece)],
        scratch_shapes=[pltpu.VMEM((4, part, features), BF16), pltpu.SemaphoreType.DMA((44,))],
        compiler_params=params(56),
        cost_estimate=pl.CostEstimate(
            flops=4 * rows * features * features, bytes_accessed=6 * 1024 * 1024, transcendentals=rows
        ),
        name="backward",
    )(place_word, *attended, unit, scale, grad, vectors, *pieces)


def fold_kernel(*refs, body, inputs, waits):
    body(refs[:inputs], refs[inputs + waits :])


def fold(body, arrays, shapes, after, name):
    return pl.pallas_call(
        functools.partial(fold_kernel, body=body, inputs=len(arrays), waits=len(after)),
        in_specs=[whole_spec()] * len(arrays) + [any_spec()] * len(after),
        out_specs=[whole_spec()] * len(shapes),
        out_shape=[shaped(*shape) for shape in shapes],
        compiler_params=params(40),
        cost_estimate=pl.CostEstimate(flops=0, bytes_accessed=4 * 1024 * 1024, transcendentals=0),
        name=name,
    )(*arrays, *after)


def added(*values):
    return sum(v.astype(F32) for v in values[1:]) + values[0].astype(F32)


def fold_down_core(ins, outs):
    keeps, got = ins[:2], ins[2]
    half = got.shape[1] // 2
    for i, mine in enumerate(keeps):
        outs[i][...] = added(mine[:half], got[i, :half]).astype(BF16)
        outs[2 + i][...] = added(mine[half:], got[i, half:]).astype(BF16)


def fold_up_core(ins, outs):
    size = ins[0].shape[1]
    half = ins[0].shape[0] // 2
    for keep, far, got, rows in ((*ins[:3], slice(0, size)), (*ins[3:], slice(size, None))):
        for i, part in enumerate((slice(0, half), slice(half, None))):
            outs[i][:, rows] = added(keep[part], got[0, part]).astype(BF16)
            outs[2 + i][:, rows] = added(far[part], got[1, part]).astype(BF16)


def fold_both(ins, outs):
    down, down_got, up, up_got = ins
    outs[0][...] = added(down[...], down_got[...]).astype(BF16)
    half = up.shape[0] // 2
    outs[1][...] = added(up[:half], up_got[:half]).astype(BF16)
    outs[2][...] = added(up[half:], up_got[half:]).astype(BF16)


def fold_half(ins, outs):
    mine, got = ins
    half = mine.shape[0] // 2
    outs[0][...] = added(mine[:half], got[:half]).astype(BF16)
    outs[1][...] = added(mine[half:], got[half:]).astype(BF16)


def fold_sum(ins, outs):
    outs[0][...] = added(ins[0][...], ins[1][...]).astype(BF16)


def fold_inner(ins, outs):
    mine, got = ins
    for i in range(2):
        outs[i][...] = added(mine[i], got[i]).astype(BF16)


def settle_kernel(place_ref, *refs, order, store, waits):
    held, outs = refs[:4], refs[4 + waits :]
    seq, dp = place_ref[0], place_ref[1] % NEAR
    for index in range(PIECES):
        spot = place(index, order)
        store(outs, held[spot // 2].at[spot % 2], index ^ dp, seq)


def store_down(outs, piece, p, seq):
    size = piece.shape[0]
    outs[0][pl.ds(pl.multiple_of(p * size, size), size), :] = piece[...].astype(F32)


def store_up(outs, piece, p, seq):
    size, wide = outs[0].shape[0] // 2, piece.shape[1]
    tall = piece.shape[0] - size
    row, column = pl.multiple_of((p % 2) * size, size), pl.multiple_of((p // 2) * wide, wide)
    outs[0][pl.ds(row, size), pl.ds(column, wide)] = piece[:size].astype(F32)
    outs[1][pl.ds(pl.multiple_of(p * tall, 8), tall), :] = piece[size:].astype(F32)


def store_heads(outs, piece, p, seq):
    tall, part = piece.shape[1], piece.shape[2] // 3
    rows = pl.ds(pl.multiple_of(p * tall, 8), tall)
    for c in range(4):
        columns = slice(c * part, (c + 1) * part)
        block = piece[seq ^ c].astype(F32)
        for i in range(3):
            outs[i][rows, columns] = block[:, i * part : (i + 1) * part]


def settle(place_word, held, order, store, shapes, after=()):
    return pl.pallas_call(
        functools.partial(settle_kernel, order=order, store=store, waits=len(after)),
        in_specs=[pl.BlockSpec(memory_space=pltpu.SMEM)] + [whole_spec()] * 4 + [any_spec()] * len(after),
        out_specs=[whole_spec()] * len(shapes),
        out_shape=[jax.ShapeDtypeStruct(shape, F32) for shape in shapes],
        compiler_params=params(56),
        cost_estimate=pl.CostEstimate(flops=0, bytes_accessed=4 * 1024 * 1024, transcendentals=0),
        name="settle",
    )(place_word, *held, *after)


def gate_kernel(*refs):
    pass


def gate(x, *after):
    return pl.pallas_call(
        gate_kernel,
        in_specs=[any_spec()] * (1 + len(after)),
        out_specs=any_spec(),
        out_shape=shaped(*x.shape, dtype=x.dtype),
        input_output_aliases={0: 0},
        cost_estimate=pl.CostEstimate(flops=0, bytes_accessed=0, transcendentals=0),
        name="gate",
    )(x, *after)


def reduce_dp(x, orders):
    for by in orders:
        half = x.shape[0] // 2
        x = x[:half].astype(F32) + swap(x[half:].astype(BF16), "dp", by).astype(F32)
    return x


def reduce_rest(x, last, *after):
    for by in (last, *bits("dp")[3:]):
        x = x.astype(BF16)
        got = swap(x, "dp", by)
        if after and by == last:
            (x,) = fold(fold_sum, [x, got], [x.shape], after, "sum")
        else:
            x = x.astype(F32) + got.astype(F32)
    return x.astype(BF16)


def spread_dp(x, first, last, *after):
    got = swap(x, "dp", first)
    if after:
        got = gate(got, *after)
    return x, got, swap(x, "dp", last), swap(got, "dp", last)


def body(
    text_embed,
    region_feature,
    token_mask,
    segment_mask,
    mask_vector,
    batch_gain,
    batch_shift,
    query_weight,
    query_bias,
    key_weight,
    value_weight,
    value_bias,
    output_weight,
    output_bias,
    first_gain,
    first_shift,
    up_weight,
    up_bias,
    down_weight,
    down_bias,
    second_gain,
    second_shift,
    cotangent,
):
    documents, span, features = text_embed.shape
    rows = documents * span
    seq, dp = lax.axis_index("seq"), lax.axis_index("dp")
    group = lax.axis_size("seq")
    population = rows * lax.axis_size("dp") * group
    score_scale = 1.0 / math.sqrt(HEAD_DIM)
    part = features // group
    heads = part // HEAD_DIM

    place_word = jnp.stack([seq, dp]).astype(jnp.int32)
    cut, halves, mine = pack(
        place_word, query_weight, key_weight, value_weight, output_weight, up_weight
    )

    region = region_feature.astype(F32).reshape(rows, features)
    sums = jnp.stack([jnp.sum(region, axis=0), jnp.sum(region * region, axis=0)])
    chip_sums = sums + swap(sums, "seq", 2)
    chip_sums = gate(chip_sums, cut[0])
    sums = chip_sums + swap(chip_sums, "seq", 1)
    head_blocks = exchange_blocks(cut)
    for by in bits("dp"):
        if by == 4:
            sums = gate(sums, head_blocks[2], head_blocks[3])
        sums = sums + swap(sums, "dp", by)
    average = sums[0] / population
    inverse = lax.rsqrt(sums[1] / population - average * average + EPS_BATCH)

    bias3 = jnp.stack([query_bias, jnp.zeros_like(query_bias), value_bias]).reshape(3, group, part)
    head_bias = lax.dynamic_slice_in_dim(bias3, seq, 1, 1)
    pieces = gather_weight(halves, mine, 1)

    standard = (region - average) * inverse
    token_hit = token_mask.astype(F32).reshape(rows, 1)
    segment_keep = 1.0 - segment_mask.astype(F32).reshape(rows, 1)
    embedded = (
        text_embed.astype(F32).reshape(rows, features) * (1.0 - token_hit)
        + token_hit * mask_vector
        + segment_keep * (standard * batch_gain + batch_shift)
    )
    low_in = embedded.astype(BF16).reshape(documents, span, features)
    x_blocks = gather_rows(low_in)
    far = swap(gate(down_weight, low_in, pieces[1]), "seq", 2)
    q, k, v, head_weight, logs, *attended = attend(place_word, x_blocks, head_blocks, head_bias, [])
    attn_blocks = exchange_blocks(attended)
    far = gate(far, attn_blocks[3])
    pieces += [down_weight, swap(down_weight, "seq", 1), far, swap(far, "seq", 1)]
    vectors = jnp.stack([output_bias, first_gain, first_shift, down_bias, second_gain, second_shift])
    layer_output, unit, scale, grad_first, second_sums, up_sums, *terms = forward(
        place_word,
        attn_blocks,
        embedded,
        cotangent.reshape(rows, features),
        vectors,
        up_bias.reshape(group, features),
        pieces,
    )
    grad_residual, *rest = backward(place_word, attn_blocks, unit, scale, grad_first, vectors, pieces[:6])
    grad_attn, first_sums, (out_keep, out_far, out_give) = rest[:4], rest[4], rest[5:]
    down_keep, down_far, down_give = terms[:3]
    up_keep, up_far, up_give = terms[3:]

    half = PIECES // 2
    size, tall = features // PIECES, part // PIECES
    g_blocks = exchange_blocks(grad_attn)
    down, down_far, down_near_send, down_far_send = fold(
        fold_down_core,
        [down_keep, down_far, swap(down_give, "seq", 1)],
        [(half, size, features)] * 4,
        [g_blocks[2], g_blocks[3]],
        "down_core",
    )
    up, up_more, up_send, up_more_send = fold(
        fold_up_core,
        [up_keep, up_far, swap(up_give, "seq", 1), out_keep, out_far, swap(out_give, "seq", 1)],
        [(half, size + tall, features)] * 4,
        [down_far_send],
        "up_core",
    )
    down_far_got = swap(down_far_send, "dp", DOWN_ORDER[0])
    down_near_got = swap(down_near_send, "dp", DOWN_ORDER[0])
    up_more_got = swap(up_more_send, "seq", 2)
    up_got = swap(up_send, "seq", 2)

    keep, give, heads, heads_send, head_sums = attend_back(
        place_word, g_blocks, x_blocks, attended, q, k, v, head_weight, logs, [up_more_send]
    )
    query_sums, value_sums = head_sums[0], head_sums[1]

    quarter = half // 2
    down_send, up_send, up_more_send = fold(
        fold_both,
        [down_far, down_far_got, up_more, up_more_got],
        [(half, size, features)] + [(quarter, size + tall, features)] * 2,
        [head_sums],
        "both",
    )
    inner_own, inner_send = fold(
        fold_inner, [keep, swap(gate(give, up_more_send), "seq", 1)], [keep.shape[1:]] * 2, [up_send, down_near_got], "inner"
    )
    heads, heads_send = fold(
        fold_half,
        [heads, swap(gate(heads_send, up_more_send), "dp", HEAD_ORDER[0])],
        [(half // 2, group, tall, 3 * part)] * 2,
        [up_send, up_got],
        "heads",
    )
    inner_got = swap(inner_send, "seq", 2)
    got = gate(swap(up_more_send, "dp", UP_ORDER[0]), heads_send)
    up_more = up[quarter:].astype(F32) + up_got[quarter:].astype(F32) + got.astype(F32)
    got = swap(up_send, "dp", UP_ORDER[0])
    up = up[:quarter].astype(F32) + up_got[:quarter].astype(F32) + got.astype(F32)
    got = gate(swap(down_send, "seq", 2), up_more)
    down = down.astype(F32) + down_near_got.astype(F32) + got.astype(F32)
    heads = heads.astype(F32) + gate(swap(heads_send, "dp", HEAD_ORDER[1]), down).astype(F32)
    got = gate(swap(up_more.astype(BF16), "dp", UP_ORDER[1]), inner_got, down)
    up = up + got.astype(F32)
    down = reduce_dp(down, DOWN_ORDER[1:-1])

    inner = inner_own.astype(F32) + inner_got.astype(F32)
    grad_embedded = grad_residual + inner.reshape(rows, features)
    text_gradient = (grad_embedded * (1.0 - token_hit)).astype(BF16)
    grad_normed = grad_embedded * segment_keep

    def widen(x):
        return lax.dynamic_update_slice_in_dim(jnp.zeros((features,), F32), x, seq * part, 0)

    sums = jnp.concatenate(
        [
            jnp.stack(
                [
                    jnp.sum(grad_normed * standard, axis=0),
                    jnp.sum(grad_normed, axis=0),
                    jnp.sum(grad_embedded * token_hit, axis=0),
                    widen(query_sums),
                    widen(value_sums),
                ]
            ),
            second_sums,
            first_sums,
            up_sums,
        ]
    )
    for by in bits("seq"):
        sums = sums + swap(sums, "seq", by)

    own = reduce_rest(heads, HEAD_ORDER[-1], up, down)
    own = jnp.stack(exchange_blocks([own[:, r] for r in range(group)]), axis=1)
    held_heads = spread_dp(own, 1, 2)
    total_query, total_key, total_value = settle(
        place_word, held_heads, (2, 1, 4), store_heads, [query_weight.shape] * 3
    )

    up = reduce_rest(up, UP_ORDER[-1], sums)
    sums = sums + swap(sums, "dp", 1)
    down = reduce_rest(down, DOWN_ORDER[-1], up, sums)
    held_up = spread_dp(up, 2, 1, down)
    held_down = spread_dp(down, 1, 2, held_heads[3])
    for by in bits("dp")[1:]:
        sums = sums + swap(sums, "dp", by)
    (total_down,) = settle(place_word, held_down, (2, 1, 4), store_down, [down_weight.shape], [sums])
    total_up, total_out = settle(
        place_word, held_up, (1, 2, 4), store_up, [up_weight.shape, output_weight.shape], [sums]
    )

    (
        sum_gain,
        sum_shift,
        sum_mask,
        sum_query_bias,
        sum_value_bias,
        sum_second_gain,
        sum_second_shift,
        sum_down_bias,
        sum_first_gain,
        sum_first_shift,
        sum_output_bias,
    ) = sums[:11]
    sum_up_bias = sums[11:].reshape(-1)

    region_gradient = (
        batch_gain
        * inverse
        * (grad_normed - sum_shift / population - standard * (sum_gain / population))
    ).astype(BF16)
    shape = (documents, span, features)
    return (
        layer_output.reshape(shape),
        text_gradient.reshape(shape),
        region_gradient.reshape(shape),
        sum_mask,
        sum_gain,
        sum_shift,
        total_query,
        sum_query_bias,
        total_key,
        total_value,
        sum_value_bias,
        total_out,
        sum_output_bias,
        sum_first_gain,
        sum_first_shift,
        total_up,
        sum_up_bias,
        total_down,
        sum_down_bias,
        sum_second_gain,
        sum_second_shift,
    )


def solution(mesh):
    rows, weight, copied = P("dp", "seq", None), P("seq", None), P()
    mask = P("dp", "seq")
    in_specs = (
        (rows, rows, mask, mask, copied, copied, copied)
        + (weight, copied, weight, weight, copied, weight, copied, copied, copied)
        + (weight, copied, weight, copied, copied, copied, rows)
    )
    out_specs = (
        (rows, rows, rows, copied, copied, copied)
        + (weight, copied, weight, weight, copied, weight, copied, copied, copied)
        + (weight, copied, weight, copied, copied, copied)
    )
    return jax.shard_map(body, mesh=mesh, in_specs=in_specs, out_specs=out_specs, check_vma=False)
```
